32 devices in a mesh: dp: 16 (over z, y, x), pair: 2 (over core).
Axes of the slice: x: 2, y: 2, z: 4, core: 2. Of those that a mesh axis runs over, the one named last changes fastest.
Arguments:
- tokens: bfloat16 [32768, 768], P(('dp', 'pair')), may hold values from -10 to 10
- mlm_grad: bfloat16 [32768, 768], P(('dp', 'pair')), may hold values from -6 to 6
- doc_ids: int32 [32, 8], P('dp'), may hold values from -1 to 127, as said below
- span_counts: int32 [32], P('dp'), may hold values from 1 to 8, as said below
- qkv_weight: float32 [768, 2304], P(('dp', 'pair')), may hold values from -0.21875 to 0.21875
- proj_weight: float32 [768, 768], P(('dp', 'pair')), may hold values from -0.625 to 0.625
- inner_weight: float32 [768, 3072], P(('dp', 'pair')), may hold values from -0.21875 to 0.21875
- outer_weight: float32 [3072, 768], P(('dp', 'pair')), may hold values from -0.109375 to 0.109375
- affine_params: float32 [12, 768], P(None, ('dp', 'pair')), may hold values from -0.5 to 2.5
- qkv_moment: float32 [768, 2304], P(('dp', 'pair')), may hold values from -0.625 to 0.625
- proj_moment: float32 [768, 768], P(('dp', 'pair')), may hold values from -0.625 to 0.625
- inner_moment: float32 [768, 3072], P(('dp', 'pair')), may hold values from -0.625 to 0.625
- outer_moment: float32 [3072, 768], P(('dp', 'pair')), may hold values from -0.625 to 0.625
- affine_moment: float32 [12, 768], P(None, ('dp', 'pair')), may hold values from -2.5 to 2.5
- qkv_square: float32 [768, 2304], P(('dp', 'pair')), may hold values from 0.00014124246 to 0.00056496984
- proj_square: float32 [768, 768], P(('dp', 'pair')), may hold values from 0.00014124246 to 0.00056496984
- inner_square: float32 [768, 3072], P(('dp', 'pair')), may hold values from 0.00014124246 to 0.00056496984
- outer_square: float32 [3072, 768], P(('dp', 'pair')), may hold values from 0.00014124246 to 0.00056496984
- affine_square: float32 [12, 768], P(None, ('dp', 'pair')), may hold values from 0.0022598794 to 0.0090395175
Outputs:
- weight_qkv: float32 [768, 2304], P(('dp', 'pair'))
- weight_proj: float32 [768, 768], P(('dp', 'pair'))
- weight_inner: float32 [768, 3072], P(('dp', 'pair'))
- weight_outer: float32 [3072, 768], P(('dp', 'pair'))
- weight_affine: float32 [12, 768], P(None, ('dp', 'pair'))
- moment_qkv: float32 [768, 2304], P(('dp', 'pair'))
- moment_proj: float32 [768, 768], P(('dp', 'pair'))
- moment_inner: float32 [768, 3072], P(('dp', 'pair'))
- moment_outer: float32 [3072, 768], P(('dp', 'pair'))
- moment_affine: float32 [12, 768], P(None, ('dp', 'pair'))
- square_qkv: float32 [768, 2304], P(('dp', 'pair'))
- square_proj: float32 [768, 768], P(('dp', 'pair'))
- square_inner: float32 [768, 3072], P(('dp', 'pair'))
- square_outer: float32 [3072, 768], P(('dp', 'pair'))
- square_affine: float32 [12, 768], P(None, ('dp', 'pair'))
- layer_out: bfloat16 [32768, 768], P(('dp', 'pair'))
- input_grad: float32 [32768, 768], P(('dp', 'pair'))
- grad_norm: float32 [], replicated
- mean_loss: float32 [], replicated
The draws below stay inside these ranges and needn't reach their ends.
Inputs may be any that keep to these rules, and one draw needn't show every extreme that they name: `doc_ids`: row 2g+p holds the document of each span slot of pair index p in group g; live slots are the first span_counts[2g+p]; on pair index 0 the live slot s holds g * 8 + s; each live slot of pair index 1 holds the id of a distinct live slot of pair index 0 of the same group; slots past the live count hold -1. `span_counts`: entry 2g+1 is never larger than entry 2g.
All inputs are finite; a program needn't handle non-finite values.
Results may differ from the reference program's by a relative error of at most 0.018.
Values may be sent and summed in bfloat16 or wider, within the bound.
No kernel may reach another device: no remote copies, remote signals or barrier semaphores. Data moves between devices by JAX's collectives and lax.ppermute only.
A program may use at most 192 MiB of HBM per device.

```python
import math
import jax
import jax.numpy as jnp
from jax import lax

D = 768
HEADS = 12
HD = 64
FF = 3072
L = 128
SPANS_DEV = 8
STEP = 10
GROUPS = 16
TOTAL_SPANS = 256
TOKENS = 32768
NPARAM = 7087104


def span_layout(key):
    key = jax.random.fold_in(key, 5)
    count_key, lone_key, order_key = jax.random.split(key, 3)
    groups = jnp.arange(GROUPS)
    base_count = 2 + (SPANS_DEV - 2) * groups // max(GROUPS - 1, 1)
    wobble = jax.random.randint(count_key, (GROUPS,), -1, 2)
    leading = jnp.clip(base_count + wobble, 2, SPANS_DEV)
    leading = jnp.where(groups == GROUPS - 1, SPANS_DEV, leading)
    lone = jax.random.randint(lone_key, (GROUPS,), 0, 1 << 20) % (leading // 2 + 1)
    second = leading - lone
    slot_index = jnp.arange(SPANS_DEV)
    scores = jax.random.randint(order_key, (GROUPS, SPANS_DEV), 0, 1 << 20) * SPANS_DEV + slot_index[None, :]
    scores = jnp.where(slot_index[None, :] < leading[:, None], scores, (1 << 26) + slot_index[None, :])
    order = jnp.argsort(scores, axis=1, stable=True)
    first_ids = jnp.where(slot_index[None, :] < leading[:, None], groups[:, None] * SPANS_DEV + slot_index[None, :], -1)
    picked = jnp.take_along_axis(order, jnp.clip(lone[:, None] + slot_index[None, :], 0, SPANS_DEV - 1), axis=1)
    second_ids = jnp.where(slot_index[None, :] < second[:, None], groups[:, None] * SPANS_DEV + picked, -1)
    span_ids = jnp.stack([first_ids, second_ids], axis=1).reshape(2 * GROUPS, SPANS_DEV)
    counts = jnp.stack([leading, second], axis=1).reshape(2 * GROUPS)
    return (span_ids.astype(jnp.int32), counts.astype(jnp.int32))


def draw_doc_ids(key, part):
    return span_layout(key)[0]


def draw_span_counts(key, part):
    return span_layout(key)[1]


def draw_tokens(key, part):
    key = jax.random.fold_in(key, 11)
    entry_key, jitter_key = jax.random.split(key)
    feature = jnp.arange(D, dtype=jnp.float32) / (D - 1)
    rising = 0.6 * 3.0 ** feature
    entries = jax.random.truncated_normal(entry_key, -4.0, 4.0, (TOKENS, D), jnp.float32)
    jitter = jnp.exp(jax.random.uniform(jitter_key, (D,), jnp.float32, -0.25, 0.25))
    return (entries * rising[None, :] * jitter[None, :]).astype(jnp.bfloat16)


def draw_affine_params(key, part):
    key = jax.random.fold_in(key, 23)
    bias_key, jitter_key = jax.random.split(key)
    feature = jnp.arange(D, dtype=jnp.float32) / (D - 1)
    rising = 0.6 * 3.0 ** feature
    biases = 0.1 * jax.random.truncated_normal(bias_key, -4.0, 4.0, (10, D), jnp.float32)
    jitter = jnp.exp(jax.random.uniform(jitter_key, (2, D), jnp.float32, -0.2, 0.2))
    gains = rising[None, :] * jitter
    rows_list = [gains[0], biases[0], gains[1], biases[1]] + [biases[index] for index in range(2, 10)]
    return jnp.stack(rows_list).astype(jnp.float32)


def steps_of(rng, extent, cuts, low, high):
    def one(axis_at, blocks):
        draws = jax.random.uniform(jax.random.fold_in(jax.random.fold_in(rng, 6), axis_at), (blocks,), jnp.float32, low / len(cuts), high / len(cuts))
        return jnp.repeat(jnp.exp(draws), extent[axis_at] // blocks).reshape((-1,) + (1,) * (len(extent) - axis_at - 1))

    factor_of = one(*cuts[0])
    for cut in cuts[1:]:
        factor_of = factor_of * one(*cut)
    return factor_of


def gaussian(stream_key, extent, spread, most, cuts=(), kind=jnp.bfloat16):
    array = spread * jax.random.normal(stream_key, extent, jnp.float32)
    if cuts:
        array = array * steps_of(stream_key, extent, cuts, -0.22, 0.18)
    return jnp.clip(array, -most, most).astype(kind)


def setup_inputs(seed: int = 0) -> dict:
    splits = jax.random.split(jax.random.key(seed), 20)
    tokens = draw_tokens(jax.random.fold_in(splits[19], 71), 0)
    mlm_grad = gaussian(splits[1], (TOKENS, D), 1.0, 6.0, ((0, 32),))
    doc_ids = draw_doc_ids(jax.random.fold_in(splits[19], 71), 0)
    span_counts = draw_span_counts(jax.random.fold_in(splits[19], 71), 0)
    qkv_weight = gaussian(splits[4], (D, 3 * D), D ** -0.5, 0.21875, ((0, 32),), jnp.float32)
    proj_weight = gaussian(splits[5], (D, D), (D // 8) ** -0.5, 0.625, ((0, 32),), jnp.float32)
    inner_weight = gaussian(splits[6], (D, FF), D ** -0.5, 0.21875, ((0, 32),), jnp.float32)
    outer_weight = gaussian(splits[7], (FF, D), FF ** -0.5, 0.109375, ((0, 32),), jnp.float32)
    affine_params = draw_affine_params(jax.random.fold_in(splits[19], 71), 0)
    qkv_moment = gaussian(splits[9], (D, 3 * D), (111.0 / NPARAM ** 0.5), 0.625, ((0, 32),), jnp.float32)
    proj_moment = gaussian(splits[10], (D, D), (111.0 / NPARAM ** 0.5), 0.625, ((0, 32),), jnp.float32)
    inner_moment = gaussian(splits[11], (D, FF), (111.0 / NPARAM ** 0.5), 0.625, ((0, 32),), jnp.float32)
    outer_moment = gaussian(splits[12], (FF, D), (111.0 / NPARAM ** 0.5), 0.625, ((0, 32),), jnp.float32)
    affine_moment = gaussian(splits[13], (12, D), (444.0 / NPARAM ** 0.5), 2.5, ((1, 32),), jnp.float32)
    qkv_square = jnp.clip(jnp.exp(math.log(0.00056496984) - 1.3862944 * jax.random.uniform(splits[14], (D, 3 * D), jnp.float32) ** steps_of(splits[14], (D, 3 * D), ((0, 32),), -0.2, 0.2)), 0.00014124246, 0.00056496984)
    proj_square = jnp.clip(jnp.exp(math.log(0.00056496984) - 1.3862944 * jax.random.uniform(splits[15], (D, D), jnp.float32) ** steps_of(splits[15], (D, D), ((0, 32),), -0.2, 0.2)), 0.00014124246, 0.00056496984)
    inner_square = jnp.clip(jnp.exp(math.log(0.00056496984) - 1.3862944 * jax.random.uniform(splits[16], (D, FF), jnp.float32) ** steps_of(splits[16], (D, FF), ((0, 32),), -0.2, 0.2)), 0.00014124246, 0.00056496984)
    outer_square = jnp.clip(jnp.exp(math.log(0.00056496984) - 1.3862944 * jax.random.uniform(splits[17], (FF, D), jnp.float32) ** steps_of(splits[17], (FF, D), ((0, 32),), -0.2, 0.2)), 0.00014124246, 0.00056496984)
    affine_square = jnp.clip(jnp.exp(math.log(0.0090395175) - 1.3862944 * jax.random.uniform(splits[18], (12, D), jnp.float32) ** steps_of(splits[18], (12, D), ((1, 32),), -0.2, 0.2)), 0.0022598794, 0.0090395175)
    return dict(tokens=tokens, mlm_grad=mlm_grad, doc_ids=doc_ids, span_counts=span_counts, qkv_weight=qkv_weight, proj_weight=proj_weight, inner_weight=inner_weight, outer_weight=outer_weight, affine_params=affine_params, qkv_moment=qkv_moment, proj_moment=proj_moment, inner_moment=inner_moment, outer_moment=outer_moment, affine_moment=affine_moment, qkv_square=qkv_square, proj_square=proj_square, inner_square=inner_square, outer_square=outer_square, affine_square=affine_square)


HIGH = lax.Precision.HIGHEST
LN_EPS = 1e-12
LOSS_WEIGHT = 8.0
CLIP_NORM = 1000.0
BETA_ONE = 0.9
BETA_TWO = 0.999
ADAM_EPS = 1e-08
RATE_MATRIX = 0.05
DECAY_MATRIX = 0.01
RATE_AFFINE = 0.8
DECAY_AFFINE = 0.0

@jax.custom_vjp
def low(v):
    return lax.optimization_barrier(v.astype(jnp.bfloat16)).astype(jnp.float32)

@jax.custom_vjp
def low_back(v):
    return v

def low_keep(v):
    return (low(v), None)

def low_pass(kept, grad):
    return (grad,)

def back_keep(v):
    return (v, None)

def back_low(kept, grad):
    return (low(grad),)
low.defvjp(low_keep, low_pass)
low_back.defvjp(back_keep, back_low)

def master_low(weight):
    return lax.optimization_barrier(weight.astype(jnp.bfloat16)).astype(jnp.float32)

def layer_norm(total, gain, shift):
    centered = total - lax.optimization_barrier(jnp.mean(total, axis=-1, keepdims=True))
    variance = lax.optimization_barrier(jnp.mean(centered * centered, axis=-1, keepdims=True))
    return centered * lax.rsqrt(variance + LN_EPS) * gain + shift

def contrast_side(anchor, keys_side, anchor_ids, key_ids, anchor_live, key_live):
    sims = jnp.dot(anchor, keys_side.T, precision=HIGH) * anchor.shape[1] ** (-0.5)
    masked = jnp.where(key_live[None, :], sims, -1000000000.0)
    peak_score = lax.optimization_barrier(jnp.max(masked, axis=1, keepdims=True))
    weights_exp = jnp.where(key_live[None, :], jnp.exp(masked - peak_score), 0.0)
    log_total = peak_score[:, 0] + jnp.log(lax.optimization_barrier(jnp.sum(weights_exp, axis=1)))
    match = (anchor_ids[:, None] == key_ids[None, :]) & key_live[None, :] & anchor_live[:, None]
    active_rows = jnp.any(match, axis=1)
    hit_score = lax.optimization_barrier(jnp.sum(jnp.where(match, sims, 0.0), axis=1))
    return jnp.sum(jnp.where(active_rows, log_total - hit_score, 0.0))

def group_forward(params, group_rows, span_ids, counts):
    qkv_w, proj_w, inner_w, outer_w, affine = params
    spans = 2 * SPANS_DEV
    gain_one, shift_one, gain_two, shift_two = (affine[0], affine[1], affine[2], affine[3])
    bias_query, bias_value, bias_proj, bias_outer = (affine[4], affine[5], affine[6], affine[7])
    bias_inner = affine[8:12].reshape(FF)
    qkv_bias = jnp.concatenate([bias_query, jnp.zeros((D,), jnp.float32), bias_value])
    projected = low(low_back(jnp.dot(group_rows, qkv_w, precision=HIGH)) + qkv_bias)
    projected = projected.reshape(spans, L, 3, HEADS, HD)
    queries, key_rows, values = (projected[:, :, 0], projected[:, :, 1], projected[:, :, 2])
    scores = low_back(jnp.einsum('nqhe,nkhe->nhqk', queries, key_rows, precision=HIGH)) * HD ** (-0.5)
    peak_score = lax.optimization_barrier(jnp.max(scores, axis=-1, keepdims=True))
    exponent = jnp.exp(scores - peak_score)
    attention = exponent / lax.optimization_barrier(jnp.sum(exponent, axis=-1, keepdims=True))
    context = jnp.einsum('nhqk,nkhe->nqhe', low(attention), values, precision=HIGH)
    context = low_back(low(context)).reshape(spans * L, D)
    attended = low_back(jnp.dot(context, proj_w, precision=HIGH)) + bias_proj
    skip_rows = layer_norm(group_rows + attended, gain_one, shift_one)
    inner_pre = low_back(jnp.dot(low(skip_rows), inner_w, precision=HIGH)) + bias_inner
    activated = low(jax.nn.gelu(inner_pre, approximate=False))
    outer_out = low_back(jnp.dot(activated, outer_w, precision=HIGH)) + bias_outer
    result = layer_norm(skip_rows + outer_out, gain_two, shift_two)
    cls_rows = low(result.reshape(spans, L, D)[:, 0, :])
    slot_index = jnp.arange(SPANS_DEV)
    live_first = slot_index < counts[0]
    live_second = slot_index < counts[1]
    leading, second = (cls_rows[:SPANS_DEV], cls_rows[SPANS_DEV:])
    loss_sum = contrast_side(leading, second, span_ids[0], span_ids[1], live_first, live_second)
    loss_sum = loss_sum + contrast_side(second, leading, span_ids[1], span_ids[0], live_second, live_first)
    return (result, loss_sum)

def adamw(master, moment, square, gradient, factor, rate, decay):
    clipped = gradient * factor
    moment_new = BETA_ONE * moment + (1.0 - BETA_ONE) * clipped
    square_new = BETA_TWO * square + (1.0 - BETA_TWO) * clipped * clipped
    mean_hat = moment_new / (1.0 - BETA_ONE ** STEP)
    square_hat = square_new / (1.0 - BETA_TWO ** STEP)
    master_new = master - rate * (mean_hat / (jnp.sqrt(square_hat) + ADAM_EPS) + decay * master)
    return (master_new, moment_new, square_new)

def add_trees(left_tree, right_tree):
    return jax.tree.map(jnp.add, left_tree, right_tree)

def reference(tokens, mlm_grad, doc_ids, span_counts, qkv_weight, proj_weight, inner_weight, outer_weight, affine_params, qkv_moment, proj_moment, inner_moment, outer_moment, affine_moment, qkv_square, proj_square, inner_square, outer_square, affine_square):
    masters = (qkv_weight, proj_weight, inner_weight, outer_weight, affine_params)
    params = tuple((master_low(weight) for weight in masters))
    rows_all = tokens.astype(jnp.float32).reshape(GROUPS, 2 * SPANS_DEV * L, D)
    upstream_all = mlm_grad.astype(jnp.float32).reshape(GROUPS, 2 * SPANS_DEV * L, D)
    ids_all = doc_ids.reshape(GROUPS, 2, SPANS_DEV)
    counts_all = span_counts.reshape(GROUPS, 2)

    def advance(totals, inputs):
        group_rows, upstream, span_ids, counts = inputs

        def forward_group(weights_in, rows_in):
            return group_forward(weights_in, rows_in, span_ids, counts)
        (result, loss_sum), pull_back = jax.vjp(forward_group, params, group_rows)
        slot_index = jnp.arange(SPANS_DEV)
        span_live = jnp.concatenate([slot_index < counts[0], slot_index < counts[1]])
        row_live = jnp.repeat(span_live, L).astype(jnp.float32)
        gradients, row_grad = pull_back((upstream * row_live[:, None], jnp.asarray(LOSS_WEIGHT, jnp.float32)))
        return (add_trees(totals, gradients), (result.astype(jnp.bfloat16), row_grad, loss_sum))
    zeros = jax.tree.map(jnp.zeros_like, params)
    gradients, (results, row_grads, losses) = lax.scan(advance, zeros, (rows_all, upstream_all, ids_all, counts_all))
    squares = jnp.sum(jnp.stack([jnp.sum(grad_item * grad_item) for grad_item in gradients]))
    grad_norm = jnp.sqrt(squares)
    factor = jnp.minimum(1.0, CLIP_NORM / (grad_norm + 1e-06))
    moments = (qkv_moment, proj_moment, inner_moment, outer_moment, affine_moment)
    squares_old = (qkv_square, proj_square, inner_square, outer_square, affine_square)
    rates = (RATE_MATRIX, RATE_MATRIX, RATE_MATRIX, RATE_MATRIX, RATE_AFFINE)
    decays = (DECAY_MATRIX, DECAY_MATRIX, DECAY_MATRIX, DECAY_MATRIX, DECAY_AFFINE)
    updated = [adamw(masters[index], moments[index], squares_old[index], gradients[index], factor, rates[index], decays[index]) for index in range(5)]
    mean_loss = jnp.sum(losses) / TOTAL_SPANS
    return (updated[0][0], updated[1][0], updated[2][0], updated[3][0], updated[4][0], updated[0][1], updated[1][1], updated[2][1], updated[3][1], updated[4][1], updated[0][2], updated[1][2], updated[2][2], updated[3][2], updated[4][2], results.reshape(TOKENS, D), row_grads.reshape(TOKENS, D), grad_norm, mean_loss)
```

```python
from functools import partial

import jax
import jax.numpy as jnp
from jax import lax
from jax.experimental import pallas as pl
from jax.experimental.pallas import tpu as pltpu
from jax.sharding import PartitionSpec as P

HEADS = 12
HD = 64
L = 128
STEP = 10
LANES = 128
AXES = ("dp", "pair")


LN_EPS = 1e-12
LOSS_WEIGHT = 8.0
CLIP_NORM = 1000.0
BETA_ONE = 0.9
BETA_TWO = 0.999
ADAM_EPS = 1e-08
RATE_MATRIX = 0.05
DECAY_MATRIX = 0.01
RATE_AFFINE = 0.8
DECAY_AFFINE = 0.0

BF16 = jnp.bfloat16
F32 = jnp.float32


def flip_steps(chips):
    bits = chips.bit_length() - 1
    if bits == 4:
        return ((2, 3), (3, 2), (0, 1), (1, 0))
    return tuple((bit, bit) for bit in reversed(range(bits)))


def flip_route(chips, pair_of_bits):
    return [
        (2 * d + c, 2 * (d ^ (1 << pair_of_bits[c])) + c) for d in range(chips) for c in range(2)
    ]


def core_route(chips):
    return [(2 * d + c, 2 * d + 1 - c) for d in range(chips) for c in range(2)]


def flipped(block, bits):
    chips = lax.axis_size("dp")
    return lax.ppermute(block, AXES, flip_route(chips, bits))


def core_swapped(block):
    return lax.ppermute(block, AXES, core_route(lax.axis_size("dp")))


def block_order():
    chips = lax.axis_size("dp")
    d, c = lax.axis_index("dp"), lax.axis_index("pair")
    steps = flip_steps(chips)
    rows = []
    for core in range(2):
        rows.append(
            jnp.array(
                [
                    sum((place >> k & 1) << steps[k][core] for k in range(len(steps)))
                    for place in range(chips)
                ],
                jnp.int32,
            )
            ^ d
        )
    own = jnp.where(c == 0, rows[0], rows[1])
    other = jnp.where(c == 0, rows[1], rows[0])
    return jnp.stack([own, other, jnp.full((chips,), c, jnp.int32)])


def pick(core, first, second):
    return jnp.where(core == 0, first, second)


def halves_of(low, pieces):
    core = lax.axis_index("pair")
    first, second, at = [], [], 0
    for width in pieces:
        first.append(low[:, at : at + width])
        second.append(low[:, at + width : at + 2 * width])
        at += 2 * width
    first, second = jnp.concatenate(first, 1), jnp.concatenate(second, 1)
    return pick(core, first, second), pick(core, second, first)


def chip_rows(low, pieces, extra=None):
    core = lax.axis_index("pair")
    own, other = halves_of(low, pieces)
    if extra is not None:
        own, other = (jnp.concatenate([half, extra], 1) for half in (own, other))
    got = core_swapped(other)
    return pick(core, jnp.concatenate([own, got]), jnp.concatenate([got, own]))


def shard_of(half_rows, pieces, core):
    rows = half_rows.shape[0] // 2
    first, second = half_rows[:rows], half_rows[rows:]
    own = pick(core, first, second)
    got = core_swapped(pick(core, second, first).astype(BF16)).astype(F32)
    low, high = pick(core, own, got), pick(core, got, own)
    out, at = [], 0
    for width in pieces:
        out += [low[:, at : at + width], high[:, at : at + width]]
        at += width
    return jnp.concatenate(out, 1)


def gather_blocks(block):
    held = block[None]
    for bits in flip_steps(lax.axis_size("dp")):
        held = jnp.concatenate([held, flipped(held, bits)], axis=0)
    return held, core_swapped(held)


def reduce_blocks(own, other):
    parts = [own, core_swapped(other)]
    count = own.shape[0]
    for bits in reversed(flip_steps(lax.axis_size("dp"))):
        count //= 2
        sent = sum(p[count : 2 * count].astype(F32) for p in parts).astype(BF16)
        parts = parts + [flipped(sent, bits)]
        parts = [p[:count] for p in parts]
    return sum(p[0].astype(F32) for p in parts)


def total_over_devices(value):
    chips = lax.axis_size("dp")
    value = value + core_swapped(value)
    for bit in range(chips.bit_length() - 1):
        value = value + flipped(value, (bit, bit))
    return value


def moved(order, own, other, whole_shapes, pieces):
    chips, rows, _ = own.shape
    if rows % 16:
        core = order[2, 0]
        lined = [
            jnp.zeros(ref.shape, BF16).at[order[side]].set(ref).reshape(chips * rows, -1)
            for side, ref in enumerate((own, other))
        ]
        low, high = pick(core, lined[0], lined[1]), pick(core, lined[1], lined[0])
        return tuple(
            jnp.concatenate(
                [
                    ref[:, lane : lane + width]
                    for at, _, width, lane in pieces
                    if at == whole
                    for ref in (low, high)
                ],
                axis=1,
            )
            for whole in range(len(whole_shapes))
        )

    def kernel(order_ref, own_ref, other_ref, *rest):
        wholes, sems = rest[:-1], rest[-1]
        core = order_ref[2, 0]
        copies = []
        for side, ref in enumerate((own_ref, other_ref)):
            half = core if side == 0 else 1 - core
            for place in range(chips):
                row = pl.multiple_of(order_ref[side, place] * rows, rows)
                for whole, start, width, lane in pieces:
                    col = pl.multiple_of(start + half * width, LANES)
                    copies.append(
                        pltpu.make_async_copy(
                            ref.at[place, :, pl.ds(lane, width)],
                            wholes[whole].at[pl.ds(row, rows), pl.ds(col, width)],
                            sems.at[len(copies)],
                        )
                    )
        for copy in copies:
            copy.start()
        for copy in copies:
            copy.wait()

    return pl.pallas_call(
        kernel,
        out_shape=tuple(jax.ShapeDtypeStruct(s, BF16) for s in whole_shapes),
        in_specs=[
            pl.BlockSpec(memory_space=pltpu.SMEM),
            pl.BlockSpec(memory_space=pl.ANY),
            pl.BlockSpec(memory_space=pl.ANY),
        ],
        out_specs=tuple(pl.BlockSpec(memory_space=pltpu.VMEM) for _ in whole_shapes),
        scratch_shapes=[pltpu.SemaphoreType.DMA((2 * chips * len(pieces),))],
    )(order, own, other)


def parted(order, wholes, rows, cols, pieces):
    chips = order.shape[1]
    if rows % 16:
        core = order[2, 0]
        low, high = (
            jnp.concatenate(
                [
                    wholes[at][:, start + half * width : start + (half + 1) * width]
                    for at, start, width, _ in pieces
                ],
                axis=1,
            ).reshape(chips, rows, cols)
            for half in range(2)
        )
        own, other = pick(core, low, high), pick(core, high, low)
        return own[order[0]], other[order[1]]
    shape = jax.ShapeDtypeStruct((chips, rows, cols), BF16)

    def kernel(order_ref, *rest):
        wholes, (own_ref, other_ref, sems) = rest[:-3], rest[-3:]
        core = order_ref[2, 0]
        copies = []
        for side, ref in enumerate((own_ref, other_ref)):
            half = core if side == 0 else 1 - core
            for place in range(chips):
                row = pl.multiple_of(order_ref[side, place] * rows, rows)
                for whole, start, width, lane in pieces:
                    col = pl.multiple_of(start + half * width, LANES)
                    copies.append(
                        pltpu.make_async_copy(
                            wholes[whole].at[pl.ds(row, rows), pl.ds(col, width)],
                            ref.at[place, :, pl.ds(lane, width)],
                            sems.at[len(copies)],
                        )
                    )
        for copy in copies:
            copy.start()
        for copy in copies:
            copy.wait()

    return pl.pallas_call(
        kernel,
        out_shape=(shape, shape),
        in_specs=[pl.BlockSpec(memory_space=pltpu.SMEM)]
        + [pl.BlockSpec(memory_space=pltpu.VMEM) for _ in wholes],
        out_specs=(pl.BlockSpec(memory_space=pl.ANY), pl.BlockSpec(memory_space=pl.ANY)),
        scratch_shapes=[pltpu.SemaphoreType.DMA((2 * chips * len(pieces),))],
    )(order, *wholes)


def contract_rows(left, right):
    return lax.dot_general(
        left, right, (((0,), (0,)), ((), ())), preferred_element_type=jnp.float32
    )


def contract_cols(left, right):
    return lax.dot_general(
        left, right, (((1,), (1,)), ((), ())), preferred_element_type=jnp.float32
    )


def normalize(total):
    centered = total - jnp.mean(total, axis=-1, keepdims=True)
    variance = jnp.mean(centered * centered, axis=-1, keepdims=True)
    scale_inv = lax.rsqrt(variance + LN_EPS)
    return (centered * scale_inv, scale_inv)


def normalize_back(upstream, normed, scale_inv, gain):
    scaled = upstream * gain
    return scale_inv * (
        scaled
        - jnp.mean(scaled, axis=-1, keepdims=True)
        - normed * jnp.mean(scaled * normed, axis=-1, keepdims=True)
    )


def attend(tokens, qkv_w, qkv_bias):
    rows, width = tokens.shape
    projected = (jnp.dot(tokens, qkv_w, preferred_element_type=jnp.float32) + qkv_bias).astype(
        jnp.bfloat16
    )
    split_heads = projected.reshape(rows // L, L, 3, HEADS, HD)
    queries, key_rows, values = (split_heads[:, :, 0], split_heads[:, :, 1], split_heads[:, :, 2])
    scores = jnp.einsum(
        "nqhe,nkhe->nhqk", queries, key_rows, preferred_element_type=jnp.float32
    ) * HD ** (-0.5)
    peak_score = jnp.max(scores, axis=-1, keepdims=True)
    exponent = jnp.exp(scores - peak_score)
    attention = exponent / jnp.sum(exponent, axis=-1, keepdims=True)
    attention_low = attention.astype(jnp.bfloat16)
    context = jnp.einsum(
        "nhqk,nkhe->nqhe", attention_low, values, preferred_element_type=jnp.float32
    )
    context = context.astype(jnp.bfloat16).reshape(rows, width)
    return (queries, key_rows, values, attention, attention_low, context)


def contrast(anchor, keys_side, anchor_ids, key_ids, anchor_live, key_live):
    sims = lax.dot_general(
        anchor,
        keys_side,
        (((1,), (1,)), ((), ())),
        precision=lax.Precision.HIGHEST,
        preferred_element_type=jnp.float32,
    ) * anchor.shape[1] ** (-0.5)
    masked = jnp.where(key_live[None, :], sims, -1000000000.0)
    peak_score = jnp.max(masked, axis=1, keepdims=True)
    weights_exp = jnp.where(key_live[None, :], jnp.exp(masked - peak_score), 0.0)
    log_total = peak_score[:, 0] + jnp.log(jnp.sum(weights_exp, axis=1))
    match = (anchor_ids[:, None] == key_ids[None, :]) & key_live[None, :] & anchor_live[:, None]
    active_rows = jnp.any(match, axis=1)
    hit_score = jnp.sum(jnp.where(match, sims, 0.0), axis=1)
    return jnp.sum(jnp.where(active_rows, log_total - hit_score, 0.0))


def adamw(master, moment, square, gradient, factor, rate, decay):
    clipped = gradient * factor
    moment_new = BETA_ONE * moment + (1.0 - BETA_ONE) * clipped
    square_new = BETA_TWO * square + (1.0 - BETA_TWO) * clipped * clipped
    mean_hat = moment_new / (1.0 - BETA_ONE**STEP)
    square_hat = square_new / (1.0 - BETA_TWO**STEP)
    master_new = master - rate * (mean_hat / (jnp.sqrt(square_hat) + ADAM_EPS) + decay * master)
    return (master_new, moment_new, square_new)


def body(
    tokens,
    mlm_grad,
    doc_ids,
    span_counts,
    qkv_weight,
    proj_weight,
    inner_weight,
    outer_weight,
    affine_params,
    qkv_moment,
    proj_moment,
    inner_moment,
    outer_moment,
    affine_moment,
    qkv_square,
    proj_square,
    inner_square,
    outer_square,
    affine_square,
):
    rows, width = tokens.shape
    spans = rows // L
    half = width // 2
    order = block_order()
    hidden = inner_weight.shape[1]
    affine_cols = jnp.pad(affine_params.astype(BF16).T, ((0, 0), (0, LANES - affine_params.shape[0])))
    block_one = chip_rows(qkv_weight.astype(BF16), (half, half, half), affine_cols)
    block_two = chip_rows(
        jnp.concatenate([proj_weight.astype(BF16), inner_weight.astype(BF16)], 1), (half, hidden // 2)
    )
    block_three = chip_rows(outer_weight.astype(BF16), (half,))
    qkv_pieces = tuple((0, width * k, half, half * k) for k in range(3))
    two_pieces = ((0, 0, half, 0), (1, 0, hidden // 2, half))
    outer_pieces = ((0, 0, half, 0),)
    own_one, other_one = gather_blocks(block_one)
    own_two, other_two = gather_blocks(block_two)
    own_three, other_three = gather_blocks(block_three)
    qkv_w, = moved(order, own_one, other_one, ((width, 3 * width),), qkv_pieces)
    affine = (
        jnp.zeros(own_one.shape[:2] + (LANES,), BF16)
        .at[order[0]]
        .set(own_one[:, :, 3 * half :])
        .reshape(width, LANES)
        .T.astype(F32)
    )
    proj_w, inner_w = moved(order, own_two, other_two, ((width, width), (width, hidden)), two_pieces)
    outer_w, = moved(order, own_three, other_three, ((hidden, width),), outer_pieces)
    gain_one, shift_one, gain_two, shift_two = (affine[0], affine[1], affine[2], affine[3])
    bias_query, bias_value, bias_proj, bias_outer = (affine[4], affine[5], affine[6], affine[7])
    bias_inner = affine[8:12].reshape(hidden)
    qkv_bias = jnp.concatenate([bias_query, jnp.zeros((width,), jnp.float32), bias_value])
    queries, key_rows, values, attention, attention_low, context = attend(tokens, qkv_w, qkv_bias)
    attended = jnp.dot(context, proj_w, preferred_element_type=jnp.float32) + bias_proj
    normed_one, inv_one = normalize(tokens.astype(jnp.float32) + attended)
    skip_rows = normed_one * gain_one + shift_one
    skip_low = skip_rows.astype(jnp.bfloat16)
    inner_pre = jnp.dot(skip_low, inner_w, preferred_element_type=jnp.float32) + bias_inner
    activated = jax.nn.gelu(inner_pre, approximate=False).astype(jnp.bfloat16)
    outer_out = jnp.dot(activated, outer_w, preferred_element_type=jnp.float32) + bias_outer
    normed_two, inv_two = normalize(skip_rows + outer_out)
    result = normed_two * gain_two + shift_two
    layer_out = result.astype(jnp.bfloat16)
    cls_rows = layer_out.reshape(spans, L, width)[:, 0, :]
    side = lax.axis_index("pair")
    own_ids = jnp.where(side == 0, doc_ids[0], doc_ids[1])
    other_ids = jnp.where(side == 0, doc_ids[1], doc_ids[0])
    own_count = jnp.where(side == 0, span_counts[0], span_counts[1])
    other_count = jnp.where(side == 0, span_counts[1], span_counts[0])
    slot_index = jnp.arange(spans)
    own_live = slot_index < own_count
    other_live = slot_index < other_count
    partner_cls = core_swapped(cls_rows)

    def contrast_local(anchor, keys_side):
        return contrast(anchor, keys_side, own_ids, other_ids, own_live, other_live)

    loss_part, pull_back = jax.vjp(
        contrast_local, cls_rows.astype(jnp.float32), partner_cls.astype(jnp.float32)
    )
    grad_own, grad_other = pull_back(jnp.asarray(LOSS_WEIGHT, jnp.float32))
    grad_returned = core_swapped(grad_other)
    grad_cls = grad_own + grad_returned
    row_live = jnp.repeat(own_live, L).astype(jnp.float32)
    upstream = mlm_grad.astype(jnp.float32) * row_live[:, None]
    upstream = upstream.reshape(spans, L, width).at[:, 0, :].add(grad_cls).reshape(rows, width)
    gain_two_grad = jnp.sum(upstream * normed_two, axis=0)
    shift_two_grad = jnp.sum(upstream, axis=0)
    grad_two = normalize_back(upstream, normed_two, inv_two, gain_two)
    bias_outer_grad = jnp.sum(grad_two, axis=0)
    grad_two_low = grad_two.astype(jnp.bfloat16)
    outer_grad = contract_rows(activated, grad_two_low)
    act_grad = contract_cols(grad_two_low, outer_w)
    _, gelu_pull = jax.vjp(partial(jax.nn.gelu, approximate=False), inner_pre)
    inner_grad_pre = gelu_pull(act_grad)[0]
    bias_inner_grad = jnp.sum(inner_grad_pre, axis=0)
    inner_low = inner_grad_pre.astype(jnp.bfloat16)
    inner_grad = contract_rows(skip_low, inner_low)
    skip_grad = contract_cols(inner_low, inner_w) + grad_two
    gain_one_grad = jnp.sum(skip_grad * normed_one, axis=0)
    shift_one_grad = jnp.sum(skip_grad, axis=0)
    grad_one = normalize_back(skip_grad, normed_one, inv_one, gain_one)
    bias_proj_grad = jnp.sum(grad_one, axis=0)
    grad_one_low = grad_one.astype(jnp.bfloat16)
    proj_grad = contract_rows(context, grad_one_low)
    context_grad = (
        contract_cols(grad_one_low, proj_w).astype(jnp.bfloat16).reshape(spans, L, HEADS, HD)
    )
    attention_grad = jnp.einsum(
        "nqhe,nkhe->nhqk", context_grad, values, preferred_element_type=jnp.float32
    )
    value_grad = jnp.einsum(
        "nhqk,nqhe->nkhe", attention_low, context_grad, preferred_element_type=jnp.float32
    )
    score_grad = attention * (
        attention_grad - jnp.sum(attention_grad * attention, axis=-1, keepdims=True)
    )
    score_low = (score_grad * HD ** (-0.5)).astype(jnp.bfloat16)
    query_grad = jnp.einsum(
        "nhqk,nkhe->nqhe", score_low, key_rows, preferred_element_type=jnp.float32
    )
    key_grad = jnp.einsum("nhqk,nqhe->nkhe", score_low, queries, preferred_element_type=jnp.float32)
    qkv_rows_grad = jnp.stack([query_grad, key_grad, value_grad], axis=2).reshape(rows, 3 * width)
    bias_query_grad = jnp.sum(query_grad.reshape(rows, width), axis=0)
    bias_value_grad = jnp.sum(value_grad.reshape(rows, width), axis=0)
    qkv_low = qkv_rows_grad.astype(jnp.bfloat16)
    qkv_grad = contract_rows(tokens, qkv_low)
    input_grad = contract_cols(qkv_low, qkv_w) + grad_one
    affine_grad = jnp.concatenate(
        [
            jnp.stack(
                [
                    gain_one_grad,
                    shift_one_grad,
                    gain_two_grad,
                    shift_two_grad,
                    bias_query_grad,
                    bias_value_grad,
                    bias_proj_grad,
                    bias_outer_grad,
                ]
            ),
            bias_inner_grad.reshape(4, width),
        ],
        axis=0,
    )
    rows_chip = block_one.shape[0]
    own, other = parted(order, (outer_grad.astype(BF16),), outer_weight.shape[0] * 2, half, outer_pieces)
    sum_outer = reduce_blocks(own, other)
    own, other = parted(order, (inner_grad.astype(BF16),), rows_chip, hidden // 2, ((0, 0, hidden // 2, 0),))
    sum_inner = reduce_blocks(own, other)
    own, other = parted(
        order,
        (proj_grad.astype(BF16), qkv_grad.astype(BF16)),
        rows_chip,
        4 * half,
        ((0, 0, half, 0),) + tuple((1, width * k, half, half * (k + 1)) for k in range(3)),
    )
    sum_rest = reduce_blocks(own, other)
    spread = jnp.pad(affine_grad, ((0, LANES - affine_grad.shape[0]), (0, 0))).T.astype(BF16)
    spread = spread.reshape(-1, rows_chip, LANES)
    sum_affine = reduce_blocks(spread[order[0]], spread[order[1]])
    rest = shard_of(sum_rest, (half, half, half, half), side)
    rows_own = qkv_weight.shape[0]
    affine_shard = lax.dynamic_slice_in_dim(sum_affine, side * rows_own, rows_own).T[: affine_params.shape[0]]
    shards = (
        rest[:, width:],
        rest[:, :width],
        shard_of(sum_inner, (hidden // 2,), side),
        shard_of(sum_outer, (half,), side),
        affine_shard,
    )
    local_squares = jnp.sum(jnp.stack([jnp.sum(shard_item * shard_item) for shard_item in shards]))
    totals = total_over_devices(jnp.stack([local_squares, loss_part])[:, None] * jnp.ones((1, LANES), F32))
    grad_norm = jnp.sqrt(totals[0, 0])
    factor = jnp.minimum(1.0, CLIP_NORM / (grad_norm + 1e-06))
    mean_loss = totals[1, 0] / (spans * lax.axis_size("dp") * lax.axis_size("pair"))
    masters = (qkv_weight, proj_weight, inner_weight, outer_weight, affine_params)
    moments = (qkv_moment, proj_moment, inner_moment, outer_moment, affine_moment)
    squares_old = (qkv_square, proj_square, inner_square, outer_square, affine_square)
    rates = (RATE_MATRIX, RATE_MATRIX, RATE_MATRIX, RATE_MATRIX, RATE_AFFINE)
    decays = (DECAY_MATRIX, DECAY_MATRIX, DECAY_MATRIX, DECAY_MATRIX, DECAY_AFFINE)
    updated = [
        adamw(
            masters[index],
            moments[index],
            squares_old[index],
            shards[index],
            factor,
            rates[index],
            decays[index],
        )
        for index in range(5)
    ]
    return (
        updated[0][0],
        updated[1][0],
        updated[2][0],
        updated[3][0],
        updated[4][0],
        updated[0][1],
        updated[1][1],
        updated[2][1],
        updated[3][1],
        updated[4][1],
        updated[0][2],
        updated[1][2],
        updated[2][2],
        updated[3][2],
        updated[4][2],
        layer_out,
        input_grad,
        grad_norm,
        mean_loss,
    )


def solution(mesh):
    placed = (
        P(("dp", "pair"), None),
        P(("dp", "pair"), None),
        P("dp", None),
        P("dp"),
        P(("dp", "pair"), None),
        P(("dp", "pair"), None),
        P(("dp", "pair"), None),
        P(("dp", "pair"), None),
        P(None, ("dp", "pair")),
        P(("dp", "pair"), None),
        P(("dp", "pair"), None),
        P(("dp", "pair"), None),
        P(("dp", "pair"), None),
        P(None, ("dp", "pair")),
        P(("dp", "pair"), None),
        P(("dp", "pair"), None),
        P(("dp", "pair"), None),
        P(("dp", "pair"), None),
        P(None, ("dp", "pair")),
    )
    return jax.shard_map(
        body,
        mesh=mesh,
        in_specs=placed,
        out_specs=(
            P(("dp", "pair"), None),
            P(("dp", "pair"), None),
            P(("dp", "pair"), None),
            P(("dp", "pair"), None),
            P(None, ("dp", "pair")),
            P(("dp", "pair"), None),
            P(("dp", "pair"), None),
            P(("dp", "pair"), None),
            P(("dp", "pair"), None),
            P(None, ("dp", "pair")),
            P(("dp", "pair"), None),
            P(("dp", "pair"), None),
            P(("dp", "pair"), None),
            P(("dp", "pair"), None),
            P(None, ("dp", "pair")),
            P(("dp", "pair"), None),
            P(("dp", "pair"), None),
            P(),
            P(),
        ),
        check_vma=False,
    )
```

```python
from functools import partial

import jax
import jax.numpy as jnp
from jax import lax
from jax.experimental import pallas as pl
from jax.experimental.pallas import tpu as pltpu
from jax.sharding import PartitionSpec as P

HEADS = 12
HD = 64
L = 128
STEP = 10
LANES = 128
AXES = ("dp", "pair")


LN_EPS = 1e-12
LOSS_WEIGHT = 8.0
CLIP_NORM = 1000.0
BETA_ONE = 0.9
BETA_TWO = 0.999
ADAM_EPS = 1e-08
RATE_MATRIX = 0.05
DECAY_MATRIX = 0.01
RATE_AFFINE = 0.8
DECAY_AFFINE = 0.0

BF16 = jnp.bfloat16
F32 = jnp.float32


def flip_steps(chips):
    bits = chips.bit_length() - 1
    if bits == 4:
        return ((2, 3), (3, 2), (0, 1), (1, 0))
    return tuple((bit, bit) for bit in reversed(range(bits)))


def flip_route(chips, pair_of_bits):
    return [
        (2 * d + c, 2 * (d ^ (1 << pair_of_bits[c])) + c) for d in range(chips) for c in range(2)
    ]


def core_route(chips):
    return [(2 * d + c, 2 * d + 1 - c) for d in range(chips) for c in range(2)]


def flipped(block, bits):
    chips = lax.axis_size("dp")
    return lax.ppermute(block, AXES, flip_route(chips, bits))


def core_swapped(block):
    return lax.ppermute(block, AXES, core_route(lax.axis_size("dp")))


def block_order():
    chips = lax.axis_size("dp")
    d, c = lax.axis_index("dp"), lax.axis_index("pair")
    steps = flip_steps(chips)
    index = jnp.arange(chips, dtype=jnp.int32)
    blocks, places = [], []
    for core in range(2):
        blocks.append(sum((index >> k & 1) << step[core] for k, step in enumerate(steps)) ^ d)
        places.append(sum(((index ^ d) >> step[core] & 1) << k for k, step in enumerate(steps)))
    rows = []
    for pairs in (blocks, places):
        rows += [pick(c, pairs[0], pairs[1]), pick(c, pairs[1], pairs[0])]
    return jnp.stack(rows + [jnp.full((chips,), c, jnp.int32)])


def kernel_order(order, rows):
    if rows % 16 == 0:
        return order
    index = jnp.arange(16, dtype=jnp.int32)
    return jnp.stack([index] * 4 + [jnp.full((16,), order[4, 0], jnp.int32)])


def in_order(order, own, other, rows):
    if rows % 16 == 0:
        return own, other
    return tuple(
        blocks.reshape(order.shape[1], rows, -1)[order[side]] for side, blocks in enumerate((own, other))
    )


def pick(core, first, second):
    return jnp.where(core == 0, first, second)


def halves_of(low, pieces):
    core = lax.axis_index("pair")
    first, second, at = [], [], 0
    for width in pieces:
        first.append(low[:, at : at + width])
        second.append(low[:, at + width : at + 2 * width])
        at += 2 * width
    first, second = jnp.concatenate(first, 1), jnp.concatenate(second, 1)
    return pick(core, first, second), pick(core, second, first)


def chip_rows(low, pieces, extra=None):
    core = lax.axis_index("pair")
    own, other = halves_of(low, pieces)
    if extra is not None:
        own, other = (jnp.concatenate([half, extra], 1) for half in (own, other))
    got = core_swapped(other)
    return pick(core, jnp.concatenate([own, got]), jnp.concatenate([got, own]))


def tied(value, *others):
    return lax.optimization_barrier((value, *others))[0]


class Gather:
    def __init__(self, block):
        self.held, self.got, self.left = block[None], None, list(flip_steps(lax.axis_size("dp")))

    def step(self, *others):
        if self.got is not None:
            self.held = jnp.concatenate([self.held, self.got], axis=0)
        self.got = flipped(tied(self.held, *others), self.left.pop(0))
        return self.got

    def finish(self, order, rows, *others):
        while self.left:
            self.step()
        own = tied(jnp.concatenate([self.held, self.got], axis=0), *others)
        other = core_swapped(own)
        if rows % 16:
            own, other = (
                jnp.zeros(ref.shape, BF16).at[order[side]].set(ref).reshape(16, -1, ref.shape[2])
                for side, ref in enumerate((own, other))
            )
        return own, other


class Reduce:
    def __init__(self, own, other):
        self.count, self.left = own.shape[0], list(reversed(flip_steps(lax.axis_size("dp"))))
        self.parts = [own, core_swapped(other)]

    def last(self):
        return self.parts[-1]

    def step(self, *others):
        self.count //= 2
        sent = sum(p[self.count : 2 * self.count].astype(F32) for p in self.parts).astype(BF16)
        self.parts.append(flipped(tied(sent, *others), self.left.pop(0)))
        return self.parts[-1]

    def finish(self):
        while self.left:
            self.step()
        return self.parts


def total_over_devices(value):
    chips = lax.axis_size("dp")
    value = value + core_swapped(value)
    for bit in range(chips.bit_length() - 1):
        value = value + flipped(value, (bit, bit))
    return value


TILE = 256
PART = 256
PAIR_LANES = 2 * HD
VMEM_LIMIT = 32 * 1024 * 1024
SMEM = pl.BlockSpec(memory_space=pltpu.SMEM)
ANY = pl.BlockSpec(memory_space=pl.ANY)


def call(kernel, grid, ins, outs, scratch=(), micros=10, after=(), order=None):
    count = len(ins) + (order is not None)

    def body(*refs):
        kernel(*refs[:count], *refs[count + len(after) :])

    in_specs = [spec for _, spec in ins] + [ANY] * len(after)
    operands = [array for array, _ in ins] + list(after)
    if order is not None:
        operands = [order] + operands
    return pl.pallas_call(
        body,
        grid_spec=pltpu.PrefetchScalarGridSpec(
            num_scalar_prefetch=int(order is not None),
            grid=grid,
            in_specs=in_specs,
            out_specs=tuple(spec for _, spec in outs),
            scratch_shapes=list(scratch),
        ),
        out_shape=tuple(shape for shape, _ in outs),
        compiler_params=pltpu.CompilerParams(
            vmem_limit_bytes=VMEM_LIMIT, dimension_semantics=("arbitrary",) * len(grid)
        ),
        cost_estimate=pl.CostEstimate(
            flops=micros * 10_000_000_000, bytes_accessed=micros * 10_000_000, transcendentals=0
        ),
    )(*operands)


def whole(shape):
    return pl.BlockSpec(shape, lambda i, *_: (0,) * len(shape))


def rows_of(count, width):
    return pl.BlockSpec((count, width), lambda i, *_: (i, 0))


def cols_of(height, count):
    return pl.BlockSpec((height, count), lambda i, *_: (0, i))


def struct(shape, dtype):
    return jax.ShapeDtypeStruct(shape, dtype)


def dot(left, right):
    return jnp.dot(left, right, preferred_element_type=F32)


def contract_rows(left, right):
    return lax.dot_general(left, right, (((0,), (0,)), ((), ())), preferred_element_type=F32)


def contract_cols(left, right):
    return lax.dot_general(left, right, (((1,), (1,)), ((), ())), preferred_element_type=F32)


def normalize(total):
    centered = total - jnp.mean(total, axis=-1, keepdims=True)
    variance = jnp.mean(centered * centered, axis=-1, keepdims=True)
    scale_inv = lax.rsqrt(variance + LN_EPS)
    return (centered * scale_inv, scale_inv)


def normalize_back(upstream, normed, scale_inv, gain):
    scaled = upstream * gain
    return scale_inv * (
        scaled
        - jnp.mean(scaled, axis=-1, keepdims=True)
        - normed * jnp.mean(scaled * normed, axis=-1, keepdims=True)
    )


def gelu_and_slope(pre):
    below = 0.5 + 0.5 * lax.erf(pre * 0.5**0.5)
    return pre * below, below + pre * jnp.exp(pre * pre * -0.5) * (2 * jnp.pi) ** -0.5


def two_heads(block, lane_low):
    zero = jnp.zeros_like(block)
    return jnp.concatenate([jnp.where(lane_low, block, zero), jnp.where(lane_low, zero, block)], 0)


def lane_is_low(rows):
    return lax.broadcasted_iota(jnp.int32, (rows, PAIR_LANES), 1) < HD


def column_sum(value):
    return jnp.sum(value, axis=0, keepdims=True)


def fetches(order_ref, own_ref, other_ref, target, sems, rows, width, start=0, lane=0):
    core = order_ref[4, 0]
    copies = []
    for b in range(sems.shape[0]):
        pair = []
        for side, ref in enumerate((own_ref, other_ref)):
            half = core if side == 0 else 1 - core
            pair.append(
                pltpu.make_async_copy(
                    ref.at[order_ref[2 + side, b], :, pl.ds(lane, width)],
                    target.at[pl.ds(b * rows, rows), pl.ds(pl.multiple_of(start + half * width, LANES), width)],
                    sems.at[b, side],
                )
            )
        copies.append(pair)
    return copies


def begin(copies):
    for pair in copies:
        for copy in pair:
            copy.start()


def finish(copies):
    for pair in copies:
        for copy in pair:
            copy.wait()


def in_turn(count, *stages):
    held = stages[0](0)
    for n in range(count):
        value, held = held, stages[0](n + 1) if n + 1 < count else None
        for stage in stages[1:]:
            value = stage(n, value)


def projection_forward(order, tokens, own, other, affine_rows, after=()):
    rows, width = tokens.shape
    half = width // 2
    chips, block = own.shape[0], own.shape[1]

    def kernel(
        order_ref, tokens_ref, own_ref, other_ref, w_ref, proj_ref, affine_ref, out_ref, columns, sems, column_sems
    ):
        step = pl.program_id(0)
        params = [
            pltpu.make_async_copy(
                own_ref.at[order_ref[2, b], :, pl.ds(4 * half, LANES)],
                columns.at[pl.ds(b * block, block), :],
                column_sems.at[b],
            )
            for b in range(chips)
        ]
        parts = [
            fetches(order_ref, own_ref, other_ref, w_ref, sems.at[k], block, half, k * width, k * half)
            for k in range(3)
        ]
        parts.append(fetches(order_ref, own_ref, other_ref, proj_ref, sems.at[3], block, half, 0, 3 * half))

        @pl.when(step == 0)
        def _():
            for copy in params:
                copy.start()
            for copies in parts:
                begin(copies)
            for copy in params:
                copy.wait()
            affine_ref[...] = columns[...].astype(F32).T[:affine_rows]

        for k in range(3):

            @pl.when(step == k)
            def _():
                finish(parts[k])
                for n in range(width // TILE):
                    cols = slice(n * TILE, (n + 1) * TILE)
                    value = dot(tokens_ref[...], w_ref[:, k * width + n * TILE : k * width + (n + 1) * TILE])
                    if k != 1:
                        value += affine_ref[4 + k // 2 : 5 + k // 2, cols]
                    out_ref[:, cols] = value.astype(BF16)

        @pl.when(step == 2)
        def _():
            finish(parts[3])

    return call(
        kernel,
        (3,),
        [(tokens, whole(tokens.shape)), (own, ANY), (other, ANY)],
        [
            (struct((width, 3 * width), BF16), whole((width, 3 * width))),
            (struct((width, width), BF16), whole((width, width))),
            (struct((affine_rows, width), F32), whole((affine_rows, width))),
            (struct((rows, 3 * width), BF16), cols_of(rows, width)),
        ],
        [
            pltpu.VMEM((width, LANES), BF16),
            pltpu.SemaphoreType.DMA((4, chips, 2)),
            pltpu.SemaphoreType.DMA((chips,)),
        ],
        8,
        after,
        order,
    )


def attention_forward(tokens, projected, proj_w, affine, after=()):
    rows, width = tokens.shape
    spans, pairs = rows // L, width // PAIR_LANES
    each = PART // L

    def kernel(
        tokens_ref, projected_ref, proj_ref, affine_ref,
        attention_ref, context_ref, normed_ref, inv_ref, skip_ref,
    ):
        lane_low = lane_is_low(L)

        def read(n, part):
            s, p = divmod(n, pairs)
            at = part * width + p * PAIR_LANES
            return projected_ref[s * L : (s + 1) * L, at : at + PAIR_LANES]

        def scored(n):
            return contract_cols(two_heads(read(n, 0) * jnp.asarray(HD**-0.5, BF16), lane_low), read(n, 1))

        def weighed(n, scores):
            s, p = divmod(n, pairs)
            exponent = jnp.exp(scores - jnp.max(scores, axis=-1, keepdims=True))
            low = (exponent * (1.0 / jnp.sum(exponent, axis=-1, keepdims=True))).astype(BF16)
            attention_ref[s, p] = low
            both = dot(low, read(n, 2))
            context_ref[s * L : (s + 1) * L, p * PAIR_LANES : (p + 1) * PAIR_LANES] = jnp.where(
                lane_low, both[:L], both[L:]
            ).astype(BF16)

        in_turn(each * pairs, scored, weighed)
        total = dot(context_ref[...], proj_ref[...]) + affine_ref[6:7, :]
        normed, inv = normalize(tokens_ref[...].astype(F32) + total)
        normed_ref[...] = normed
        inv_ref[...] = jnp.broadcast_to(inv, (PART, LANES))
        skip_ref[...] = (normed * affine_ref[0:1, :] + affine_ref[1:2, :]).astype(BF16)

    return call(
        kernel,
        (rows // PART,),
        [
            (tokens, rows_of(PART, width)),
            (projected, rows_of(PART, 3 * width)),
            (proj_w, whole(proj_w.shape)),
            (affine, whole(affine.shape)),
        ],
        [
            (
                struct((spans, pairs, 2 * L, L), BF16),
                pl.BlockSpec((each, pairs, 2 * L, L), lambda i, *_: (i, 0, 0, 0)),
            ),
            (struct((rows, width), BF16), rows_of(PART, width)),
            (struct((rows, width), F32), rows_of(PART, width)),
            (struct((rows, LANES), F32), rows_of(PART, LANES)),
            (struct((rows, width), BF16), rows_of(PART, width)),
        ],
        (),
        12,
        after,
    )


def inner_forward(order, side, skip_low, blocks, affine, after=()):
    rows, width = skip_low.shape
    chips, block, half = blocks.shape

    def kernel(order_ref, skip_ref, blocks_ref, affine_ref, w_ref, act_ref, slope_ref, sems):
        step = pl.program_id(0)

        def copies(b):
            return pltpu.make_async_copy(
                blocks_ref.at[order_ref[2 + side, b]], w_ref.at[pl.ds(b * block, block), :], sems.at[b]
            )

        @pl.when(step == 0)
        def _():
            for b in range(chips):
                copies(b).start()
            for b in range(chips):
                copies(b).wait()

        first = order_ref[4, 0] if side == 0 else 1 - order_ref[4, 0]
        bias = affine_ref[pl.ds(8 + first * (half // width) + step, 1), :]
        parts = rows // PART

        def entered(n):
            k, r = divmod(n, parts)
            weight = w_ref[:, pl.ds(pl.multiple_of(step * width + k * TILE, LANES), TILE)]
            return dot(skip_ref[r * PART : (r + 1) * PART, :], weight)

        def activated(n, value):
            k, r = divmod(n, parts)
            at, cols = slice(r * PART, (r + 1) * PART), slice(k * TILE, (k + 1) * TILE)
            act, slope = gelu_and_slope(value + bias[:, cols])
            act_ref[at, cols] = act.astype(BF16)
            slope_ref[at, cols] = slope.astype(BF16)

        in_turn(width // TILE * parts, entered, activated)

    return call(
        kernel,
        (half // width,),
        [(skip_low, whole(skip_low.shape)), (blocks, ANY), (affine, whole(affine.shape))],
        [
            (struct((width, half), BF16), whole((width, half))),
            (struct((rows, half), BF16), cols_of(rows, width)),
            (struct((rows, half), BF16), cols_of(rows, width)),
        ],
        [pltpu.SemaphoreType.DMA((chips,))],
        10,
        after,
        order,
    )


def outer_forward(order, act_own, act_other, own, other, normed_one, affine, mlm_grad, live_rows, after=()):
    rows, wide = act_own.shape
    hidden, width = 2 * wide, normed_one.shape[1]
    chips, block = own.shape[0], own.shape[1]
    spans = rows // L
    many = 2
    tile = many * PART

    def kernel(
        order_ref, act_own_ref, act_other_ref, own_ref, other_ref, normed_one_ref, affine_ref, mlm_ref, live_ref,
        w_ref, out_ref, grad_ref, low_ref, sums_ref, cls_ref, cls_normed_ref, cls_inv_ref, sems,
    ):
        step = pl.program_id(0)

        core = order_ref[4, 0]

        def entered(n):
            at = slice(n * PART, (n + 1) * PART)
            total = 0.0
            for k, ref in enumerate((act_own_ref, act_other_ref)):
                start = (core if k == 0 else 1 - core) * wide
                total = total + dot(ref[at, :], w_ref[pl.ds(pl.multiple_of(start, LANES), wide), :])
            return total

        def ended(n, total):
            at = slice(n * PART, (n + 1) * PART)
            skip = normed_one_ref[at, :] * affine_ref[0:1, :] + affine_ref[1:2, :]
            normed, inv = normalize(skip + (total + affine_ref[7:8, :]))
            out = (normed * affine_ref[2:3, :] + affine_ref[3:4, :]).astype(BF16)
            out_ref[at, :] = out
            line = lax.broadcasted_iota(jnp.int32, (PART, 1), 0)
            live = line < live_ref[0] - (step * many + n) * PART
            upstream = jnp.where(live, mlm_ref[at, :].astype(F32), 0.0)
            grad = normalize_back(upstream, normed, inv, affine_ref[2:3, :])
            grad_ref[at, :] = grad
            low_ref[at, :] = grad.astype(BF16)
            for k, value in enumerate((upstream * normed, upstream, grad)):
                sums_ref[k : k + 1, :] += column_sum(value)
            for s in range(PART // L):
                row, to = slice(s * L, s * L + 1), pl.ds((step * many + n) * (PART // L) + s, 1)
                cls_ref[to, :] = out[s * L : s * L + 16].astype(F32)[:1]
                cls_normed_ref[to, :] = normed[row]
                cls_inv_ref[to, :] = jnp.broadcast_to(inv[row], (1, LANES))

        copies = fetches(order_ref, own_ref, other_ref, w_ref, sems, block, width // 2)

        @pl.when(step == 0)
        def _():
            begin(copies)
            sums_ref[...] = jnp.zeros_like(sums_ref)
            finish(copies)

        in_turn(many, entered, ended)

    return call(
        kernel,
        (rows // tile,),
        [
            (act_own, rows_of(tile, wide)),
            (act_other, rows_of(tile, wide)),
            (own, ANY),
            (other, ANY),
            (normed_one, rows_of(tile, width)),
            (affine, whole(affine.shape)),
            (mlm_grad, rows_of(tile, width)),
            (live_rows, SMEM),
        ],
        [
            (struct((hidden, width), BF16), whole((hidden, width))),
            (struct((rows, width), BF16), rows_of(tile, width)),
            (struct((rows, width), F32), rows_of(tile, width)),
            (struct((rows, width), BF16), rows_of(tile, width)),
            (struct((8, width), F32), whole((8, width))),
            (struct((spans, width), F32), whole((spans, width))),
            (struct((spans, width), F32), whole((spans, width))),
            (struct((spans, LANES), F32), whole((spans, LANES))),
        ],
        [pltpu.SemaphoreType.DMA((chips, 2))],
        8,
        after,
        order,
    )


def loss_and_gradient(own, other, match, key_live, anchor_live):
    scale = own.shape[1] ** -0.5
    sims = contract_cols(own.astype(BF16), other.astype(BF16)) * scale
    step = jnp.zeros_like(sims)
    loss = None
    for axis, live in ((1, key_live), (0, anchor_live)):
        masked = jnp.where(live > 0, sims, -1000000000.0)
        peak = jnp.max(masked, axis=axis, keepdims=True)
        weights = jnp.where(live > 0, jnp.exp(masked - peak), 0.0)
        total = jnp.sum(weights, axis=axis, keepdims=True)
        active = jnp.max(match, axis=axis, keepdims=True)
        step += active * (weights / total - match)
        if loss is None:
            hit = jnp.sum(match * sims, axis=axis, keepdims=True)
            loss = jnp.sum(jnp.where(active > 0, peak + jnp.log(total) - hit, 0.0), axis=0, keepdims=True)
    step *= LOSS_WEIGHT * scale
    gradient = jnp.zeros_like(own)
    for k in range(other.shape[0]):
        gradient += step[:, k : k + 1] * other[k : k + 1, :]
    return loss, gradient


def outer_backward(order, grad_low, sums, cls, cls_other, masks, cls_normed, cls_inv, act_own, act_other, affine, after=()):
    rows, width = grad_low.shape
    hidden = 2 * act_own.shape[1]
    chips = order.shape[1]
    block, half = hidden // chips, width // 2
    tile = 4 * block
    turn = chips // 8
    spans = rows // L

    def kernel(
        order_ref, low_in_ref, sums_in_ref, cls_ref, cls_other_ref, masks_ref, normed_ref, inv_ref, act_own_ref, act_other_ref, affine_ref,
        low_ref, more_ref, sums_ref, loss_ref, own_ref, other_ref, own_held, other_held, sems,
    ):
        step = pl.program_id(0)

        @pl.when(step == 0)
        def _():
            loss, up = loss_and_gradient(
                cls_ref[...], cls_other_ref[...], masks_ref[0], masks_ref[1], masks_ref[2]
            )
            normed = normed_ref[...]
            more = normalize_back(up, normed, inv_ref[:, :1], affine_ref[2:3, :])
            more_ref[...] = more
            loss_ref[...] = jnp.broadcast_to(loss, loss_ref.shape)
            for k, value in enumerate((up * normed, up, more)):
                sums_ref[k : k + 1, :] = sums_in_ref[k : k + 1, :] + column_sum(value)
            low_ref[...] = low_in_ref[...]
            line = lax.broadcasted_iota(jnp.int32, (16, 1), 0)
            for s in range(spans):
                at = slice(s * L, s * L + 16)
                changed = low_in_ref[at, :].astype(F32) + jnp.where(line == 0, more[s : s + 1], 0.0)
                low_ref[at, :] = changed.astype(BF16)

        core = order_ref[4, 0]

        def gradient(act_ref, first):
            def entered(n):
                return contract_rows(act_ref[:, n * 2 * block : (n + 1) * 2 * block], low_ref[...])

            def ended(n, value):
                low, high = value[:, :half], value[:, half:]
                parts = (jnp.where(core == 0, low, high), jnp.where(core == 0, high, low))
                for side, (part, held, out) in enumerate(
                    zip(parts, (own_held, other_held), (own_ref, other_ref))
                ):
                    for k in range(2):
                        b = first + 2 * n + k
                        held[b] = part[k * block : (k + 1) * block].astype(BF16)
                        pltpu.make_async_copy(
                            held.at[b], out.at[order_ref[2 + side, b]], sems.at[side, b]
                        ).start()

            in_turn(2, entered, ended)

        @pl.when(step < turn)
        def _():
            gradient(act_own_ref, core * (chips // 2) + 4 * step)

        @pl.when(step >= turn)
        def _():
            gradient(act_other_ref, (1 - core) * (chips // 2) + 4 * (step - turn))

        @pl.when(step == 2 * turn - 1)
        def _():
            for side, (held, out) in enumerate(((own_held, own_ref), (other_held, other_ref))):
                for b in range(chips):
                    pltpu.make_async_copy(
                        held.at[b], out.at[order_ref[2 + side, b]], sems.at[side, b]
                    ).wait()

    shape = (chips, block, half)
    return call(
        kernel,
        (hidden // tile,),
        [
            (grad_low, whole(grad_low.shape)),
            (sums, whole(sums.shape)),
            (cls, whole(cls.shape)),
            (cls_other, whole(cls.shape)),
            (masks, whole(masks.shape)),
            (cls_normed, whole(cls.shape)),
            (cls_inv, whole(cls_inv.shape)),
            (act_own, pl.BlockSpec((rows, tile), lambda i, *_: (0, jnp.minimum(i, turn - 1)))),
            (act_other, pl.BlockSpec((rows, tile), lambda i, *_: (0, jnp.maximum(i - turn, 0)))),
            (affine, whole(affine.shape)),
        ],
        [
            (struct((rows, width), BF16), whole((rows, width))),
            (struct((spans, width), F32), whole((spans, width))),
            (struct((8, width), F32), whole((8, width))),
            (struct((8, LANES), F32), whole((8, LANES))),
            (struct(shape, BF16), ANY),
            (struct(shape, BF16), ANY),
        ],
        [
            pltpu.VMEM(shape, BF16),
            pltpu.VMEM(shape, BF16),
            pltpu.SemaphoreType.DMA((2, chips)),
        ],
        8,
        after,
        order,
    )


def inner_backward(order, side, low, slope, outer_w, skip_low, after=()):
    rows, width = low.shape
    hidden = 2 * slope.shape[1]
    chips = order.shape[1]
    block = width // chips
    steps = hidden // 2 // width

    def kernel(order_ref, low_ref, slope_ref, outer_ref, skip_ref, inner_ref, bias_ref, out_ref):
        step = pl.program_id(0)

        def entered(n):
            return contract_cols(low_ref[...], outer_ref[n * TILE : (n + 1) * TILE, :])

        def sloped(n, value):
            cols = slice(n * TILE, (n + 1) * TILE)
            inner_grad = value * slope_ref[:, cols].astype(F32)
            bias_ref[pl.ds(step, 1), cols] = column_sum(inner_grad)
            inner_low = inner_grad.astype(BF16)
            inner_ref[:, cols] = inner_low
            return contract_rows(skip_ref[...], inner_low).astype(BF16)

        def stored(n, value):
            for b in range(chips):
                out_ref[order_ref[2 + side, b], :, n * TILE : (n + 1) * TILE] = value[b * block : (b + 1) * block]

        in_turn(width // TILE, entered, sloped, stored)

    def place(i, table):
        half = table[4, 0] if side == 0 else 1 - table[4, 0]
        return half * steps + i

    return call(
        kernel,
        (steps,),
        [
            (low, whole(low.shape)),
            (slope, cols_of(rows, width)),
            (outer_w, pl.BlockSpec((width, width), lambda i, table: (place(i, table), 0))),
            (skip_low, whole(skip_low.shape)),
        ],
        [
            (struct((rows, hidden // 2), BF16), cols_of(rows, width)),
            (struct((8, width), F32), whole((8, width))),
            (
                struct((chips, block, hidden // 2), BF16),
                pl.BlockSpec((chips, block, width), lambda i, *_: (0, 0, i)),
            ),
        ],
        (),
        8,
        after,
        order,
    )


def skip_backward(inner_own, inner_other, w_own, w_other, grad_two, more, normed_one, inv_one, affine, proj_w, after=()):
    rows, width = grad_two.shape
    half = w_own.shape[1]
    many = 2
    tile = many * PART

    def kernel(
        own_ref, other_ref, w_own_ref, w_other_ref, grad_two_ref, more_ref, normed_ref, inv_ref, affine_ref, proj_ref,
        grad_ref, low_ref, sums_ref, context_ref,
    ):
        step = pl.program_id(0)

        @pl.when(step == 0)
        def _():
            sums_ref[...] = jnp.zeros_like(sums_ref)

        def entered(n):
            at = slice(n * PART, (n + 1) * PART)
            up = grad_two_ref[at, :]
            for ref, weight in ((own_ref, w_own_ref), (other_ref, w_other_ref)):
                up = up + contract_cols(ref[at, :], weight[...])
            return up

        def ended(n, up):
            at = slice(n * PART, (n + 1) * PART)
            line = lax.broadcasted_iota(jnp.int32, (PART, 1), 0)
            for s in range(PART // L):
                row = pl.ds((step * many + n) * (PART // L) + s, 1)
                up = up + jnp.where(line == s * L, more_ref[row, :], 0.0)
            normed = normed_ref[at, :]
            grad = normalize_back(up, normed, inv_ref[at, :1], affine_ref[0:1, :])
            grad_ref[at, :] = grad
            low = grad.astype(BF16)
            low_ref[at, :] = low
            for k, value in enumerate((up * normed, up, grad)):
                sums_ref[k : k + 1, :] += column_sum(value)
            context_ref[at, :] = contract_cols(low, proj_ref[...]).astype(BF16)

        in_turn(many, entered, ended)

    return call(
        kernel,
        (rows // tile,),
        [
            (inner_own, rows_of(tile, half)),
            (inner_other, rows_of(tile, half)),
            (w_own, whole(w_own.shape)),
            (w_other, whole(w_other.shape)),
            (grad_two, rows_of(tile, width)),
            (more, whole(more.shape)),
            (normed_one, rows_of(tile, width)),
            (inv_one, rows_of(tile, LANES)),
            (affine, whole(affine.shape)),
            (proj_w, whole(proj_w.shape)),
        ],
        [
            (struct((rows, width), F32), rows_of(tile, width)),
            (struct((rows, width), BF16), rows_of(tile, width)),
            (struct((8, width), F32), whole((8, width))),
            (struct((rows, width), BF16), rows_of(tile, width)),
        ],
        (),
        8,
        after,
    )


def attention_backward(pairs, context_grad, projected, attention, after=()):
    rows, width = context_grad.shape
    spans, count = rows // L, len(pairs)
    wide = 3 * count * PAIR_LANES
    each = 2

    def kernel(grad_ref, projected_ref, attention_ref, out_ref, sums_ref):
        @pl.when(pl.program_id(0) == 0)
        def _():
            sums_ref[...] = jnp.zeros_like(sums_ref)

        lane_low = lane_is_low(L)
        def entered(m):
            s, n = divmod(m, count)
            at, line = pairs[n] * PAIR_LANES, slice(s * L, (s + 1) * L)
            grads = two_heads(grad_ref[line, at : at + PAIR_LANES], lane_low)
            v = projected_ref[line, 2 * width + at : 2 * width + at + PAIR_LANES]
            return grads, contract_cols(grads, v)

        def ended(m, value):
            s, n = divmod(m, count)
            at, line = pairs[n] * PAIR_LANES, slice(s * L, (s + 1) * L)
            q, k = (
                projected_ref[line, part * width + at : part * width + at + PAIR_LANES] for part in range(2)
            )
            grads, back = value
            low = attention_ref[s, pairs[n]]
            weights = low.astype(F32)
            product = back * weights
            score = (product - weights * jnp.sum(product, axis=-1, keepdims=True)) * HD**-0.5
            score_low = score.astype(BF16)
            both = dot(score_low, k)
            parts = (
                jnp.where(lane_low, both[:L], both[L:]),
                contract_rows(score_low, two_heads(q, lane_low)),
                contract_rows(low, grads),
            )
            for part, value in enumerate(parts):
                to = slice((part * count + n) * PAIR_LANES, (part * count + n + 1) * PAIR_LANES)
                out_ref[line, to] = value.astype(BF16)
                sums_ref[:, to] += column_sum(value)

        in_turn(each * count, entered, ended)

    return call(
        kernel,
        (spans // each,),
        [
            (context_grad, rows_of(each * L, width)),
            (projected, rows_of(each * L, 3 * width)),
            (attention, pl.BlockSpec((each, width // PAIR_LANES, 2 * L, L), lambda i, *_: (i, 0, 0, 0))),
        ],
        [
            (struct((rows, wide), BF16), rows_of(each * L, wide)),
            (struct((1, wide), F32), whole((1, wide))),
        ],
        (),
        3 * count,
        after,
    )


def store_blocks(order_ref, low, high, rows, own_ref, other_ref, lane):
    core = order_ref[4, 0]
    own = jnp.where(core == 0, low, high).astype(BF16)
    other = jnp.where(core == 0, high, low).astype(BF16)
    width = low.shape[1]
    for b in range(low.shape[0] // rows):
        at = slice(b * rows, (b + 1) * rows)
        own_ref[order_ref[2, b], :, lane : lane + width] = own[at]
        other_ref[order_ref[3, b], :, lane : lane + width] = other[at]


def qkv_backward(order, tokens, qkv_low, proj=None, sums=None, after=()):
    rows, width = tokens.shape
    chips = order.shape[1]
    block, half = width // chips, width // 2
    each = qkv_low.shape[1] // 6
    extra = half if proj is not None else LANES

    def affine_rows(sums_one, sums_two, first, second, bias_own, bias_other, lines, core):
        lines[...] = jnp.zeros_like(lines)
        lines[0:2, :] = sums_one[0:2, :]
        lines[2:4, :] = sums_two[0:2, :]
        for row, part in ((4, 0), (5, 2)):
            for h in range(2):
                at = h * half
                for ref in (first, second):
                    wide = ref.shape[1] // 6
                    lines[row : row + 1, at : at + wide] = ref[:, (2 * part + h) * wide : (2 * part + h + 1) * wide]
                    at += wide
        lines[6:7, :] = sums_one[2:3, :]
        lines[7:8, :] = sums_two[2:3, :]
        lines[8:10, :] = jnp.where(core == 0, bias_own[0:2, :], bias_other[0:2, :])
        lines[10:12, :] = jnp.where(core == 0, bias_other[0:2, :], bias_own[0:2, :])
        return lines[...].T

    def kernel(order_ref, tokens_ref, qkv_ref, *rest):
        rest, (own_ref, other_ref, lines) = rest[:-3], rest[-3:]

        def entered(k):
            if k < 3:
                return contract_rows(tokens_ref[...], qkv_ref[:, 2 * k * each : 2 * (k + 1) * each])
            if proj is not None:
                return contract_rows(rest[0][...], rest[1][...])
            value = affine_rows(*rest, lines, order_ref[4, 0])
            return jnp.concatenate([value, value], axis=1)

        def ended(k, value):
            middle = value.shape[1] // 2
            store_blocks(order_ref, value[:, :middle], value[:, middle:], block, own_ref, other_ref, k * each)

        in_turn(4, entered, ended)

    shape = (chips, block, 3 * each + extra)
    more = list(proj if proj is not None else sums)
    return call(
        kernel,
        (1,),
        [(array, whole(array.shape)) for array in (tokens, qkv_low, *more)],
        [(struct(shape, BF16), whole(shape)), (struct(shape, BF16), whole(shape))],
        [pltpu.VMEM((LANES, width), F32)],
        5,
        after,
        order,
    )


def tokens_backward(groups, qkv_lows, qkv_w, grad_one, after=()):
    rows, width = grad_one.shape

    def kernel(*refs):
        lows, (w_ref, grad_ref, out_ref, held) = refs[: len(groups)], refs[len(groups) :]
        for pairs, ref in zip(groups, lows):
            for part in range(3):
                for n, p in enumerate(pairs):
                    held[:, part * width + p * PAIR_LANES : part * width + (p + 1) * PAIR_LANES] = ref[
                        :, (part * len(pairs) + n) * PAIR_LANES : (part * len(pairs) + n + 1) * PAIR_LANES
                    ]
        out_ref[...] = contract_cols(held[...], w_ref[...]) + grad_ref[...]

    return call(
        kernel,
        (rows // PART,),
        [(low, rows_of(PART, low.shape[1])) for low in qkv_lows]
        + [(qkv_w, whole(qkv_w.shape)), (grad_one, rows_of(PART, width))],
        [(struct((rows, width), F32), rows_of(PART, width))],
        [pltpu.VMEM((PART, 3 * width), BF16)],
        8,
        after,
    )[0]


def summed(order, chunks, doubled=(), loss=None, before=None):
    counts = [len(parts) for parts in chunks]
    shapes = [(parts[0].shape[1] // 2, parts[0].shape[2]) for parts in chunks]
    extras = [loss] if loss is not None else []
    extras += [before] if before is not None else []
    arrays = [p for parts in chunks for p in parts]

    def kernel(order_ref, *refs):
        core = order_ref[4, 0]
        squares = 0.0
        outs = refs[len(arrays) + len(extras) :]
        at = 0
        for n, count in enumerate(counts):
            rows, cols = shapes[n]
            total = sum(ref[0].astype(F32) for ref in refs[at : at + count])
            at += count
            first, second = total[:rows], total[rows:]
            mine, theirs = jnp.where(core == 0, first, second), jnp.where(core == 0, second, first)
            outs[2 * n][...] = mine
            outs[2 * n + 1][...] = theirs
            squares += jnp.sum(mine * mine)
            theirs = theirs[:, : cols - LANES] if n in doubled else theirs
            squares += jnp.sum(theirs * theirs)
        line = lax.broadcasted_iota(jnp.int32, (8, LANES), 0)
        result = jnp.where(line == 0, squares, 0.0)
        if loss is not None:
            result += jnp.where(line == 1, refs[len(arrays)][0:1, :], 0.0)
        if before is not None:
            result += refs[len(arrays) + len(extras) - 1][...]
        outs[-1][...] = result

    return call(
        kernel,
        (1,),
        [(p, pl.BlockSpec((1, *p.shape[1:]), lambda i, *_: (0, 0, 0))) for p in arrays]
        + [(x, whole(x.shape)) for x in extras],
        [(struct(s, F32), whole(s)) for s in shapes for _ in range(2)]
        + [(struct((8, LANES), F32), whole((8, LANES)))],
        (),
        2,
        (),
        order,
    )


def adamw(order, totals, grads, weights, moments, squares, slots):
    count = len(weights)
    shapes = [w.shape for w in weights]
    rates = (RATE_MATRIX,) * (count - 1) + (RATE_AFFINE,)
    decays = (DECAY_MATRIX,) * (count - 1) + (DECAY_AFFINE,)

    def kernel(order_ref, totals_ref, *refs):
        core = order_ref[4, 0]
        grad_refs, refs = refs[: len(grads)], refs[len(grads) :]
        olds, outs = refs[: 3 * count], refs[3 * count :]
        norm = jnp.sqrt(totals_ref[0:1, :])
        outs[-1][...] = jnp.concatenate([norm, totals_ref[1:2, :] / slots, jnp.zeros((6, LANES), F32)], 0)
        factor = jnp.minimum(1.0, CLIP_NORM / (norm[:, 0:1] + 1e-06))

        def update(n, at, gradient):
            master, moment, square = (olds[3 * n + k][at] for k in range(3))
            clipped = gradient * factor
            moment = BETA_ONE * moment + (1.0 - BETA_ONE) * clipped
            square = BETA_TWO * square + (1.0 - BETA_TWO) * clipped * clipped
            mean_hat = moment / (1.0 - BETA_ONE**STEP)
            square_hat = square / (1.0 - BETA_TWO**STEP)
            master = master - rates[n] * (mean_hat / (jnp.sqrt(square_hat) + ADAM_EPS) + decays[n] * master)
            for k, value in enumerate((master, moment, square)):
                outs[3 * n + k][at] = value

        def pieces(n, start, chunk, lane, width):
            mine, got = grad_refs[2 * chunk], grad_refs[2 * chunk + 1]
            for h in range(2):
                first, second = mine[:, lane : lane + width], got[:, lane : lane + width]
                value = jnp.where(core == h, first, second)
                update(n, (slice(None), slice(start[h], start[h] + width)), value)

        width = shapes[0][1] // 3
        half = width // 2
        each = half // 3
        for k in range(3):
            at = k * width
            pieces(0, (at, at + half), 3, k * each, each)
            pieces(0, (at + each, at + half + each), 2, 2 * k * each, 2 * each)
        pieces(1, (0, half), 2, 6 * each, half)
        pieces(2, (0, shapes[2][1] // 2), 1, 0, shapes[2][1] // 2)
        pieces(3, (0, half), 0, 0, half)
        update(4, (slice(None), slice(None)), grad_refs[-1][...])

    olds = [array for n in range(count) for array in (weights[n], moments[n], squares[n])]
    return call(
        kernel,
        (1,),
        [(a, whole(a.shape)) for a in (totals, *grads, *olds)],
        [(struct(s, F32), whole(s)) for s in shapes for _ in range(3)]
        + [(struct((8, LANES), F32), whole((8, LANES)))],
        (),
        4,
        (),
        order,
    )


def body(
    tokens,
    mlm_grad,
    doc_ids,
    span_counts,
    qkv_weight,
    proj_weight,
    inner_weight,
    outer_weight,
    affine_params,
    qkv_moment,
    proj_moment,
    inner_moment,
    outer_moment,
    affine_moment,
    qkv_square,
    proj_square,
    inner_square,
    outer_square,
    affine_square,
):
    rows, width = tokens.shape
    spans = rows // L
    half = width // 2
    order = block_order()
    hidden = inner_weight.shape[1]
    pairs = width // PAIR_LANES
    affine_rows = affine_params.shape[0]
    affine_cols = jnp.pad(affine_params.astype(BF16).T, ((0, 0), (0, LANES - affine_rows)))
    block_one = chip_rows(
        jnp.concatenate([qkv_weight.astype(BF16), proj_weight.astype(BF16)], 1), (half,) * 4, affine_cols
    )
    block_two = chip_rows(inner_weight.astype(BF16), (hidden // 2,))
    block_three = chip_rows(outer_weight.astype(BF16), (half,))
    rows_chip, rows_outer = block_one.shape[0], block_three.shape[0]
    table = kernel_order(order, rows_chip)

    side = lax.axis_index("pair")
    own_ids, other_ids = pick(side, doc_ids[0], doc_ids[1]), pick(side, doc_ids[1], doc_ids[0])
    own_count, other_count = (
        pick(side, span_counts[0], span_counts[1]),
        pick(side, span_counts[1], span_counts[0]),
    )
    slot = jnp.arange(spans)
    anchor_live = jnp.broadcast_to((slot < own_count)[:, None], (spans, spans))
    key_live = jnp.broadcast_to((slot < other_count)[None, :], (spans, spans))
    match = (own_ids[:, None] == other_ids[None, :]) & anchor_live & key_live
    masks = jnp.stack([match, key_live, anchor_live]).astype(F32)
    live_rows = (own_count * L)[None]

    one, two, three = Gather(block_one), Gather(block_two), Gather(block_three)
    one.step()
    first = one.step()
    one.step()
    two.step(first)
    second = (one.got, two.got)
    one.step(*second)
    two.step(*second)
    three.step(*second)
    third = (one.got, two.got, three.got)
    own, other = one.finish(order, rows_chip, *third)
    two.step(*third)
    three.step(*third)
    fourth = (two.got, three.got)
    two.step(*fourth, other)
    qkv_w, proj_w, affine, projected = projection_forward(table, tokens, own, other, affine_rows)
    three.step(two.got, projected)
    attention, context, normed_one, inv_one, skip_low = attention_forward(tokens, projected, proj_w, affine)
    own, other = two.finish(order, rows_chip)
    three.step(skip_low)
    w_own, act_own, slope_own = inner_forward(table, 0, skip_low, own, affine)
    w_other, act_other, slope_other = inner_forward(table, 1, skip_low, other, affine)
    own, other = three.finish(order, rows_outer, act_own)
    outer_w, layer_out, grad_two, low, sums_two, cls, cls_normed, cls_inv = outer_forward(
        table, act_own, act_other, own, other, normed_one, affine, mlm_grad, live_rows
    )
    low, more, sums_two, loss, own, other = outer_backward(
        table, low, sums_two, cls, core_swapped(cls), masks, cls_normed, cls_inv, act_own, act_other, affine
    )

    red_outer = Reduce(*in_order(order, own, other, rows_outer))
    inner_other, bias_other, blocks_other = inner_backward(table, 1, low, slope_other, outer_w, skip_low)
    got = red_outer.last()
    inner_own, bias_own, blocks_own = inner_backward(table, 0, low, slope_own, outer_w, skip_low, (got,))
    red_outer.step()
    red_inner = Reduce(*in_order(order, blocks_own, blocks_other, rows_chip))
    grad_one, grad_one_low, sums_one, context_grad = skip_backward(
        inner_own, inner_other, w_own, w_other, grad_two, more, normed_one, inv_one, affine, proj_w,
        (red_inner.last(),),
    )
    groups = (
        tuple(p for p in range(pairs) if p % (pairs // 2)),
        tuple(p for p in range(pairs) if not p % (pairs // 2)),
    )
    qkv_low, qkv_sums = [None, None], [None, None]
    qkv_low[0], qkv_sums[0] = attention_backward(
        groups[0], context_grad, projected, attention, (red_outer.last(),)
    )
    red_outer.step()
    red_inner.step()
    own, other = qkv_backward(
        table, tokens, qkv_low[0], (context, grad_one_low), None, (red_outer.last(),)
    )
    red_first = Reduce(*in_order(order, own, other, rows_chip))
    red_outer.step()
    qkv_low[1], qkv_sums[1] = attention_backward(
        groups[1], context_grad, projected, attention, (red_inner.last(), red_outer.last(), red_first.last())
    )
    red_first.step()
    red_inner.step()
    own, other = qkv_backward(
        table, tokens, qkv_low[1], None, (sums_one, sums_two, qkv_sums[1], qkv_sums[0], bias_own, bias_other)
    )
    red_second = Reduce(*in_order(order, own, other, rows_chip))
    red_second.step()
    input_grad = tokens_backward(groups, qkv_low, qkv_w, grad_one)
    red_second.step(input_grad)
    outer_mine, outer_theirs, inner_mine, inner_theirs, squares = summed(
        table, (red_outer.finish(), red_inner.finish())
    )
    first_mine, first_theirs, second_mine, second_theirs, squares = summed(
        table, (red_first.finish(), red_second.finish()), (1,), loss, squares
    )
    totals = total_over_devices(squares)
    grads = []
    for mine, theirs in (
        (outer_mine, outer_theirs),
        (inner_mine, inner_theirs),
        (first_mine, first_theirs),
        (second_mine, second_theirs),
    ):
        grads += [mine, core_swapped(theirs)]
    grads.append(second_mine[:, half : half + affine_rows].T)
    slots = spans * lax.axis_size("dp") * lax.axis_size("pair")
    updated = adamw(
        table,
        totals,
        grads,
        (qkv_weight, proj_weight, inner_weight, outer_weight, affine_params),
        (qkv_moment, proj_moment, inner_moment, outer_moment, affine_moment),
        (qkv_square, proj_square, inner_square, outer_square, affine_square),
        slots,
    )
    state = [updated[3 * n + k] for k in range(3) for n in range(5)]
    return (*state, layer_out, input_grad, updated[-1][0, 0], updated[-1][1, 0])


def solution(mesh):
    placed = (
        P(("dp", "pair"), None),
        P(("dp", "pair"), None),
        P("dp", None),
        P("dp"),
        P(("dp", "pair"), None),
        P(("dp", "pair"), None),
        P(("dp", "pair"), None),
        P(("dp", "pair"), None),
        P(None, ("dp", "pair")),
        P(("dp", "pair"), None),
        P(("dp", "pair"), None),
        P(("dp", "pair"), None),
        P(("dp", "pair"), None),
        P(None, ("dp", "pair")),
        P(("dp", "pair"), None),
        P(("dp", "pair"), None),
        P(("dp", "pair"), None),
        P(("dp", "pair"), None),
        P(None, ("dp", "pair")),
    )
    return jax.shard_map(
        body,
        mesh=mesh,
        in_specs=placed,
        out_specs=(
            P(("dp", "pair"), None),
            P(("dp", "pair"), None),
            P(("dp", "pair"), None),
            P(("dp", "pair"), None),
            P(None, ("dp", "pair")),
            P(("dp", "pair"), None),
            P(("dp", "pair"), None),
            P(("dp", "pair"), None),
            P(("dp", "pair"), None),
            P(None, ("dp", "pair")),
            P(("dp", "pair"), None),
            P(("dp", "pair"), None),
            P(("dp", "pair"), None),
            P(("dp", "pair"), None),
            P(None, ("dp", "pair")),
            P(("dp", "pair"), None),
            P(("dp", "pair"), None),
            P(),
            P(),
        ),
        check_vma=False,
    )
```

```python
from functools import partial

import jax
import jax.numpy as jnp
from jax import lax
from jax.experimental import pallas as pl
from jax.experimental.pallas import tpu as pltpu
from jax.sharding import PartitionSpec as P

HEADS = 12
HD = 64
L = 128
STEP = 10
LANES = 128
AXES = ("dp", "pair")


LN_EPS = 1e-12
LOSS_WEIGHT = 8.0
CLIP_NORM = 1000.0
BETA_ONE = 0.9
BETA_TWO = 0.999
ADAM_EPS = 1e-08
RATE_MATRIX = 0.05
DECAY_MATRIX = 0.01
RATE_AFFINE = 0.8
DECAY_AFFINE = 0.0

BF16 = jnp.bfloat16
F32 = jnp.float32


def flip_steps(chips):
    bits = chips.bit_length() - 1
    if bits == 4:
        return ((2, 3), (3, 2), (0, 1), (1, 0))
    return tuple((bit, bit) for bit in reversed(range(bits)))


def flip_route(chips, pair_of_bits):
    return [
        (2 * d + c, 2 * (d ^ (1 << pair_of_bits[c])) + c) for d in range(chips) for c in range(2)
    ]


def core_route(chips):
    return [(2 * d + c, 2 * d + 1 - c) for d in range(chips) for c in range(2)]


def flipped(block, bits):
    chips = lax.axis_size("dp")
    return lax.ppermute(block, AXES, flip_route(chips, bits))


def core_swapped(block):
    return lax.ppermute(block, AXES, core_route(lax.axis_size("dp")))


def near_first(chips):
    steps = flip_steps(chips)
    return steps[2:] + steps[:2] if len(steps) == 4 else steps


def block_order(steps):
    chips = lax.axis_size("dp")
    d, c = lax.axis_index("dp"), lax.axis_index("pair")
    index = jnp.arange(chips, dtype=jnp.int32)
    blocks, places = [], []
    for core in range(2):
        blocks.append(sum((index >> k & 1) << step[core] for k, step in enumerate(steps)) ^ d)
        places.append(sum(((index ^ d) >> step[core] & 1) << k for k, step in enumerate(steps)))
    rows = []
    for pairs in (blocks, places):
        rows += [pick(c, pairs[0], pairs[1]), pick(c, pairs[1], pairs[0])]
    return jnp.stack(rows + [jnp.full((chips,), c, jnp.int32)])


def kernel_order(order, rows):
    if rows % 16 == 0:
        return order
    index = jnp.arange(16, dtype=jnp.int32)
    return jnp.stack([index] * 4 + [jnp.full((16,), order[4, 0], jnp.int32)])


def in_order(order, own, other, rows):
    if rows % 16 == 0:
        return own, other
    return tuple(
        blocks.reshape(order.shape[1], rows, -1)[order[side]] for side, blocks in enumerate((own, other))
    )


def pick(core, first, second):
    return jnp.where(core == 0, first, second)


def halves_of(low, pieces):
    core = lax.axis_index("pair")
    first, second, at = [], [], 0
    for width in pieces:
        first.append(low[:, at : at + width])
        second.append(low[:, at + width : at + 2 * width])
        at += 2 * width
    first, second = jnp.concatenate(first, 1), jnp.concatenate(second, 1)
    return pick(core, first, second), pick(core, second, first)


def chip_rows(low, pieces, extra=None):
    core = lax.axis_index("pair")
    own, other = halves_of(low, pieces)
    if extra is not None:
        own, other = (jnp.concatenate([half, extra], 1) for half in (own, other))
    got = core_swapped(other)
    return pick(core, jnp.concatenate([own, got]), jnp.concatenate([got, own]))


def tied(value, *others):
    return lax.optimization_barrier((value, *others))[0]


class Gather:
    def __init__(self, block, steps):
        self.held, self.got, self.left = block[None], None, list(steps)

    def step(self, *others):
        if self.got is not None:
            self.held = jnp.concatenate([self.held, self.got], axis=0)
        self.got = flipped(tied(self.held, *others), self.left.pop(0))
        return self.got

    def finish(self, order, rows, *others):
        while self.left:
            self.step()
        own = (self.held, self.got)
        other = tuple(core_swapped(tied(part, *others)) for part in own)
        if rows % 16:
            own, other = (
                jnp.zeros((2 * self.held.shape[0], *self.held.shape[1:]), BF16)
                .at[order[side]]
                .set(jnp.concatenate(parts))
                .reshape(2, 8, -1, self.held.shape[2])
                for side, parts in enumerate((own, other))
            )
            own, other = (own[0], own[1]), (other[0], other[1])
        return own, other


class Reduce:
    def __init__(self, own, other):
        self.count, self.left = own.shape[0], list(reversed(flip_steps(lax.axis_size("dp"))))
        self.parts = [own, core_swapped(other)]

    def last(self):
        return self.parts[-1]

    def step(self, *others):
        self.count //= 2
        sent = sum(p[self.count : 2 * self.count].astype(F32) for p in self.parts).astype(BF16)
        self.parts.append(flipped(tied(sent, *others), self.left.pop(0)))
        return self.parts[-1]

    def finish(self):
        while self.left:
            self.step()
        return self.parts


def total_over_devices(value):
    bits = lax.axis_size("dp").bit_length() - 1
    value = value + core_swapped(value)
    for low in range(0, bits, 2):
        first = flipped(value, (low, low))
        if low + 1 < bits:
            second = flipped(value, (low + 1, low + 1))
            route = [(2 * d + c, 2 * (d ^ (3 << low)) + c) for d in range(1 << bits) for c in range(2)]
            both = lax.ppermute(value, AXES, route)
            bit, over = (lax.axis_index("dp") >> low & 1) == 0, (lax.axis_index("dp") >> low & 2) == 0
            near = jnp.where(bit, value, first) + jnp.where(bit, first, value)
            far_sum = jnp.where(bit, second, both) + jnp.where(bit, both, second)
            value = jnp.where(over, near, far_sum) + jnp.where(over, far_sum, near)
        else:
            value = value + first
    return value


TILE = 256
PART = 256
PAIR_LANES = 2 * HD
VMEM_LIMIT = 32 * 1024 * 1024
SMEM = pl.BlockSpec(memory_space=pltpu.SMEM)
ANY = pl.BlockSpec(memory_space=pl.ANY)


def call(kernel, grid, ins, outs, scratch=(), micros=10, after=(), order=None):
    count = len(ins) + (order is not None)

    def body(*refs):
        kernel(*refs[:count], *refs[count + len(after) :])

    in_specs = [spec for _, spec in ins] + [ANY] * len(after)
    operands = [array for array, _ in ins] + list(after)
    if order is not None:
        operands = [order] + operands
    return pl.pallas_call(
        body,
        grid_spec=pltpu.PrefetchScalarGridSpec(
            num_scalar_prefetch=int(order is not None),
            grid=grid,
            in_specs=in_specs,
            out_specs=tuple(spec for _, spec in outs),
            scratch_shapes=list(scratch),
        ),
        out_shape=tuple(shape for shape, _ in outs),
        compiler_params=pltpu.CompilerParams(
            vmem_limit_bytes=VMEM_LIMIT, dimension_semantics=("arbitrary",) * len(grid)
        ),
        cost_estimate=pl.CostEstimate(
            flops=micros * 300_000_000, bytes_accessed=micros * 300_000, transcendentals=0
        ),
    )(*operands)


def whole(shape):
    return pl.BlockSpec(shape, lambda i, *_: (0,) * len(shape))


def rows_of(count, width):
    return pl.BlockSpec((count, width), lambda i, *_: (i, 0))


def cols_of(height, count):
    return pl.BlockSpec((height, count), lambda i, *_: (0, i))


def struct(shape, dtype):
    return jax.ShapeDtypeStruct(shape, dtype)


def streamed(array):
    return pltpu.with_memory_space_constraint(array, pltpu.HBM)


def far(shape, dtype):
    return pltpu.HBM(shape, dtype)


def dot(left, right):
    return jnp.dot(left, right, preferred_element_type=F32)


def contract_rows(left, right):
    return lax.dot_general(left, right, (((0,), (0,)), ((), ())), preferred_element_type=F32)


def contract_cols(left, right):
    return lax.dot_general(left, right, (((1,), (1,)), ((), ())), preferred_element_type=F32)


def normalize(total):
    centered = total - jnp.mean(total, axis=-1, keepdims=True)
    variance = jnp.mean(centered * centered, axis=-1, keepdims=True)
    scale_inv = lax.rsqrt(variance + LN_EPS)
    return (centered * scale_inv, scale_inv)


def normalize_back(upstream, normed, scale_inv, gain):
    scaled = upstream * gain
    return scale_inv * (
        scaled
        - jnp.mean(scaled, axis=-1, keepdims=True)
        - normed * jnp.mean(scaled * normed, axis=-1, keepdims=True)
    )


def gelu_and_slope(pre):
    below = 0.5 + 0.5 * lax.erf(pre * 0.5**0.5)
    return pre * below, below + pre * jnp.exp(pre * pre * -0.5) * (2 * jnp.pi) ** -0.5


def two_heads(block, lane_low):
    zero = jnp.zeros_like(block)
    return jnp.concatenate([jnp.where(lane_low, block, zero), jnp.where(lane_low, zero, block)], 0)


def lane_is_low(rows):
    return lax.broadcasted_iota(jnp.int32, (rows, PAIR_LANES), 1) < HD


def column_sum(value):
    return jnp.sum(value, axis=0, keepdims=True)


def placed(refs, place):
    count = refs[0].shape[0]
    return refs[place // count].at[place % count]


def fetches(order_ref, own_refs, other_refs, target, sems, rows, width, start=0, lane=0):
    core = order_ref[4, 0]
    copies = []
    for place in range(sems.shape[0]):
        pair = []
        for side, refs in enumerate((own_refs, other_refs)):
            half = core if side == 0 else 1 - core
            row = pl.multiple_of(order_ref[side, place] * rows, rows)
            pair.append(
                pltpu.make_async_copy(
                    placed(refs, place).at[:, pl.ds(lane, width)],
                    target.at[pl.ds(row, rows), pl.ds(pl.multiple_of(start + half * width, LANES), width)],
                    sems.at[place, side],
                )
            )
        copies.append(pair)
    return copies


def begin(copies):
    for pair in copies:
        for copy in pair:
            copy.start()


def finish(copies):
    for pair in copies:
        for copy in pair:
            copy.wait()


def in_turn(count, *stages):
    held = stages[0](0)
    for n in range(count):
        value, held = held, stages[0](n + 1) if n + 1 < count else None
        for stage in stages[1:]:
            value = stage(n, value)


def projection_forward(order, tokens, own, other, affine_rows, after=()):
    rows, width = tokens.shape
    half = width // 2
    chips, block = 2 * own[0].shape[0], own[0].shape[1]

    def kernel(
        order_ref, tokens_ref, own_a, own_b, other_a, other_b,
        w_ref, proj_ref, affine_ref, out_ref, columns, sems, column_sems,
    ):
        own_refs, other_refs = (own_a, own_b), (other_a, other_b)
        step = pl.program_id(0)
        params = [
            pltpu.make_async_copy(
                placed(own_refs, p).at[:, pl.ds(4 * half, LANES)],
                columns.at[pl.ds(pl.multiple_of(order_ref[0, p] * block, block), block), :],
                column_sems.at[p],
            )
            for p in range(chips)
        ]
        parts = [
            fetches(order_ref, own_refs, other_refs, w_ref, sems.at[k], block, half, k * width, k * half)
            for k in range(3)
        ]
        parts.append(fetches(order_ref, own_refs, other_refs, proj_ref, sems.at[3], block, half, 0, 3 * half))

        @pl.when(step == 0)
        def _():
            for copy in params:
                copy.start()
            for copies in parts:
                begin(copies)
            for copy in params:
                copy.wait()
            affine_ref[...] = columns[...].astype(F32).T[:affine_rows]

        for k in range(3):

            @pl.when(step == k)
            def _():
                finish(parts[k])
                for n in range(width // TILE):
                    cols = slice(n * TILE, (n + 1) * TILE)
                    value = dot(tokens_ref[...], w_ref[:, k * width + n * TILE : k * width + (n + 1) * TILE])
                    if k != 1:
                        value += affine_ref[4 + k // 2 : 5 + k // 2, cols]
                    out_ref[:, cols] = value.astype(BF16)

        @pl.when(step == 2)
        def _():
            finish(parts[3])

    return call(
        kernel,
        (3,),
        [(tokens, whole(tokens.shape)), *((blocks, ANY) for blocks in (*own, *other))],
        [
            (far((width, 3 * width), BF16), whole((width, 3 * width))),
            (struct((width, width), BF16), whole((width, width))),
            (struct((affine_rows, width), F32), whole((affine_rows, width))),
            (struct((rows, 3 * width), BF16), cols_of(rows, width)),
        ],
        [
            pltpu.VMEM((width, LANES), BF16),
            pltpu.SemaphoreType.DMA((4, chips, 2)),
            pltpu.SemaphoreType.DMA((chips,)),
        ],
        8,
        after,
        order,
    )


def attention_forward(tokens, projected, proj_w, affine, after=()):
    rows, width = tokens.shape
    spans, pairs = rows // L, width // PAIR_LANES
    each = PART // L

    def kernel(
        tokens_ref, projected_ref, proj_ref, affine_ref,
        attention_ref, context_ref, normed_ref, inv_ref, skip_ref,
    ):
        lane_low = lane_is_low(L)

        def read(n, part):
            s, p = divmod(n, pairs)
            at = part * width + p * PAIR_LANES
            return projected_ref[s * L : (s + 1) * L, at : at + PAIR_LANES]

        def scored(n):
            return contract_cols(two_heads(read(n, 0) * jnp.asarray(HD**-0.5, BF16), lane_low), read(n, 1))

        def weighed(n, scores):
            s, p = divmod(n, pairs)
            exponent = jnp.exp(scores - jnp.max(scores, axis=-1, keepdims=True))
            low = (exponent * (1.0 / jnp.sum(exponent, axis=-1, keepdims=True))).astype(BF16)
            attention_ref[s, p] = low
            both = dot(low, read(n, 2))
            context_ref[s * L : (s + 1) * L, p * PAIR_LANES : (p + 1) * PAIR_LANES] = jnp.where(
                lane_low, both[:L], both[L:]
            ).astype(BF16)

        in_turn(each * pairs, scored, weighed)
        total = dot(context_ref[...], proj_ref[...]) + affine_ref[6:7, :]
        normed, inv = normalize(tokens_ref[...].astype(F32) + total)
        normed_ref[...] = normed
        inv_ref[...] = jnp.broadcast_to(inv, (PART, LANES))
        skip_ref[...] = (normed * affine_ref[0:1, :] + affine_ref[1:2, :]).astype(BF16)

    return call(
        kernel,
        (rows // PART,),
        [
            (tokens, rows_of(PART, width)),
            (projected, rows_of(PART, 3 * width)),
            (proj_w, whole(proj_w.shape)),
            (affine, whole(affine.shape)),
        ],
        [
            (
                far((spans, pairs, 2 * L, L), BF16),
                pl.BlockSpec((each, pairs, 2 * L, L), lambda i, *_: (i, 0, 0, 0)),
            ),
            (far((rows, width), BF16), rows_of(PART, width)),
            (far((rows, width), F32), rows_of(PART, width)),
            (far((rows, LANES), F32), rows_of(PART, LANES)),
            (struct((rows, width), BF16), rows_of(PART, width)),
        ],
        (),
        12,
        after,
    )


def inner_forward(order, side, skip_low, blocks, affine, after=()):
    rows, width = skip_low.shape
    count, block, half = blocks[0].shape
    chips = 2 * count

    def kernel(order_ref, skip_ref, first_ref, second_ref, affine_ref, w_ref, act_ref, slope_ref, sems):
        step = pl.program_id(0)

        def copies(p):
            row = pl.multiple_of(order_ref[side, p] * block, block)
            return pltpu.make_async_copy(
                placed((first_ref, second_ref), p), w_ref.at[pl.ds(row, block), :], sems.at[p]
            )

        @pl.when(step == 0)
        def _():
            for b in range(chips):
                copies(b).start()
            for b in range(chips):
                copies(b).wait()

        first = order_ref[4, 0] if side == 0 else 1 - order_ref[4, 0]
        bias = affine_ref[pl.ds(8 + first * (half // width) + step, 1), :]
        parts = rows // PART

        def entered(n):
            k, r = divmod(n, parts)
            weight = w_ref[:, pl.ds(pl.multiple_of(step * width + k * TILE, LANES), TILE)]
            return dot(skip_ref[r * PART : (r + 1) * PART, :], weight)

        def activated(n, value):
            k, r = divmod(n, parts)
            at, cols = slice(r * PART, (r + 1) * PART), slice(k * TILE, (k + 1) * TILE)
            act, slope = gelu_and_slope(value + bias[:, cols])
            act_ref[at, cols] = act.astype(BF16)
            slope_ref[at, cols] = slope.astype(BF16)

        in_turn(width // TILE * parts, entered, activated)

    return call(
        kernel,
        (half // width,),
        [(skip_low, whole(skip_low.shape)), (blocks[0], ANY), (blocks[1], ANY), (affine, whole(affine.shape))],
        [
            (far((width, half), BF16), whole((width, half))),
            (struct((rows, half), BF16), cols_of(rows, width)),
            (far((rows, half), BF16), cols_of(rows, width)),
        ],
        [pltpu.SemaphoreType.DMA((chips,))],
        10,
        after,
        order,
    )


def outer_forward(order, act_own, act_other, own, other, normed_one, affine, mlm_grad, live_rows, after=()):
    rows, wide = act_own.shape
    hidden, width = 2 * wide, normed_one.shape[1]
    chips, block = 2 * own[0].shape[0], own[0].shape[1]
    spans = rows // L
    many = 2
    tile = many * PART

    def kernel(
        order_ref, act_own_ref, act_other_ref, own_a, own_b, other_a, other_b, normed_one_ref, affine_ref, mlm_ref, live_ref,
        w_ref, out_ref, grad_ref, low_ref, sums_ref, cls_ref, cls_normed_ref, cls_inv_ref, sems,
    ):
        step = pl.program_id(0)

        core = order_ref[4, 0]

        def entered(n):
            at = slice(n * PART, (n + 1) * PART)
            total = 0.0
            for k, ref in enumerate((act_own_ref, act_other_ref)):
                start = (core if k == 0 else 1 - core) * wide
                total = total + dot(ref[at, :], w_ref[pl.ds(pl.multiple_of(start, LANES), wide), :])
            return total

        def ended(n, total):
            at = slice(n * PART, (n + 1) * PART)
            skip = normed_one_ref[at, :] * affine_ref[0:1, :] + affine_ref[1:2, :]
            normed, inv = normalize(skip + (total + affine_ref[7:8, :]))
            out = (normed * affine_ref[2:3, :] + affine_ref[3:4, :]).astype(BF16)
            out_ref[at, :] = out
            line = lax.broadcasted_iota(jnp.int32, (PART, 1), 0)
            live = line < live_ref[0] - (step * many + n) * PART
            upstream = jnp.where(live, mlm_ref[at, :].astype(F32), 0.0)
            grad = normalize_back(upstream, normed, inv, affine_ref[2:3, :])
            grad_ref[at, :] = grad
            low_ref[at, :] = grad.astype(BF16)
            for k, value in enumerate((upstream * normed, upstream, grad)):
                sums_ref[k : k + 1, :] += column_sum(value)
            for s in range(PART // L):
                row, to = slice(s * L, s * L + 1), pl.ds((step * many + n) * (PART // L) + s, 1)
                cls_ref[to, :] = out[s * L : s * L + 16].astype(F32)[:1]
                cls_normed_ref[to, :] = normed[row]
                cls_inv_ref[to, :] = jnp.broadcast_to(inv[row], (1, LANES))

        copies = fetches(order_ref, (own_a, own_b), (other_a, other_b), w_ref, sems, block, width // 2)

        @pl.when(step == 0)
        def _():
            begin(copies)
            sums_ref[...] = jnp.zeros_like(sums_ref)
            finish(copies)

        in_turn(many, entered, ended)

    return call(
        kernel,
        (rows // tile,),
        [
            (act_own, rows_of(tile, wide)),
            (act_other, rows_of(tile, wide)),
            *((blocks, ANY) for blocks in (*own, *other)),
            (streamed(normed_one), rows_of(tile, width)),
            (affine, whole(affine.shape)),
            (streamed(mlm_grad), rows_of(tile, width)),
            (live_rows, SMEM),
        ],
        [
            (far((hidden, width), BF16), whole((hidden, width))),
            (far((rows, width), BF16), rows_of(tile, width)),
            (far((rows, width), F32), rows_of(tile, width)),
            (struct((rows, width), BF16), rows_of(tile, width)),
            (struct((8, width), F32), whole((8, width))),
            (struct((spans, width), F32), whole((spans, width))),
            (struct((spans, width), F32), whole((spans, width))),
            (struct((spans, LANES), F32), whole((spans, LANES))),
        ],
        [pltpu.SemaphoreType.DMA((chips, 2))],
        8,
        after,
        order,
    )


def loss_and_gradient(own, other, match, key_live, anchor_live):
    scale = own.shape[1] ** -0.5
    sims = contract_cols(own.astype(BF16), other.astype(BF16)) * scale
    step = jnp.zeros_like(sims)
    loss = None
    for axis, live in ((1, key_live), (0, anchor_live)):
        masked = jnp.where(live > 0, sims, -1000000000.0)
        peak = jnp.max(masked, axis=axis, keepdims=True)
        weights = jnp.where(live > 0, jnp.exp(masked - peak), 0.0)
        total = jnp.sum(weights, axis=axis, keepdims=True)
        active = jnp.max(match, axis=axis, keepdims=True)
        step += active * (weights / total - match)
        if loss is None:
            hit = jnp.sum(match * sims, axis=axis, keepdims=True)
            loss = jnp.sum(jnp.where(active > 0, peak + jnp.log(total) - hit, 0.0), axis=0, keepdims=True)
    step *= LOSS_WEIGHT * scale
    gradient = jnp.zeros_like(own)
    for k in range(other.shape[0]):
        gradient += step[:, k : k + 1] * other[k : k + 1, :]
    return loss, gradient


def outer_backward(order, grad_low, sums, cls, cls_other, masks, cls_normed, cls_inv, act_own, act_other, affine, after=()):
    rows, width = grad_low.shape
    hidden = 2 * act_own.shape[1]
    chips = order.shape[1]
    block, half = hidden // chips, width // 2
    tile = 4 * block
    turn = chips // 8
    spans = rows // L

    def kernel(
        order_ref, low_in_ref, sums_in_ref, cls_ref, cls_other_ref, masks_ref, normed_ref, inv_ref, act_own_ref, act_other_ref, affine_ref,
        low_ref, more_ref, sums_ref, loss_ref, own_ref, other_ref, own_held, other_held, sems,
    ):
        step = pl.program_id(0)

        @pl.when(step == 0)
        def _():
            loss, up = loss_and_gradient(
                cls_ref[...], cls_other_ref[...], masks_ref[0], masks_ref[1], masks_ref[2]
            )
            normed = normed_ref[...]
            more = normalize_back(up, normed, inv_ref[:, :1], affine_ref[2:3, :])
            more_ref[...] = more
            loss_ref[...] = jnp.broadcast_to(loss, loss_ref.shape)
            for k, value in enumerate((up * normed, up, more)):
                sums_ref[k : k + 1, :] = sums_in_ref[k : k + 1, :] + column_sum(value)
            low_ref[...] = low_in_ref[...]
            line = lax.broadcasted_iota(jnp.int32, (16, 1), 0)
            for s in range(spans):
                at = slice(s * L, s * L + 16)
                changed = low_in_ref[at, :].astype(F32) + jnp.where(line == 0, more[s : s + 1], 0.0)
                low_ref[at, :] = changed.astype(BF16)

        core = order_ref[4, 0]

        def gradient(act_ref, first):
            def entered(n):
                return contract_rows(act_ref[:, n * 2 * block : (n + 1) * 2 * block], low_ref[...])

            def ended(n, value):
                low, high = value[:, :half], value[:, half:]
                parts = (jnp.where(core == 0, low, high), jnp.where(core == 0, high, low))
                for side, (part, held, out) in enumerate(
                    zip(parts, (own_held, other_held), (own_ref, other_ref))
                ):
                    for k in range(2):
                        b = first + 2 * n + k
                        held[b] = part[k * block : (k + 1) * block].astype(BF16)
                        pltpu.make_async_copy(
                            held.at[b], out.at[order_ref[2 + side, b]], sems.at[side, b]
                        ).start()

            in_turn(2, entered, ended)

        @pl.when(step < turn)
        def _():
            gradient(act_own_ref, core * (chips // 2) + 4 * step)

        @pl.when(step >= turn)
        def _():
            gradient(act_other_ref, (1 - core) * (chips // 2) + 4 * (step - turn))

        @pl.when(step == 2 * turn - 1)
        def _():
            for side, (held, out) in enumerate(((own_held, own_ref), (other_held, other_ref))):
                for b in range(chips):
                    pltpu.make_async_copy(
                        held.at[b], out.at[order_ref[2 + side, b]], sems.at[side, b]
                    ).wait()

    shape = (chips, block, half)
    return call(
        kernel,
        (hidden // tile,),
        [
            (grad_low, whole(grad_low.shape)),
            (sums, whole(sums.shape)),
            (cls, whole(cls.shape)),
            (cls_other, whole(cls.shape)),
            (masks, whole(masks.shape)),
            (cls_normed, whole(cls.shape)),
            (cls_inv, whole(cls_inv.shape)),
            (act_own, pl.BlockSpec((rows, tile), lambda i, *_: (0, jnp.minimum(i, turn - 1)))),
            (act_other, pl.BlockSpec((rows, tile), lambda i, *_: (0, jnp.maximum(i - turn, 0)))),
            (affine, whole(affine.shape)),
        ],
        [
            (struct((rows, width), BF16), whole((rows, width))),
            (struct((spans, width), F32), whole((spans, width))),
            (struct((8, width), F32), whole((8, width))),
            (struct((8, LANES), F32), whole((8, LANES))),
            (struct(shape, BF16), ANY),
            (struct(shape, BF16), ANY),
        ],
        [
            pltpu.VMEM(shape, BF16),
            pltpu.VMEM(shape, BF16),
            pltpu.SemaphoreType.DMA((2, chips)),
        ],
        8,
        after,
        order,
    )


def inner_backward(order, side, low, slope, outer_w, skip_low, after=()):
    rows, width = low.shape
    hidden = 2 * slope.shape[1]
    chips = order.shape[1]
    block = width // chips
    steps = hidden // 2 // width

    def kernel(order_ref, low_ref, slope_ref, outer_ref, skip_ref, inner_ref, bias_ref, out_ref):
        step = pl.program_id(0)

        def entered(n):
            return contract_cols(low_ref[...], outer_ref[n * TILE : (n + 1) * TILE, :])

        def sloped(n, value):
            cols = slice(n * TILE, (n + 1) * TILE)
            inner_grad = value * slope_ref[:, cols].astype(F32)
            bias_ref[pl.ds(step, 1), cols] = column_sum(inner_grad)
            inner_low = inner_grad.astype(BF16)
            inner_ref[:, cols] = inner_low
            return contract_rows(skip_ref[...], inner_low).astype(BF16)

        def stored(n, value):
            for b in range(chips):
                out_ref[order_ref[2 + side, b], :, n * TILE : (n + 1) * TILE] = value[b * block : (b + 1) * block]

        in_turn(width // TILE, entered, sloped, stored)

    def place(i, table):
        half = table[4, 0] if side == 0 else 1 - table[4, 0]
        return half * steps + i

    return call(
        kernel,
        (steps,),
        [
            (low, whole(low.shape)),
            (streamed(slope), cols_of(rows, width)),
            (streamed(outer_w), pl.BlockSpec((width, width), lambda i, table: (place(i, table), 0))),
            (skip_low, whole(skip_low.shape)),
        ],
        [
            (struct((rows, hidden // 2), BF16), cols_of(rows, width)),
            (struct((8, width), F32), whole((8, width))),
            (
                struct((chips, block, hidden // 2), BF16),
                pl.BlockSpec((chips, block, width), lambda i, *_: (0, 0, i)),
            ),
        ],
        (),
        8,
        after,
        order,
    )


def skip_backward(inner_own, inner_other, w_own, w_other, grad_two, more, normed_one, inv_one, affine, proj_w, after=()):
    rows, width = grad_two.shape
    half = w_own.shape[1]
    many = 2
    tile = many * PART

    def kernel(
        own_ref, other_ref, w_own_ref, w_other_ref, grad_two_ref, more_ref, normed_ref, inv_ref, affine_ref, proj_ref,
        grad_ref, low_ref, sums_ref, context_ref,
    ):
        step = pl.program_id(0)

        @pl.when(step == 0)
        def _():
            sums_ref[...] = jnp.zeros_like(sums_ref)

        def entered(n):
            at = slice(n * PART, (n + 1) * PART)
            up = grad_two_ref[at, :]
            for ref, weight in ((own_ref, w_own_ref), (other_ref, w_other_ref)):
                up = up + contract_cols(ref[at, :], weight[...])
            return up

        def ended(n, up):
            at = slice(n * PART, (n + 1) * PART)
            line = lax.broadcasted_iota(jnp.int32, (PART, 1), 0)
            for s in range(PART // L):
                row = pl.ds((step * many + n) * (PART // L) + s, 1)
                up = up + jnp.where(line == s * L, more_ref[row, :], 0.0)
            normed = normed_ref[at, :]
            grad = normalize_back(up, normed, inv_ref[at, :1], affine_ref[0:1, :])
            grad_ref[at, :] = grad
            low = grad.astype(BF16)
            low_ref[at, :] = low
            for k, value in enumerate((up * normed, up, grad)):
                sums_ref[k : k + 1, :] += column_sum(value)
            context_ref[at, :] = contract_cols(low, proj_ref[...]).astype(BF16)

        in_turn(many, entered, ended)

    return call(
        kernel,
        (rows // tile,),
        [
            (inner_own, rows_of(tile, half)),
            (inner_other, rows_of(tile, half)),
            (streamed(w_own), whole(w_own.shape)),
            (streamed(w_other), whole(w_other.shape)),
            (streamed(grad_two), rows_of(tile, width)),
            (more, whole(more.shape)),
            (streamed(normed_one), rows_of(tile, width)),
            (streamed(inv_one), rows_of(tile, LANES)),
            (affine, whole(affine.shape)),
            (proj_w, whole(proj_w.shape)),
        ],
        [
            (far((rows, width), F32), rows_of(tile, width)),
            (struct((rows, width), BF16), rows_of(tile, width)),
            (struct((8, width), F32), whole((8, width))),
            (struct((rows, width), BF16), rows_of(tile, width)),
        ],
        (),
        8,
        after,
    )


def attention_backward(pairs, context_grad, projected, attention, after=()):
    rows, width = context_grad.shape
    spans, count = rows // L, len(pairs)
    wide = 3 * count * PAIR_LANES
    each = 2

    def kernel(grad_ref, projected_ref, attention_ref, out_ref, sums_ref):
        @pl.when(pl.program_id(0) == 0)
        def _():
            sums_ref[...] = jnp.zeros_like(sums_ref)

        lane_low = lane_is_low(L)
        def entered(m):
            s, n = divmod(m, count)
            at, line = pairs[n] * PAIR_LANES, slice(s * L, (s + 1) * L)
            grads = two_heads(grad_ref[line, at : at + PAIR_LANES], lane_low)
            v = projected_ref[line, 2 * width + at : 2 * width + at + PAIR_LANES]
            return grads, contract_cols(grads, v)

        def ended(m, value):
            s, n = divmod(m, count)
            at, line = pairs[n] * PAIR_LANES, slice(s * L, (s + 1) * L)
            q, k = (
                projected_ref[line, part * width + at : part * width + at + PAIR_LANES] for part in range(2)
            )
            grads, back = value
            low = attention_ref[s, pairs[n]]
            weights = low.astype(F32)
            product = back * weights
            score = (product - weights * jnp.sum(product, axis=-1, keepdims=True)) * HD**-0.5
            score_low = score.astype(BF16)
            both = dot(score_low, k)
            parts = (
                jnp.where(lane_low, both[:L], both[L:]),
                contract_rows(score_low, two_heads(q, lane_low)),
                contract_rows(low, grads),
            )
            for part, value in enumerate(parts):
                to = slice((part * count + n) * PAIR_LANES, (part * count + n + 1) * PAIR_LANES)
                out_ref[line, to] = value.astype(BF16)
                sums_ref[:, to] += column_sum(value)

        in_turn(each * count, entered, ended)

    return call(
        kernel,
        (spans // each,),
        [
            (context_grad, rows_of(each * L, width)),
            (streamed(projected), rows_of(each * L, 3 * width)),
            (streamed(attention), pl.BlockSpec((each, width // PAIR_LANES, 2 * L, L), lambda i, *_: (i, 0, 0, 0))),
        ],
        [
            (struct((rows, wide), BF16), rows_of(each * L, wide)),
            (struct((1, wide), F32), whole((1, wide))),
        ],
        (),
        3 * count,
        after,
    )


def store_blocks(order_ref, low, high, rows, own_ref, other_ref, lane):
    core = order_ref[4, 0]
    own = jnp.where(core == 0, low, high).astype(BF16)
    other = jnp.where(core == 0, high, low).astype(BF16)
    width = low.shape[1]
    for b in range(low.shape[0] // rows):
        at = slice(b * rows, (b + 1) * rows)
        own_ref[order_ref[2, b], :, lane : lane + width] = own[at]
        other_ref[order_ref[3, b], :, lane : lane + width] = other[at]


def qkv_backward(order, tokens, qkv_low, proj=None, sums=None, after=()):
    rows, width = tokens.shape
    chips = order.shape[1]
    block, half = width // chips, width // 2
    each = qkv_low.shape[1] // 6
    extra = half if proj is not None else LANES

    def affine_rows(sums_one, sums_two, first, second, bias_own, bias_other, lines, core):
        lines[...] = jnp.zeros_like(lines)
        lines[0:2, :] = sums_one[0:2, :]
        lines[2:4, :] = sums_two[0:2, :]
        for row, part in ((4, 0), (5, 2)):
            for h in range(2):
                at = h * half
                for ref in (first, second):
                    wide = ref.shape[1] // 6
                    lines[row : row + 1, at : at + wide] = ref[:, (2 * part + h) * wide : (2 * part + h + 1) * wide]
                    at += wide
        lines[6:7, :] = sums_one[2:3, :]
        lines[7:8, :] = sums_two[2:3, :]
        lines[8:10, :] = jnp.where(core == 0, bias_own[0:2, :], bias_other[0:2, :])
        lines[10:12, :] = jnp.where(core == 0, bias_other[0:2, :], bias_own[0:2, :])
        return lines[...].T

    def kernel(order_ref, tokens_ref, qkv_ref, *rest):
        rest, (own_ref, other_ref, lines) = rest[:-3], rest[-3:]

        def entered(k):
            if k < 3:
                return contract_rows(tokens_ref[...], qkv_ref[:, 2 * k * each : 2 * (k + 1) * each])
            if proj is not None:
                return contract_rows(rest[0][...], rest[1][...])
            value = affine_rows(*rest, lines, order_ref[4, 0])
            return jnp.concatenate([value, value], axis=1)

        def ended(k, value):
            middle = value.shape[1] // 2
            store_blocks(order_ref, value[:, :middle], value[:, middle:], block, own_ref, other_ref, k * each)

        in_turn(4, entered, ended)

    shape = (chips, block, 3 * each + extra)
    more = list(proj if proj is not None else sums)
    return call(
        kernel,
        (1,),
        [(array, whole(array.shape)) for array in (tokens, qkv_low, *more)],
        [(struct(shape, BF16), whole(shape)), (struct(shape, BF16), whole(shape))],
        [pltpu.VMEM((LANES, width), F32)],
        5,
        after,
        order,
    )


def tokens_backward(groups, qkv_lows, qkv_w, grad_one, after=()):
    rows, width = grad_one.shape

    def kernel(*refs):
        lows, (w_ref, grad_ref, out_ref, held) = refs[: len(groups)], refs[len(groups) :]
        for pairs, ref in zip(groups, lows):
            for part in range(3):
                for n, p in enumerate(pairs):
                    held[:, part * width + p * PAIR_LANES : part * width + (p + 1) * PAIR_LANES] = ref[
                        :, (part * len(pairs) + n) * PAIR_LANES : (part * len(pairs) + n + 1) * PAIR_LANES
                    ]
        out_ref[...] = contract_cols(held[...], w_ref[...]) + grad_ref[...]

    return call(
        kernel,
        (rows // PART,),
        [(low, rows_of(PART, low.shape[1])) for low in qkv_lows]
        + [(streamed(qkv_w), whole(qkv_w.shape)), (streamed(grad_one), rows_of(PART, width))],
        [(struct((rows, width), F32), rows_of(PART, width))],
        [pltpu.VMEM((PART, 3 * width), BF16)],
        8,
        after,
    )[0]


def summed(order, chunks, doubled=(), loss=None, before=None):
    counts = [len(parts) for parts in chunks]
    shapes = [(parts[0].shape[1] // 2, parts[0].shape[2]) for parts in chunks]
    extras = [loss] if loss is not None else []
    extras += [before] if before is not None else []
    arrays = [p for parts in chunks for p in parts]

    def kernel(order_ref, *refs):
        core = order_ref[4, 0]
        squares = 0.0
        outs = refs[len(arrays) + len(extras) :]
        at = 0
        for n, count in enumerate(counts):
            rows, cols = shapes[n]
            total = sum(ref[0].astype(F32) for ref in refs[at : at + count])
            at += count
            first, second = total[:rows], total[rows:]
            mine, theirs = jnp.where(core == 0, first, second), jnp.where(core == 0, second, first)
            outs[2 * n][...] = mine
            outs[2 * n + 1][...] = theirs
            squares += jnp.sum(mine * mine)
            theirs = theirs[:, : cols - LANES] if n in doubled else theirs
            squares += jnp.sum(theirs * theirs)
        line = lax.broadcasted_iota(jnp.int32, (8, LANES), 0)
        result = jnp.where(line == 0, squares, 0.0)
        if loss is not None:
            result += jnp.where(line == 1, refs[len(arrays)][0:1, :], 0.0)
        if before is not None:
            result += refs[len(arrays) + len(extras) - 1][...]
        outs[-1][...] = result

    return call(
        kernel,
        (1,),
        [(p, pl.BlockSpec((1, *p.shape[1:]), lambda i, *_: (0, 0, 0))) for p in arrays]
        + [(x, whole(x.shape)) for x in extras],
        [(struct(s, F32), whole(s)) for s in shapes for _ in range(2)]
        + [(struct((8, LANES), F32), whole((8, LANES)))],
        (),
        2,
        (),
        order,
    )


def adamw(order, totals, grads, weights, moments, squares, slots):
    count = len(weights)
    shapes = [w.shape for w in weights]
    rates = (RATE_MATRIX,) * (count - 1) + (RATE_AFFINE,)
    decays = (DECAY_MATRIX,) * (count - 1) + (DECAY_AFFINE,)

    def kernel(order_ref, totals_ref, *refs):
        core = order_ref[4, 0]
        grad_refs, refs = refs[: len(grads)], refs[len(grads) :]
        olds, outs = refs[: 3 * count], refs[3 * count :]
        norm = jnp.sqrt(totals_ref[0:1, :])
        outs[-1][...] = jnp.concatenate([norm, totals_ref[1:2, :] / slots, jnp.zeros((6, LANES), F32)], 0)
        factor = jnp.minimum(1.0, CLIP_NORM / (norm[:, 0:1] + 1e-06))

        def update(n, at, gradient):
            master, moment, square = (olds[3 * n + k][at] for k in range(3))
            clipped = gradient * factor
            moment = BETA_ONE * moment + (1.0 - BETA_ONE) * clipped
            square = BETA_TWO * square + (1.0 - BETA_TWO) * clipped * clipped
            mean_hat = moment / (1.0 - BETA_ONE**STEP)
            square_hat = square / (1.0 - BETA_TWO**STEP)
            master = master - rates[n] * (mean_hat / (jnp.sqrt(square_hat) + ADAM_EPS) + decays[n] * master)
            for k, value in enumerate((master, moment, square)):
                outs[3 * n + k][at] = value

        def pieces(n, start, chunk, lane, width):
            mine, got = grad_refs[2 * chunk], grad_refs[2 * chunk + 1]
            for h in range(2):
                first, second = mine[:, lane : lane + width], got[:, lane : lane + width]
                value = jnp.where(core == h, first, second)
                update(n, (slice(None), slice(start[h], start[h] + width)), value)

        width = shapes[0][1] // 3
        half = width // 2
        each = half // 3
        for k in range(3):
            at = k * width
            pieces(0, (at, at + half), 3, k * each, each)
            pieces(0, (at + each, at + half + each), 2, 2 * k * each, 2 * each)
        pieces(1, (0, half), 2, 6 * each, half)
        pieces(2, (0, shapes[2][1] // 2), 1, 0, shapes[2][1] // 2)
        pieces(3, (0, half), 0, 0, half)
        update(4, (slice(None), slice(None)), grad_refs[-1][...])

    olds = [array for n in range(count) for array in (weights[n], moments[n], squares[n])]
    return call(
        kernel,
        (1,),
        [(a, whole(a.shape)) for a in (totals, *grads, *map(streamed, olds))],
        [(far(s, F32), whole(s)) for s in shapes for _ in range(3)]
        + [(struct((8, LANES), F32), whole((8, LANES)))],
        (),
        4,
        (),
        order,
    )


def body(
    tokens,
    mlm_grad,
    doc_ids,
    span_counts,
    qkv_weight,
    proj_weight,
    inner_weight,
    outer_weight,
    affine_params,
    qkv_moment,
    proj_moment,
    inner_moment,
    outer_moment,
    affine_moment,
    qkv_square,
    proj_square,
    inner_square,
    outer_square,
    affine_square,
):
    rows, width = tokens.shape
    spans = rows // L
    half = width // 2
    chips = lax.axis_size("dp")
    order = block_order(flip_steps(chips))
    order_outer = block_order(near_first(chips))
    hidden = inner_weight.shape[1]
    pairs = width // PAIR_LANES
    affine_rows = affine_params.shape[0]
    affine_cols = jnp.pad(affine_params.astype(BF16).T, ((0, 0), (0, LANES - affine_rows)))
    block_one = chip_rows(
        jnp.concatenate([qkv_weight.astype(BF16), proj_weight.astype(BF16)], 1), (half,) * 4, affine_cols
    )
    block_two = chip_rows(inner_weight.astype(BF16), (hidden // 2,))
    block_three = chip_rows(outer_weight.astype(BF16), (half,))
    rows_chip, rows_outer = block_one.shape[0], block_three.shape[0]
    table, table_outer = kernel_order(order, rows_chip), kernel_order(order_outer, rows_chip)

    side = lax.axis_index("pair")
    own_ids, other_ids = pick(side, doc_ids[0], doc_ids[1]), pick(side, doc_ids[1], doc_ids[0])
    own_count, other_count = (
        pick(side, span_counts[0], span_counts[1]),
        pick(side, span_counts[1], span_counts[0]),
    )
    slot = jnp.arange(spans)
    anchor_live = jnp.broadcast_to((slot < own_count)[:, None], (spans, spans))
    key_live = jnp.broadcast_to((slot < other_count)[None, :], (spans, spans))
    match = (own_ids[:, None] == other_ids[None, :]) & anchor_live & key_live
    masks = jnp.stack([match, key_live, anchor_live]).astype(F32)
    live_rows = (own_count * L)[None]

    steps, steps_outer = flip_steps(chips), near_first(chips)
    one, two, three = Gather(block_one, steps), Gather(block_two, steps), Gather(block_three, steps_outer)
    one.step()
    three.step()
    first = one.step()
    three.step(three.got)
    first = (first, three.got)
    one.step(*first)
    two.step(*first)
    second = (one.got, two.got)
    one.step(*second)
    two.step(*second)
    third = (one.got, two.got)
    three.step(*second)
    own, other = one.finish(order, rows_chip, *third)
    two.step(*third)
    qkv_w, proj_w, affine, projected = projection_forward(table, tokens, own, other, affine_rows)
    two.step(two.got, projected)
    three.step()
    attention, context, normed_one, inv_one, skip_low = attention_forward(tokens, projected, proj_w, affine)
    own, other = two.finish(order, rows_chip, skip_low)
    w_own, act_own, slope_own = inner_forward(table, 0, skip_low, own, affine)
    w_other, act_other, slope_other = inner_forward(table, 1, skip_low, other, affine)
    own, other = three.finish(order_outer, rows_outer, act_own)
    outer_w, layer_out, grad_two, low, sums_two, cls, cls_normed, cls_inv = outer_forward(
        table_outer, act_own, act_other, own, other, normed_one, affine, mlm_grad, live_rows
    )
    low, more, sums_two, loss, own, other = outer_backward(
        table, low, sums_two, cls, core_swapped(cls), masks, cls_normed, cls_inv, act_own, act_other, affine
    )

    red_outer = Reduce(*in_order(order, own, other, rows_outer))
    inner_other, bias_other, blocks_other = inner_backward(table, 1, low, slope_other, outer_w, skip_low)
    core_done = red_outer.last()
    got = red_outer.step()
    inner_own, bias_own, blocks_own = inner_backward(table, 0, low, slope_own, outer_w, skip_low, (core_done,))
    red_inner = Reduce(*in_order(order, blocks_own, blocks_other, rows_chip))
    grad_one, grad_one_low, sums_one, context_grad = skip_backward(
        inner_own, inner_other, w_own, w_other, grad_two, more, normed_one, inv_one, affine, proj_w,
        (red_inner.last(), got),
    )
    groups = (
        tuple(p for p in range(pairs) if p % (pairs // 2)),
        tuple(p for p in range(pairs) if not p % (pairs // 2)),
    )
    qkv_low, qkv_sums = [None, None], [None, None]
    got_outer, got_inner = red_outer.step(), red_inner.step()
    qkv_low[0], qkv_sums[0] = attention_backward(groups[0], context_grad, projected, attention)
    own, other = qkv_backward(table, tokens, qkv_low[0], (context, grad_one_low), None, (got_outer,))
    red_first = Reduce(*in_order(order, own, other, rows_chip))
    core_done = red_first.last()
    qkv_low[1], qkv_sums[1] = attention_backward(groups[1], context_grad, projected, attention, (got_inner,))
    got_outer, got_inner = red_outer.step(), red_inner.step()
    own, other = qkv_backward(
        table, tokens, qkv_low[1], None, (sums_one, sums_two, qkv_sums[1], qkv_sums[0], bias_own, bias_other),
        (core_done,),
    )
    red_first.step(got_inner)
    red_second = Reduce(*in_order(order, own, other, rows_chip))
    core_done = red_second.last()
    red_second.step()
    input_grad = tokens_backward(groups, qkv_low, qkv_w, grad_one, (core_done,))
    red_first.step(input_grad)
    red_second.step(input_grad)
    outer_mine, outer_theirs, inner_mine, inner_theirs, squares = summed(
        table, (red_outer.finish(), red_inner.finish())
    )
    first_mine, first_theirs, second_mine, second_theirs, squares = summed(
        table, (red_first.finish(), red_second.finish()), (1,), loss, squares
    )
    totals = total_over_devices(squares)
    grads = []
    for mine, theirs in (
        (outer_mine, outer_theirs),
        (inner_mine, inner_theirs),
        (first_mine, first_theirs),
        (second_mine, second_theirs),
    ):
        grads += [mine, core_swapped(theirs)]
    grads.append(second_mine[:, half : half + affine_rows].T)
    slots = spans * lax.axis_size("dp") * lax.axis_size("pair")
    updated = adamw(
        table,
        totals,
        grads,
        (qkv_weight, proj_weight, inner_weight, outer_weight, affine_params),
        (qkv_moment, proj_moment, inner_moment, outer_moment, affine_moment),
        (qkv_square, proj_square, inner_square, outer_square, affine_square),
        slots,
    )
    state = [updated[3 * n + k] for k in range(3) for n in range(5)]
    return (*state, layer_out, input_grad, updated[-1][0, 0], updated[-1][1, 0])


def solution(mesh):
    placed = (
        P(("dp", "pair"), None),
        P(("dp", "pair"), None),
        P("dp", None),
        P("dp"),
        P(("dp", "pair"), None),
        P(("dp", "pair"), None),
        P(("dp", "pair"), None),
        P(("dp", "pair"), None),
        P(None, ("dp", "pair")),
        P(("dp", "pair"), None),
        P(("dp", "pair"), None),
        P(("dp", "pair"), None),
        P(("dp", "pair"), None),
        P(None, ("dp", "pair")),
        P(("dp", "pair"), None),
        P(("dp", "pair"), None),
        P(("dp", "pair"), None),
        P(("dp", "pair"), None),
        P(None, ("dp", "pair")),
    )
    return jax.shard_map(
        body,
        mesh=mesh,
        in_specs=placed,
        out_specs=(
            P(("dp", "pair"), None),
            P(("dp", "pair"), None),
            P(("dp", "pair"), None),
            P(("dp", "pair"), None),
            P(None, ("dp", "pair")),
            P(("dp", "pair"), None),
            P(("dp", "pair"), None),
            P(("dp", "pair"), None),
            P(("dp", "pair"), None),
            P(None, ("dp", "pair")),
            P(("dp", "pair"), None),
            P(("dp", "pair"), None),
            P(("dp", "pair"), None),
            P(("dp", "pair"), None),
            P(None, ("dp", "pair")),
            P(("dp", "pair"), None),
            P(("dp", "pair"), None),
            P(),
            P(),
        ),
        check_vma=False,
    )
```

```python
from functools import partial

import jax
import jax.numpy as jnp
from jax import lax
from jax.experimental import pallas as pl
from jax.experimental.pallas import tpu as pltpu
from jax.sharding import PartitionSpec as P

HEADS = 12
HD = 64
L = 128
STEP = 10
LANES = 128
AXES = ("dp", "pair")


LN_EPS = 1e-12
LOSS_WEIGHT = 8.0
CLIP_NORM = 1000.0
BETA_ONE = 0.9
BETA_TWO = 0.999
ADAM_EPS = 1e-08
RATE_MATRIX = 0.05
DECAY_MATRIX = 0.01
RATE_AFFINE = 0.8
DECAY_AFFINE = 0.0

BF16 = jnp.bfloat16
F32 = jnp.float32


def flip_steps(chips):
    bits = chips.bit_length() - 1
    if bits == 4:
        return ((2, 3), (3, 2), (0, 1), (1, 0))
    return tuple((bit, bit) for bit in reversed(range(bits)))


def flip_route(chips, pair_of_bits):
    return [
        (2 * d + c, 2 * (d ^ (1 << pair_of_bits[c])) + c) for d in range(chips) for c in range(2)
    ]


def core_route(chips):
    return [(2 * d + c, 2 * d + 1 - c) for d in range(chips) for c in range(2)]


def flipped(block, bits):
    chips = lax.axis_size("dp")
    return lax.ppermute(block, AXES, flip_route(chips, bits))


def core_swapped(block):
    return lax.ppermute(block, AXES, core_route(lax.axis_size("dp")))


def near_first(chips):
    steps = flip_steps(chips)
    return steps[2:] + steps[:2] if len(steps) == 4 else steps


def block_order(steps):
    chips = lax.axis_size("dp")
    d, c = lax.axis_index("dp"), lax.axis_index("pair")
    index = jnp.arange(chips, dtype=jnp.int32)
    blocks, places = [], []
    for core in range(2):
        blocks.append(sum((index >> k & 1) << step[core] for k, step in enumerate(steps)) ^ d)
        places.append(sum(((index ^ d) >> step[core] & 1) << k for k, step in enumerate(steps)))
    rows = []
    for pairs in (blocks, places):
        rows += [pick(c, pairs[0], pairs[1]), pick(c, pairs[1], pairs[0])]
    return jnp.stack(rows + [jnp.full((chips,), c, jnp.int32)])


def kernel_order(order, rows):
    if rows % 16 == 0:
        return order
    index = jnp.arange(16, dtype=jnp.int32)
    return jnp.stack([index] * 4 + [jnp.full((16,), order[4, 0], jnp.int32)])


def in_order(order, own, other, rows):
    if rows % 16 == 0:
        return own, other
    return tuple(
        blocks.reshape(order.shape[1], rows, -1)[order[side]] for side, blocks in enumerate((own, other))
    )


def pick(core, first, second):
    return jnp.where(core == 0, first, second)


def halves_of(low, pieces):
    core = lax.axis_index("pair")
    first, second, at = [], [], 0
    for width in pieces:
        first.append(low[:, at : at + width])
        second.append(low[:, at + width : at + 2 * width])
        at += 2 * width
    first, second = jnp.concatenate(first, 1), jnp.concatenate(second, 1)
    return pick(core, first, second), pick(core, second, first)


def chip_rows(low, pieces, extra=None):
    core = lax.axis_index("pair")
    own, other = halves_of(low, pieces)
    if extra is not None:
        own, other = (jnp.concatenate([half, extra], 1) for half in (own, other))
    got = core_swapped(other)
    return pick(core, jnp.concatenate([own, got]), jnp.concatenate([got, own]))


def tied(value, *others):
    return lax.optimization_barrier((value, *others))[0]


class Gather:
    def __init__(self, block, steps):
        self.held, self.got, self.left = block[None], None, list(steps)

    def step(self, *others):
        if self.got is not None:
            self.held = jnp.concatenate([self.held, self.got], axis=0)
        self.got = flipped(tied(self.held, *others), self.left.pop(0))
        return self.got

    def finish(self, order, rows, *others):
        while self.left:
            self.step()
        own = (self.held, self.got)
        other = tuple(core_swapped(tied(part, *others)) for part in own)
        if rows % 16:
            own, other = (
                jnp.zeros((2 * self.held.shape[0], *self.held.shape[1:]), BF16)
                .at[order[side]]
                .set(jnp.concatenate(parts))
                .reshape(2, 8, -1, self.held.shape[2])
                for side, parts in enumerate((own, other))
            )
            own, other = (own[0], own[1]), (other[0], other[1])
        return own, other


class Reduce:
    def __init__(self, own, other):
        self.count, self.left = own.shape[0], list(reversed(flip_steps(lax.axis_size("dp"))))
        self.parts = [own, core_swapped(other)]

    def last(self):
        return self.parts[-1]

    def step(self, *others):
        self.count //= 2
        sent = sum(p[self.count : 2 * self.count].astype(F32) for p in self.parts).astype(BF16)
        self.parts.append(flipped(tied(sent, *others), self.left.pop(0)))
        return self.parts[-1]

    def finish(self):
        while self.left:
            self.step()
        return self.parts


def total_over_devices(value):
    bits = lax.axis_size("dp").bit_length() - 1
    value = value + core_swapped(value)
    for low in range(0, bits, 2):
        first = flipped(value, (low, low))
        if low + 1 < bits:
            second = flipped(value, (low + 1, low + 1))
            route = [(2 * d + c, 2 * (d ^ (3 << low)) + c) for d in range(1 << bits) for c in range(2)]
            both = lax.ppermute(value, AXES, route)
            bit, over = (lax.axis_index("dp") >> low & 1) == 0, (lax.axis_index("dp") >> low & 2) == 0
            near = jnp.where(bit, value, first) + jnp.where(bit, first, value)
            far_sum = jnp.where(bit, second, both) + jnp.where(bit, both, second)
            value = jnp.where(over, near, far_sum) + jnp.where(over, far_sum, near)
        else:
            value = value + first
    return value


TILE = 256
PART = 256
PAIR_LANES = 2 * HD
VMEM_LIMIT = 32 * 1024 * 1024
SMEM = pl.BlockSpec(memory_space=pltpu.SMEM)
ANY = pl.BlockSpec(memory_space=pl.ANY)


def call(kernel, grid, ins, outs, scratch=(), micros=10, after=(), order=None):
    count = len(ins) + (order is not None)

    def body(*refs):
        kernel(*refs[:count], *refs[count + len(after) :])

    in_specs = [spec for _, spec in ins] + [ANY] * len(after)
    operands = [array for array, _ in ins] + list(after)
    if order is not None:
        operands = [order] + operands
    return pl.pallas_call(
        body,
        grid_spec=pltpu.PrefetchScalarGridSpec(
            num_scalar_prefetch=int(order is not None),
            grid=grid,
            in_specs=in_specs,
            out_specs=tuple(spec for _, spec in outs),
            scratch_shapes=list(scratch),
        ),
        out_shape=tuple(shape for shape, _ in outs),
        compiler_params=pltpu.CompilerParams(
            vmem_limit_bytes=VMEM_LIMIT, dimension_semantics=("arbitrary",) * len(grid)
        ),
        cost_estimate=pl.CostEstimate(
            flops=micros * 300_000_000, bytes_accessed=micros * 300_000, transcendentals=0
        ),
    )(*operands)


def whole(shape):
    return pl.BlockSpec(shape, lambda i, *_: (0,) * len(shape))


def rows_of(count, width):
    return pl.BlockSpec((count, width), lambda i, *_: (i, 0))


def cols_of(height, count):
    return pl.BlockSpec((height, count), lambda i, *_: (0, i))


def struct(shape, dtype):
    return jax.ShapeDtypeStruct(shape, dtype)


def streamed(array):
    return pltpu.with_memory_space_constraint(array, pltpu.HBM)


def far(shape, dtype):
    return pltpu.HBM(shape, dtype)


def dot(left, right):
    return jnp.dot(left, right, preferred_element_type=F32)


def contract_rows(left, right):
    return lax.dot_general(left, right, (((0,), (0,)), ((), ())), preferred_element_type=F32)


def contract_cols(left, right):
    return lax.dot_general(left, right, (((1,), (1,)), ((), ())), preferred_element_type=F32)


def normalize(total):
    centered = total - jnp.mean(total, axis=-1, keepdims=True)
    variance = jnp.mean(centered * centered, axis=-1, keepdims=True)
    scale_inv = lax.rsqrt(variance + LN_EPS)
    return (centered * scale_inv, scale_inv)


def normalize_back(upstream, normed, scale_inv, gain):
    scaled = upstream * gain
    return scale_inv * (
        scaled
        - jnp.mean(scaled, axis=-1, keepdims=True)
        - normed * jnp.mean(scaled * normed, axis=-1, keepdims=True)
    )


def gelu_and_slope(pre):
    below = 0.5 + 0.5 * lax.erf(pre * 0.5**0.5)
    return pre * below, below + pre * jnp.exp(pre * pre * -0.5) * (2 * jnp.pi) ** -0.5


def two_heads(block, lane_low):
    zero = jnp.zeros_like(block)
    return jnp.concatenate([jnp.where(lane_low, block, zero), jnp.where(lane_low, zero, block)], 0)


def lane_is_low(rows):
    return lax.broadcasted_iota(jnp.int32, (rows, PAIR_LANES), 1) < HD


def column_sum(value):
    return jnp.sum(value, axis=0, keepdims=True)


def placed(refs, place):
    count = refs[0].shape[0]
    return refs[place // count].at[place % count]


def fetches(order_ref, own_refs, other_refs, target, sems, rows, width, start=0, lane=0):
    core = order_ref[4, 0]
    copies = []
    for place in range(sems.shape[0]):
        pair = []
        for side, refs in enumerate((own_refs, other_refs)):
            half = core if side == 0 else 1 - core
            row = pl.multiple_of(order_ref[side, place] * rows, rows)
            pair.append(
                pltpu.make_async_copy(
                    placed(refs, place).at[:, pl.ds(lane, width)],
                    target.at[pl.ds(row, rows), pl.ds(pl.multiple_of(start + half * width, LANES), width)],
                    sems.at[place, side],
                )
            )
        copies.append(pair)
    return copies


def begin(copies):
    for pair in copies:
        for copy in pair:
            copy.start()


def finish(copies):
    for pair in copies:
        for copy in pair:
            copy.wait()


def in_turn(count, *stages):
    held = stages[0](0)
    for n in range(count):
        value, held = held, stages[0](n + 1) if n + 1 < count else None
        for stage in stages[1:]:
            value = stage(n, value)


def projection_forward(order, tokens, own, other, affine_rows, after=()):
    rows, width = tokens.shape
    half = width // 2
    chips, block = 2 * own[0].shape[0], own[0].shape[1]

    def kernel(
        order_ref, tokens_ref, own_a, own_b, other_a, other_b,
        w_ref, proj_ref, affine_ref, out_ref, columns, sems, column_sems,
    ):
        own_refs, other_refs = (own_a, own_b), (other_a, other_b)
        step = pl.program_id(0)
        params = [
            pltpu.make_async_copy(
                placed(own_refs, p).at[:, pl.ds(4 * half, LANES)],
                columns.at[pl.ds(pl.multiple_of(order_ref[0, p] * block, block), block), :],
                column_sems.at[p],
            )
            for p in range(chips)
        ]
        parts = [
            fetches(order_ref, own_refs, other_refs, w_ref, sems.at[k], block, half, k * width, k * half)
            for k in range(3)
        ]
        parts.append(fetches(order_ref, own_refs, other_refs, proj_ref, sems.at[3], block, half, 0, 3 * half))

        @pl.when(step == 0)
        def _():
            for copy in params:
                copy.start()
            for copies in parts:
                begin(copies)
            for copy in params:
                copy.wait()
            affine_ref[...] = columns[...].astype(F32).T[:affine_rows]

        for k in range(3):

            @pl.when(step == k)
            def _():
                finish(parts[k])
                for n in range(width // TILE):
                    cols = slice(n * TILE, (n + 1) * TILE)
                    value = dot(tokens_ref[...], w_ref[:, k * width + n * TILE : k * width + (n + 1) * TILE])
                    if k != 1:
                        value += affine_ref[4 + k // 2 : 5 + k // 2, cols]
                    out_ref[:, cols] = value.astype(BF16)

        @pl.when(step == 2)
        def _():
            finish(parts[3])

    return call(
        kernel,
        (3,),
        [(tokens, whole(tokens.shape)), *((blocks, ANY) for blocks in (*own, *other))],
        [
            (far((width, 3 * width), BF16), whole((width, 3 * width))),
            (struct((width, width), BF16), whole((width, width))),
            (struct((affine_rows, width), F32), whole((affine_rows, width))),
            (struct((rows, 3 * width), BF16), cols_of(rows, width)),
        ],
        [
            pltpu.VMEM((width, LANES), BF16),
            pltpu.SemaphoreType.DMA((4, chips, 2)),
            pltpu.SemaphoreType.DMA((chips,)),
        ],
        8,
        after,
        order,
    )


def attention_forward(tokens, projected, proj_w, affine, after=()):
    rows, width = tokens.shape
    spans, pairs = rows // L, width // PAIR_LANES
    each = PART // L

    def kernel(
        tokens_ref, projected_ref, proj_ref, affine_ref,
        attention_ref, context_ref, normed_ref, inv_ref, skip_ref,
    ):
        lane_low = lane_is_low(L)

        def read(n, part):
            s, p = divmod(n, pairs)
            at = part * width + p * PAIR_LANES
            return projected_ref[s * L : (s + 1) * L, at : at + PAIR_LANES]

        def scored(n):
            return contract_cols(two_heads(read(n, 0) * jnp.asarray(HD**-0.5, BF16), lane_low), read(n, 1))

        def weighed(n, scores):
            s, p = divmod(n, pairs)
            exponent = jnp.exp(scores - jnp.max(scores, axis=-1, keepdims=True))
            low = (exponent * (1.0 / jnp.sum(exponent, axis=-1, keepdims=True))).astype(BF16)
            attention_ref[s, p] = low
            both = dot(low, read(n, 2))
            context_ref[s * L : (s + 1) * L, p * PAIR_LANES : (p + 1) * PAIR_LANES] = jnp.where(
                lane_low, both[:L], both[L:]
            ).astype(BF16)

        in_turn(each * pairs, scored, weighed)
        total = dot(context_ref[...], proj_ref[...]) + affine_ref[6:7, :]
        normed, inv = normalize(tokens_ref[...].astype(F32) + total)
        normed_ref[...] = normed.astype(BF16)
        inv_ref[...] = jnp.broadcast_to(inv, (PART, LANES))
        skip_ref[...] = (normed * affine_ref[0:1, :] + affine_ref[1:2, :]).astype(BF16)

    return call(
        kernel,
        (rows // PART,),
        [
            (tokens, rows_of(PART, width)),
            (projected, rows_of(PART, 3 * width)),
            (proj_w, whole(proj_w.shape)),
            (affine, whole(affine.shape)),
        ],
        [
            (
                far((spans, pairs, 2 * L, L), BF16),
                pl.BlockSpec((each, pairs, 2 * L, L), lambda i, *_: (i, 0, 0, 0)),
            ),
            (far((rows, width), BF16), rows_of(PART, width)),
            (far((rows, width), BF16), rows_of(PART, width)),
            (far((rows, LANES), F32), rows_of(PART, LANES)),
            (struct((rows, width), BF16), rows_of(PART, width)),
        ],
        (),
        12,
        after,
    )


def inner_forward(order, side, skip_low, blocks, affine, after=()):
    rows, width = skip_low.shape
    count, block, half = blocks[0].shape
    chips = 2 * count

    def kernel(order_ref, skip_ref, first_ref, second_ref, affine_ref, w_ref, act_ref, slope_ref, sems):
        step = pl.program_id(0)

        def copies(p):
            row = pl.multiple_of(order_ref[side, p] * block, block)
            return pltpu.make_async_copy(
                placed((first_ref, second_ref), p), w_ref.at[pl.ds(row, block), :], sems.at[p]
            )

        @pl.when(step == 0)
        def _():
            for b in range(chips):
                copies(b).start()
            for b in range(chips):
                copies(b).wait()

        first = order_ref[4, 0] if side == 0 else 1 - order_ref[4, 0]
        bias = affine_ref[pl.ds(8 + first * (half // width) + step, 1), :]
        parts = rows // PART

        def entered(n):
            k, r = divmod(n, parts)
            weight = w_ref[:, pl.ds(pl.multiple_of(step * width + k * TILE, LANES), TILE)]
            return dot(skip_ref[r * PART : (r + 1) * PART, :], weight)

        def activated(n, value):
            k, r = divmod(n, parts)
            at, cols = slice(r * PART, (r + 1) * PART), slice(k * TILE, (k + 1) * TILE)
            act, slope = gelu_and_slope(value + bias[:, cols])
            act_ref[at, cols] = act.astype(BF16)
            slope_ref[at, cols] = slope.astype(BF16)

        in_turn(width // TILE * parts, entered, activated)

    return call(
        kernel,
        (half // width,),
        [(skip_low, whole(skip_low.shape)), (blocks[0], ANY), (blocks[1], ANY), (affine, whole(affine.shape))],
        [
            (far((width, half), BF16), whole((width, half))),
            (struct((rows, half), BF16), cols_of(rows, width)),
            (far((rows, half), BF16), cols_of(rows, width)),
        ],
        [pltpu.SemaphoreType.DMA((chips,))],
        10,
        after,
        order,
    )


def outer_forward(order, act_own, act_other, own, other, skip_low, affine, mlm_grad, live_rows, after=()):
    rows, wide = act_own.shape
    hidden, width = 2 * wide, skip_low.shape[1]
    chips, block = 2 * own[0].shape[0], own[0].shape[1]
    spans = rows // L
    many = 2
    tile = many * PART

    def kernel(
        order_ref, act_own_ref, act_other_ref, own_a, own_b, other_a, other_b, skip_ref, affine_ref, mlm_ref, live_ref,
        w_ref, out_ref, low_ref, sums_ref, cls_ref, cls_normed_ref, cls_inv_ref, sems,
    ):
        step = pl.program_id(0)

        core = order_ref[4, 0]

        def entered(n):
            at = slice(n * PART, (n + 1) * PART)
            total = 0.0
            for k, ref in enumerate((act_own_ref, act_other_ref)):
                start = (core if k == 0 else 1 - core) * wide
                total = total + dot(ref[at, :], w_ref[pl.ds(pl.multiple_of(start, LANES), wide), :])
            return total

        def ended(n, total):
            at = slice(n * PART, (n + 1) * PART)
            normed, inv = normalize(skip_ref[at, :].astype(F32) + (total + affine_ref[7:8, :]))
            out = (normed * affine_ref[2:3, :] + affine_ref[3:4, :]).astype(BF16)
            out_ref[at, :] = out
            line = lax.broadcasted_iota(jnp.int32, (PART, 1), 0)
            live = line < live_ref[0] - (step * many + n) * PART
            upstream = jnp.where(live, mlm_ref[at, :].astype(F32), 0.0)
            grad = normalize_back(upstream, normed, inv, affine_ref[2:3, :])
            low_ref[at, :] = grad.astype(BF16)
            for k, value in enumerate((upstream * normed, upstream, grad)):
                sums_ref[k : k + 1, :] += column_sum(value)
            for s in range(PART // L):
                row, to = slice(s * L, s * L + 1), pl.ds((step * many + n) * (PART // L) + s, 1)
                cls_ref[to, :] = out[s * L : s * L + 16].astype(F32)[:1]
                cls_normed_ref[to, :] = normed[row]
                cls_inv_ref[to, :] = jnp.broadcast_to(inv[row], (1, LANES))

        copies = fetches(order_ref, (own_a, own_b), (other_a, other_b), w_ref, sems, block, width // 2)

        @pl.when(step == 0)
        def _():
            begin(copies)
            sums_ref[...] = jnp.zeros_like(sums_ref)
            finish(copies)

        in_turn(many, entered, ended)

    return call(
        kernel,
        (rows // tile,),
        [
            (act_own, rows_of(tile, wide)),
            (act_other, rows_of(tile, wide)),
            *((blocks, ANY) for blocks in (*own, *other)),
            (skip_low, rows_of(tile, width)),
            (affine, whole(affine.shape)),
            (streamed(mlm_grad), rows_of(tile, width)),
            (live_rows, SMEM),
        ],
        [
            (far((hidden, width), BF16), whole((hidden, width))),
            (far((rows, width), BF16), rows_of(tile, width)),
            (struct((rows, width), BF16), rows_of(tile, width)),
            (struct((8, width), F32), whole((8, width))),
            (struct((spans, width), F32), whole((spans, width))),
            (struct((spans, width), F32), whole((spans, width))),
            (struct((spans, LANES), F32), whole((spans, LANES))),
        ],
        [pltpu.SemaphoreType.DMA((chips, 2))],
        8,
        after,
        order,
    )


def loss_and_gradient(own, other, match, key_live, anchor_live):
    scale = own.shape[1] ** -0.5
    sims = contract_cols(own.astype(BF16), other.astype(BF16)) * scale
    step = jnp.zeros_like(sims)
    loss = None
    for axis, live in ((1, key_live), (0, anchor_live)):
        masked = jnp.where(live > 0, sims, -1000000000.0)
        peak = jnp.max(masked, axis=axis, keepdims=True)
        weights = jnp.where(live > 0, jnp.exp(masked - peak), 0.0)
        total = jnp.sum(weights, axis=axis, keepdims=True)
        active = jnp.max(match, axis=axis, keepdims=True)
        step += active * (weights / total - match)
        if loss is None:
            hit = jnp.sum(match * sims, axis=axis, keepdims=True)
            loss = jnp.sum(jnp.where(active > 0, peak + jnp.log(total) - hit, 0.0), axis=0, keepdims=True)
    step *= LOSS_WEIGHT * scale
    gradient = jnp.zeros_like(own)
    for k in range(other.shape[0]):
        gradient += step[:, k : k + 1] * other[k : k + 1, :]
    return loss, gradient


def outer_backward(order, grad_low, sums, cls, cls_other, masks, cls_normed, cls_inv, act_own, act_other, affine, after=()):
    rows, width = grad_low.shape
    hidden = 2 * act_own.shape[1]
    chips = order.shape[1]
    block, half = hidden // chips, width // 2
    tile = 4 * block
    turn = chips // 8
    spans = rows // L

    def kernel(
        order_ref, low_in_ref, sums_in_ref, cls_ref, cls_other_ref, masks_ref, normed_ref, inv_ref, act_own_ref, act_other_ref, affine_ref,
        low_ref, sums_ref, loss_ref, own_ref, other_ref, own_held, other_held, sems,
    ):
        step = pl.program_id(0)

        @pl.when(step == 0)
        def _():
            loss, up = loss_and_gradient(
                cls_ref[...], cls_other_ref[...], masks_ref[0], masks_ref[1], masks_ref[2]
            )
            normed = normed_ref[...]
            more = normalize_back(up, normed, inv_ref[:, :1], affine_ref[2:3, :])
            loss_ref[...] = jnp.broadcast_to(loss, loss_ref.shape)
            for k, value in enumerate((up * normed, up, more)):
                sums_ref[k : k + 1, :] = sums_in_ref[k : k + 1, :] + column_sum(value)
            low_ref[...] = low_in_ref[...]
            line = lax.broadcasted_iota(jnp.int32, (16, 1), 0)
            for s in range(spans):
                at = slice(s * L, s * L + 16)
                changed = low_in_ref[at, :].astype(F32) + jnp.where(line == 0, more[s : s + 1], 0.0)
                low_ref[at, :] = changed.astype(BF16)

        core = order_ref[4, 0]

        def gradient(act_ref, first):
            def entered(n):
                return contract_rows(act_ref[:, n * 2 * block : (n + 1) * 2 * block], low_ref[...])

            def ended(n, value):
                low, high = value[:, :half], value[:, half:]
                parts = (jnp.where(core == 0, low, high), jnp.where(core == 0, high, low))
                for side, (part, held, out) in enumerate(
                    zip(parts, (own_held, other_held), (own_ref, other_ref))
                ):
                    for k in range(2):
                        b = first + 2 * n + k
                        held[b] = part[k * block : (k + 1) * block].astype(BF16)
                        pltpu.make_async_copy(
                            held.at[b], out.at[order_ref[2 + side, b]], sems.at[side, b]
                        ).start()

            in_turn(2, entered, ended)

        @pl.when(step < turn)
        def _():
            gradient(act_own_ref, core * (chips // 2) + 4 * step)

        @pl.when(step >= turn)
        def _():
            gradient(act_other_ref, (1 - core) * (chips // 2) + 4 * (step - turn))

        @pl.when(step == 2 * turn - 1)
        def _():
            for side, (held, out) in enumerate(((own_held, own_ref), (other_held, other_ref))):
                for b in range(chips):
                    pltpu.make_async_copy(
                        held.at[b], out.at[order_ref[2 + side, b]], sems.at[side, b]
                    ).wait()

    shape = (chips, block, half)
    return call(
        kernel,
        (hidden // tile,),
        [
            (grad_low, whole(grad_low.shape)),
            (sums, whole(sums.shape)),
            (cls, whole(cls.shape)),
            (cls_other, whole(cls.shape)),
            (masks, whole(masks.shape)),
            (cls_normed, whole(cls.shape)),
            (cls_inv, whole(cls_inv.shape)),
            (act_own, pl.BlockSpec((rows, tile), lambda i, *_: (0, jnp.minimum(i, turn - 1)))),
            (act_other, pl.BlockSpec((rows, tile), lambda i, *_: (0, jnp.maximum(i - turn, 0)))),
            (affine, whole(affine.shape)),
        ],
        [
            (struct((rows, width), BF16), whole((rows, width))),
            (struct((8, width), F32), whole((8, width))),
            (struct((8, LANES), F32), whole((8, LANES))),
            (far(shape, BF16), ANY),
            (far(shape, BF16), ANY),
        ],
        [
            pltpu.VMEM(shape, BF16),
            pltpu.VMEM(shape, BF16),
            pltpu.SemaphoreType.DMA((2, chips)),
        ],
        8,
        after,
        order,
    )


def inner_backward(order, side, low, slope, outer_w, skip_low, after=()):
    rows, width = low.shape
    hidden = 2 * slope.shape[1]
    chips = order.shape[1]
    block = width // chips
    steps = hidden // 2 // width

    def kernel(order_ref, low_ref, slope_ref, outer_ref, skip_ref, inner_ref, bias_ref, out_ref):
        step = pl.program_id(0)

        def entered(n):
            return contract_cols(low_ref[...], outer_ref[n * TILE : (n + 1) * TILE, :])

        def sloped(n, value):
            cols = slice(n * TILE, (n + 1) * TILE)
            inner_grad = value * slope_ref[:, cols].astype(F32)
            bias_ref[pl.ds(step, 1), cols] = column_sum(inner_grad)
            inner_low = inner_grad.astype(BF16)
            inner_ref[:, cols] = inner_low
            return contract_rows(skip_ref[...], inner_low).astype(BF16)

        def stored(n, value):
            for b in range(chips):
                out_ref[order_ref[2 + side, b], :, n * TILE : (n + 1) * TILE] = value[b * block : (b + 1) * block]

        in_turn(width // TILE, entered, sloped, stored)

    def place(i, table):
        half = table[4, 0] if side == 0 else 1 - table[4, 0]
        return half * steps + i

    return call(
        kernel,
        (steps,),
        [
            (low, whole(low.shape)),
            (streamed(slope), cols_of(rows, width)),
            (streamed(outer_w), pl.BlockSpec((width, width), lambda i, table: (place(i, table), 0))),
            (skip_low, whole(skip_low.shape)),
        ],
        [
            (struct((rows, hidden // 2), BF16), cols_of(rows, width)),
            (struct((8, width), F32), whole((8, width))),
            (
                struct((chips, block, hidden // 2), BF16),
                pl.BlockSpec((chips, block, width), lambda i, *_: (0, 0, i)),
            ),
        ],
        (),
        8,
        after,
        order,
    )


def skip_backward(inner_own, inner_other, w_own, w_other, grad_two_low, normed_one, inv_one, affine, proj_w, after=()):
    rows, width = grad_two_low.shape
    half = w_own.shape[1]
    many = 2
    tile = many * PART

    def kernel(
        own_ref, other_ref, w_own_ref, w_other_ref, grad_two_ref, normed_ref, inv_ref, affine_ref, proj_ref,
        low_ref, sums_ref, context_ref,
    ):
        step = pl.program_id(0)

        @pl.when(step == 0)
        def _():
            sums_ref[...] = jnp.zeros_like(sums_ref)

        def entered(n):
            at = slice(n * PART, (n + 1) * PART)
            up = grad_two_ref[at, :].astype(F32)
            for ref, weight in ((own_ref, w_own_ref), (other_ref, w_other_ref)):
                up = up + contract_cols(ref[at, :], weight[...])
            return up

        def ended(n, up):
            at = slice(n * PART, (n + 1) * PART)
            normed = normed_ref[at, :].astype(F32)
            grad = normalize_back(up, normed, inv_ref[at, :1], affine_ref[0:1, :])
            low = grad.astype(BF16)
            low_ref[at, :] = low
            for k, value in enumerate((up * normed, up, grad)):
                sums_ref[k : k + 1, :] += column_sum(value)
            context_ref[at, :] = contract_cols(low, proj_ref[...]).astype(BF16)

        in_turn(many, entered, ended)

    return call(
        kernel,
        (rows // tile,),
        [
            (inner_own, rows_of(tile, half)),
            (inner_other, rows_of(tile, half)),
            (streamed(w_own), whole(w_own.shape)),
            (streamed(w_other), whole(w_other.shape)),
            (grad_two_low, rows_of(tile, width)),
            (streamed(normed_one), rows_of(tile, width)),
            (streamed(inv_one), rows_of(tile, LANES)),
            (affine, whole(affine.shape)),
            (proj_w, whole(proj_w.shape)),
        ],
        [
            (struct((rows, width), BF16), rows_of(tile, width)),
            (struct((8, width), F32), whole((8, width))),
            (struct((rows, width), BF16), rows_of(tile, width)),
        ],
        (),
        8,
        after,
    )


def attention_backward(pairs, context_grad, projected, attention, after=()):
    rows, width = context_grad.shape
    spans, count = rows // L, len(pairs)
    wide = 3 * count * PAIR_LANES
    each = 2

    def kernel(grad_ref, projected_ref, attention_ref, out_ref, sums_ref):
        @pl.when(pl.program_id(0) == 0)
        def _():
            sums_ref[...] = jnp.zeros_like(sums_ref)

        lane_low = lane_is_low(L)
        def entered(m):
            s, n = divmod(m, count)
            at, line = pairs[n] * PAIR_LANES, slice(s * L, (s + 1) * L)
            grads = two_heads(grad_ref[line, at : at + PAIR_LANES], lane_low)
            v = projected_ref[line, 2 * width + at : 2 * width + at + PAIR_LANES]
            return grads, contract_cols(grads, v)

        def ended(m, value):
            s, n = divmod(m, count)
            at, line = pairs[n] * PAIR_LANES, slice(s * L, (s + 1) * L)
            q, k = (
                projected_ref[line, part * width + at : part * width + at + PAIR_LANES] for part in range(2)
            )
            grads, back = value
            low = attention_ref[s, pairs[n]]
            weights = low.astype(F32)
            product = back * weights
            score = (product - weights * jnp.sum(product, axis=-1, keepdims=True)) * HD**-0.5
            score_low = score.astype(BF16)
            both = dot(score_low, k)
            parts = (
                jnp.where(lane_low, both[:L], both[L:]),
                contract_rows(score_low, two_heads(q, lane_low)),
                contract_rows(low, grads),
            )
            for part, value in enumerate(parts):
                to = slice((part * count + n) * PAIR_LANES, (part * count + n + 1) * PAIR_LANES)
                out_ref[line, to] = value.astype(BF16)
                sums_ref[:, to] += column_sum(value)

        in_turn(each * count, entered, ended)

    return call(
        kernel,
        (spans // each,),
        [
            (context_grad, rows_of(each * L, width)),
            (streamed(projected), rows_of(each * L, 3 * width)),
            (streamed(attention), pl.BlockSpec((each, width // PAIR_LANES, 2 * L, L), lambda i, *_: (i, 0, 0, 0))),
        ],
        [
            (struct((rows, wide), BF16), rows_of(each * L, wide)),
            (struct((1, wide), F32), whole((1, wide))),
        ],
        (),
        3 * count,
        after,
    )


def store_blocks(order_ref, low, high, rows, own_ref, other_ref, lane):
    core = order_ref[4, 0]
    own = jnp.where(core == 0, low, high).astype(BF16)
    other = jnp.where(core == 0, high, low).astype(BF16)
    width = low.shape[1]
    for b in range(low.shape[0] // rows):
        at = slice(b * rows, (b + 1) * rows)
        own_ref[order_ref[2, b], :, lane : lane + width] = own[at]
        other_ref[order_ref[3, b], :, lane : lane + width] = other[at]


def qkv_backward(order, tokens, qkv_low, proj=None, sums=None, after=()):
    rows, width = tokens.shape
    chips = order.shape[1]
    block, half = width // chips, width // 2
    each = qkv_low.shape[1] // 6
    extra = half if proj is not None else LANES

    def affine_rows(sums_one, sums_two, first, second, bias_own, bias_other, lines, core):
        lines[...] = jnp.zeros_like(lines)
        lines[0:2, :] = sums_one[0:2, :]
        lines[2:4, :] = sums_two[0:2, :]
        for row, part in ((4, 0), (5, 2)):
            for h in range(2):
                at = h * half
                for ref in (first, second):
                    wide = ref.shape[1] // 6
                    lines[row : row + 1, at : at + wide] = ref[:, (2 * part + h) * wide : (2 * part + h + 1) * wide]
                    at += wide
        lines[6:7, :] = sums_one[2:3, :]
        lines[7:8, :] = sums_two[2:3, :]
        lines[8:10, :] = jnp.where(core == 0, bias_own[0:2, :], bias_other[0:2, :])
        lines[10:12, :] = jnp.where(core == 0, bias_other[0:2, :], bias_own[0:2, :])
        return lines[...].T

    def kernel(order_ref, tokens_ref, qkv_ref, *rest):
        rest, (own_ref, other_ref, lines) = rest[:-3], rest[-3:]

        def entered(k):
            if k < 3:
                return contract_rows(tokens_ref[...], qkv_ref[:, 2 * k * each : 2 * (k + 1) * each])
            if proj is not None:
                return contract_rows(rest[0][...], rest[1][...])
            value = affine_rows(*rest, lines, order_ref[4, 0])
            return jnp.concatenate([value, value], axis=1)

        def ended(k, value):
            middle = value.shape[1] // 2
            store_blocks(order_ref, value[:, :middle], value[:, middle:], block, own_ref, other_ref, k * each)

        in_turn(4, entered, ended)

    shape = (chips, block, 3 * each + extra)
    more = list(proj if proj is not None else sums)
    return call(
        kernel,
        (1,),
        [(array, whole(array.shape)) for array in (tokens, qkv_low, *more)],
        [(struct(shape, BF16), whole(shape)), (struct(shape, BF16), whole(shape))],
        [pltpu.VMEM((LANES, width), F32)],
        5,
        after,
        order,
    )


def tokens_backward(groups, qkv_lows, qkv_w, grad_one, after=()):
    rows, width = grad_one.shape

    def kernel(*refs):
        lows, (w_ref, grad_ref, out_ref, held) = refs[: len(groups)], refs[len(groups) :]
        for pairs, ref in zip(groups, lows):
            for part in range(3):
                for n, p in enumerate(pairs):
                    held[:, part * width + p * PAIR_LANES : part * width + (p + 1) * PAIR_LANES] = ref[
                        :, (part * len(pairs) + n) * PAIR_LANES : (part * len(pairs) + n + 1) * PAIR_LANES
                    ]
        out_ref[...] = contract_cols(held[...], w_ref[...]) + grad_ref[...].astype(F32)

    return call(
        kernel,
        (rows // PART,),
        [(low, rows_of(PART, low.shape[1])) for low in qkv_lows]
        + [(streamed(qkv_w), whole(qkv_w.shape)), (grad_one, rows_of(PART, width))],
        [(struct((rows, width), F32), rows_of(PART, width))],
        [pltpu.VMEM((PART, 3 * width), BF16)],
        8,
        after,
    )[0]


def summed(order, chunks, doubled=(), loss=None, before=None):
    counts = [len(parts) for parts in chunks]
    shapes = [(parts[0].shape[1] // 2, parts[0].shape[2]) for parts in chunks]
    extras = [loss] if loss is not None else []
    extras += [before] if before is not None else []
    arrays = [p for parts in chunks for p in parts]

    def kernel(order_ref, *refs):
        core = order_ref[4, 0]
        squares = 0.0
        outs = refs[len(arrays) + len(extras) :]
        at = 0
        for n, count in enumerate(counts):
            rows, cols = shapes[n]
            total = sum(ref[0].astype(F32) for ref in refs[at : at + count])
            at += count
            first, second = total[:rows], total[rows:]
            mine, theirs = jnp.where(core == 0, first, second), jnp.where(core == 0, second, first)
            outs[2 * n][...] = mine
            outs[2 * n + 1][...] = theirs
            squares += jnp.sum(mine * mine)
            theirs = theirs[:, : cols - LANES] if n in doubled else theirs
            squares += jnp.sum(theirs * theirs)
        line = lax.broadcasted_iota(jnp.int32, (8, LANES), 0)
        result = jnp.where(line == 0, squares, 0.0)
        if loss is not None:
            result += jnp.where(line == 1, refs[len(arrays)][0:1, :], 0.0)
        if before is not None:
            result += refs[len(arrays) + len(extras) - 1][...]
        outs[-1][...] = result

    return call(
        kernel,
        (1,),
        [(p, pl.BlockSpec((1, *p.shape[1:]), lambda i, *_: (0, 0, 0))) for p in arrays]
        + [(x, whole(x.shape)) for x in extras],
        [(struct(s, F32), whole(s)) for s in shapes for _ in range(2)]
        + [(struct((8, LANES), F32), whole((8, LANES)))],
        (),
        2,
        (),
        order,
    )


def adamw(order, totals, grads, weights, moments, squares, slots):
    count = len(weights)
    shapes = [w.shape for w in weights]
    rates = (RATE_MATRIX,) * (count - 1) + (RATE_AFFINE,)
    decays = (DECAY_MATRIX,) * (count - 1) + (DECAY_AFFINE,)

    def kernel(order_ref, totals_ref, *refs):
        core = order_ref[4, 0]
        grad_refs, refs = refs[: len(grads)], refs[len(grads) :]
        olds, outs = refs[: 3 * count], refs[3 * count :]
        norm = jnp.sqrt(totals_ref[0:1, :])
        outs[-1][...] = jnp.concatenate([norm, totals_ref[1:2, :] / slots, jnp.zeros((6, LANES), F32)], 0)
        factor = jnp.minimum(1.0, CLIP_NORM / (norm[:, 0:1] + 1e-06))

        def update(n, at, gradient):
            master, moment, square = (olds[3 * n + k][at] for k in range(3))
            clipped = gradient * factor
            moment = BETA_ONE * moment + (1.0 - BETA_ONE) * clipped
            square = BETA_TWO * square + (1.0 - BETA_TWO) * clipped * clipped
            mean_hat = moment / (1.0 - BETA_ONE**STEP)
            square_hat = square / (1.0 - BETA_TWO**STEP)
            master = master - rates[n] * (mean_hat / (jnp.sqrt(square_hat) + ADAM_EPS) + decays[n] * master)
            for k, value in enumerate((master, moment, square)):
                outs[3 * n + k][at] = value

        def pieces(n, start, chunk, lane, width):
            mine, got = grad_refs[2 * chunk], grad_refs[2 * chunk + 1]
            for h in range(2):
                first, second = mine[:, lane : lane + width], got[:, lane : lane + width]
                value = jnp.where(core == h, first, second)
                update(n, (slice(None), slice(start[h], start[h] + width)), value)

        width = shapes[0][1] // 3
        half = width // 2
        each = half // 3
        for k in range(3):
            at = k * width
            pieces(0, (at, at + half), 3, k * each, each)
            pieces(0, (at + each, at + half + each), 2, 2 * k * each, 2 * each)
        pieces(1, (0, half), 2, 6 * each, half)
        pieces(2, (0, shapes[2][1] // 2), 1, 0, shapes[2][1] // 2)
        pieces(3, (0, half), 0, 0, half)
        update(4, (slice(None), slice(None)), grad_refs[-1][...])

    olds = [array for n in range(count) for array in (weights[n], moments[n], squares[n])]
    return call(
        kernel,
        (1,),
        [(a, whole(a.shape)) for a in (totals, *grads, *map(streamed, olds))],
        [(far(s, F32), whole(s)) for s in shapes for _ in range(3)]
        + [(struct((8, LANES), F32), whole((8, LANES)))],
        (),
        4,
        (),
        order,
    )


def body(
    tokens,
    mlm_grad,
    doc_ids,
    span_counts,
    qkv_weight,
    proj_weight,
    inner_weight,
    outer_weight,
    affine_params,
    qkv_moment,
    proj_moment,
    inner_moment,
    outer_moment,
    affine_moment,
    qkv_square,
    proj_square,
    inner_square,
    outer_square,
    affine_square,
):
    rows, width = tokens.shape
    spans = rows // L
    half = width // 2
    chips = lax.axis_size("dp")
    order = block_order(flip_steps(chips))
    order_outer = block_order(near_first(chips))
    hidden = inner_weight.shape[1]
    pairs = width // PAIR_LANES
    affine_rows = affine_params.shape[0]
    affine_cols = jnp.pad(affine_params.astype(BF16).T, ((0, 0), (0, LANES - affine_rows)))
    block_one = chip_rows(
        jnp.concatenate([qkv_weight.astype(BF16), proj_weight.astype(BF16)], 1), (half,) * 4, affine_cols
    )
    block_two = chip_rows(inner_weight.astype(BF16), (hidden // 2,))
    block_three = chip_rows(outer_weight.astype(BF16), (half,))
    rows_chip, rows_outer = block_one.shape[0], block_three.shape[0]
    table, table_outer = kernel_order(order, rows_chip), kernel_order(order_outer, rows_chip)

    side = lax.axis_index("pair")
    own_ids, other_ids = pick(side, doc_ids[0], doc_ids[1]), pick(side, doc_ids[1], doc_ids[0])
    own_count, other_count = (
        pick(side, span_counts[0], span_counts[1]),
        pick(side, span_counts[1], span_counts[0]),
    )
    slot = jnp.arange(spans)
    anchor_live = jnp.broadcast_to((slot < own_count)[:, None], (spans, spans))
    key_live = jnp.broadcast_to((slot < other_count)[None, :], (spans, spans))
    match = (own_ids[:, None] == other_ids[None, :]) & anchor_live & key_live
    masks = jnp.stack([match, key_live, anchor_live]).astype(F32)
    live_rows = (own_count * L)[None]

    steps, steps_outer = flip_steps(chips), near_first(chips)
    one, two, three = Gather(block_one, steps), Gather(block_two, steps), Gather(block_three, steps_outer)
    one.step()
    three.step()
    first = one.step()
    three.step(three.got)
    first = (first, three.got)
    one.step(*first)
    two.step(*first)
    second = (one.got, two.got)
    one.step(*second)
    two.step(*second)
    third = (one.got, two.got)
    three.step(*second)
    own, other = one.finish(order, rows_chip, *third)
    two.step(*third)
    qkv_w, proj_w, affine, projected = projection_forward(table, tokens, own, other, affine_rows)
    two.step(two.got, projected)
    three.step()
    attention, context, normed_one, inv_one, skip_low = attention_forward(tokens, projected, proj_w, affine)
    own, other = two.finish(order, rows_chip, skip_low)
    w_own, act_own, slope_own = inner_forward(table, 0, skip_low, own, affine)
    w_other, act_other, slope_other = inner_forward(table, 1, skip_low, other, affine)
    own, other = three.finish(order_outer, rows_outer, act_own)
    outer_w, layer_out, low, sums_two, cls, cls_normed, cls_inv = outer_forward(
        table_outer, act_own, act_other, own, other, skip_low, affine, mlm_grad, live_rows
    )
    low, sums_two, loss, own, other = outer_backward(
        table, low, sums_two, cls, core_swapped(cls), masks, cls_normed, cls_inv, act_own, act_other, affine
    )

    red_outer = Reduce(*in_order(order, own, other, rows_outer))
    inner_other, bias_other, blocks_other = inner_backward(table, 1, low, slope_other, outer_w, skip_low)
    core_done = red_outer.last()
    got = red_outer.step()
    inner_own, bias_own, blocks_own = inner_backward(table, 0, low, slope_own, outer_w, skip_low, (core_done,))
    red_inner = Reduce(*in_order(order, blocks_own, blocks_other, rows_chip))
    grad_one_low, sums_one, context_grad = skip_backward(
        inner_own, inner_other, w_own, w_other, low, normed_one, inv_one, affine, proj_w,
        (red_inner.last(), got),
    )
    groups = (
        tuple(p for p in range(pairs) if p % (pairs // 2)),
        tuple(p for p in range(pairs) if not p % (pairs // 2)),
    )
    qkv_low, qkv_sums = [None, None], [None, None]
    got_outer, got_inner = red_outer.step(), red_inner.step()
    qkv_low[0], qkv_sums[0] = attention_backward(groups[0], context_grad, projected, attention)
    own, other = qkv_backward(table, tokens, qkv_low[0], (context, grad_one_low), None, (got_outer,))
    red_first = Reduce(*in_order(order, own, other, rows_chip))
    core_done = red_first.last()
    qkv_low[1], qkv_sums[1] = attention_backward(groups[1], context_grad, projected, attention, (got_inner,))
    got_outer, got_inner = red_outer.step(), red_inner.step()
    own, other = qkv_backward(
        table, tokens, qkv_low[1], None, (sums_one, sums_two, qkv_sums[1], qkv_sums[0], bias_own, bias_other),
        (core_done,),
    )
    red_first.step(got_inner)
    red_second = Reduce(*in_order(order, own, other, rows_chip))
    core_done = red_second.last()
    red_second.step()
    input_grad = tokens_backward(groups, qkv_low, qkv_w, grad_one_low, (core_done,))
    red_first.step(input_grad)
    red_second.step(input_grad)
    outer_mine, outer_theirs, inner_mine, inner_theirs, squares = summed(
        table, (red_outer.finish(), red_inner.finish())
    )
    first_mine, first_theirs, second_mine, second_theirs, squares = summed(
        table, (red_first.finish(), red_second.finish()), (1,), loss, squares
    )
    totals = total_over_devices(squares)
    grads = []
    for mine, theirs in (
        (outer_mine, outer_theirs),
        (inner_mine, inner_theirs),
        (first_mine, first_theirs),
        (second_mine, second_theirs),
    ):
        grads += [mine, core_swapped(theirs)]
    grads.append(second_mine[:, half : half + affine_rows].T)
    slots = spans * lax.axis_size("dp") * lax.axis_size("pair")
    updated = adamw(
        table,
        totals,
        grads,
        (qkv_weight, proj_weight, inner_weight, outer_weight, affine_params),
        (qkv_moment, proj_moment, inner_moment, outer_moment, affine_moment),
        (qkv_square, proj_square, inner_square, outer_square, affine_square),
        slots,
    )
    state = [updated[3 * n + k] for k in range(3) for n in range(5)]
    return (*state, layer_out, input_grad, updated[-1][0, 0], updated[-1][1, 0])


def solution(mesh):
    placed = (
        P(("dp", "pair"), None),
        P(("dp", "pair"), None),
        P("dp", None),
        P("dp"),
        P(("dp", "pair"), None),
        P(("dp", "pair"), None),
        P(("dp", "pair"), None),
        P(("dp", "pair"), None),
        P(None, ("dp", "pair")),
        P(("dp", "pair"), None),
        P(("dp", "pair"), None),
        P(("dp", "pair"), None),
        P(("dp", "pair"), None),
        P(None, ("dp", "pair")),
        P(("dp", "pair"), None),
        P(("dp", "pair"), None),
        P(("dp", "pair"), None),
        P(("dp", "pair"), None),
        P(None, ("dp", "pair")),
    )
    return jax.shard_map(
        body,
        mesh=mesh,
        in_specs=placed,
        out_specs=(
            P(("dp", "pair"), None),
            P(("dp", "pair"), None),
            P(("dp", "pair"), None),
            P(("dp", "pair"), None),
            P(None, ("dp", "pair")),
            P(("dp", "pair"), None),
            P(("dp", "pair"), None),
            P(("dp", "pair"), None),
            P(("dp", "pair"), None),
            P(None, ("dp", "pair")),
            P(("dp", "pair"), None),
            P(("dp", "pair"), None),
            P(("dp", "pair"), None),
            P(("dp", "pair"), None),
            P(None, ("dp", "pair")),
            P(("dp", "pair"), None),
            P(("dp", "pair"), None),
            P(),
            P(),
        ),
        check_vma=False,
    )
```

```python
from functools import partial

import jax
import jax.numpy as jnp
from jax import lax
from jax.experimental import pallas as pl
from jax.experimental.pallas import tpu as pltpu
from jax.sharding import PartitionSpec as P

HEADS = 12
HD = 64
L = 128
STEP = 10
LANES = 128
AXES = ("dp", "pair")


LN_EPS = 1e-12
LOSS_WEIGHT = 8.0
CLIP_NORM = 1000.0
BETA_ONE = 0.9
BETA_TWO = 0.999
ADAM_EPS = 1e-08
RATE_MATRIX = 0.05
DECAY_MATRIX = 0.01
RATE_AFFINE = 0.8
DECAY_AFFINE = 0.0

BF16 = jnp.bfloat16
F32 = jnp.float32


def flip_steps(chips):
    bits = chips.bit_length() - 1
    if bits == 4:
        return ((2, 3), (3, 2), (0, 1), (1, 0))
    return tuple((bit, bit) for bit in reversed(range(bits)))


def flip_route(chips, pair_of_bits):
    return [
        (2 * d + c, 2 * (d ^ (1 << pair_of_bits[c])) + c) for d in range(chips) for c in range(2)
    ]


def core_route(chips):
    return [(2 * d + c, 2 * d + 1 - c) for d in range(chips) for c in range(2)]


def flipped(block, bits):
    chips = lax.axis_size("dp")
    return lax.ppermute(block, AXES, flip_route(chips, bits))


def core_swapped(block):
    return lax.ppermute(block, AXES, core_route(lax.axis_size("dp")))


def near_first(chips):
    steps = flip_steps(chips)
    return steps[2:] + steps[:2] if len(steps) == 4 else steps


def block_order(steps):
    chips = lax.axis_size("dp")
    d, c = lax.axis_index("dp"), lax.axis_index("pair")
    index = jnp.arange(chips, dtype=jnp.int32)
    blocks, places = [], []
    for core in range(2):
        blocks.append(sum((index >> k & 1) << step[core] for k, step in enumerate(steps)) ^ d)
        places.append(sum(((index ^ d) >> step[core] & 1) << k for k, step in enumerate(steps)))
    rows = []
    for pairs in (blocks, places):
        rows += [pick(c, pairs[0], pairs[1]), pick(c, pairs[1], pairs[0])]
    return jnp.stack(rows + [jnp.full((chips,), c, jnp.int32)])


def kernel_order(order, rows):
    if rows % 16 == 0:
        return order
    index = jnp.arange(16, dtype=jnp.int32)
    return jnp.stack([index] * 4 + [jnp.full((16,), order[4, 0], jnp.int32)])


def in_order(order, own, other, rows):
    if rows % 16 == 0:
        return own, other
    return tuple(
        blocks.reshape(order.shape[1], rows, -1)[order[side]] for side, blocks in enumerate((own, other))
    )


def pick(core, first, second):
    return jnp.where(core == 0, first, second)


def halves_of(low, pieces):
    core = lax.axis_index("pair")
    first, second, at = [], [], 0
    for width in pieces:
        first.append(low[:, at : at + width])
        second.append(low[:, at + width : at + 2 * width])
        at += 2 * width
    first, second = jnp.concatenate(first, 1), jnp.concatenate(second, 1)
    return pick(core, first, second), pick(core, second, first)


def chip_rows(low, pieces, extra=None):
    core = lax.axis_index("pair")
    own, other = halves_of(low, pieces)
    if extra is not None:
        own, other = (jnp.concatenate([half, extra], 1) for half in (own, other))
    got = core_swapped(other)
    return pick(core, jnp.concatenate([own, got]), jnp.concatenate([got, own]))


def tied(value, *others):
    return lax.optimization_barrier((value, *others))[0]


class Gather:
    def __init__(self, block, steps):
        self.held, self.got, self.left = block[None], None, list(steps)

    def step(self, *others):
        if self.got is not None:
            self.held = jnp.concatenate([self.held, self.got], axis=0)
        self.got = flipped(tied(self.held, *others), self.left.pop(0))
        return self.got

    def finish(self, order, rows, *others):
        while self.left:
            self.step()
        own = (self.held, self.got)
        other = tuple(core_swapped(tied(part, *others)) for part in own)
        if rows % 16:
            own, other = (
                jnp.zeros((2 * self.held.shape[0], *self.held.shape[1:]), BF16)
                .at[order[side]]
                .set(jnp.concatenate(parts))
                .reshape(2, 8, -1, self.held.shape[2])
                for side, parts in enumerate((own, other))
            )
            own, other = (own[0], own[1]), (other[0], other[1])
        return own, other


class Reduce:
    def __init__(self, own, other):
        self.count, self.left = own.shape[0], list(reversed(flip_steps(lax.axis_size("dp"))))
        self.parts = [own, core_swapped(other)]

    def last(self):
        return self.parts[-1]

    def step(self, *others):
        self.count //= 2
        sent = sum(p[self.count : 2 * self.count].astype(F32) for p in self.parts).astype(BF16)
        self.parts.append(flipped(tied(sent, *others), self.left.pop(0)))
        return self.parts[-1]

    def finish(self):
        while self.left:
            self.step()
        return self.parts


def total_over_devices(value):
    bits = lax.axis_size("dp").bit_length() - 1
    value = value + core_swapped(value)
    for low in range(0, bits, 2):
        first = flipped(value, (low, low))
        if low + 1 < bits:
            second = flipped(value, (low + 1, low + 1))
            route = [(2 * d + c, 2 * (d ^ (3 << low)) + c) for d in range(1 << bits) for c in range(2)]
            both = lax.ppermute(value, AXES, route)
            bit, over = (lax.axis_index("dp") >> low & 1) == 0, (lax.axis_index("dp") >> low & 2) == 0
            near = jnp.where(bit, value, first) + jnp.where(bit, first, value)
            far_sum = jnp.where(bit, second, both) + jnp.where(bit, both, second)
            value = jnp.where(over, near, far_sum) + jnp.where(over, far_sum, near)
        else:
            value = value + first
    return value


TILE = 256
PART = 256
PAIR_LANES = 2 * HD
VMEM_LIMIT = 32 * 1024 * 1024
SMEM = pl.BlockSpec(memory_space=pltpu.SMEM)
ANY = pl.BlockSpec(memory_space=pl.ANY)


def call(kernel, grid, ins, outs, scratch=(), micros=10, after=(), order=None):
    count = len(ins) + (order is not None)

    def body(*refs):
        kernel(*refs[:count], *refs[count + len(after) :])

    in_specs = [spec for _, spec in ins] + [ANY] * len(after)
    operands = [array for array, _ in ins] + list(after)
    if order is not None:
        operands = [order] + operands
    return pl.pallas_call(
        body,
        grid_spec=pltpu.PrefetchScalarGridSpec(
            num_scalar_prefetch=int(order is not None),
            grid=grid,
            in_specs=in_specs,
            out_specs=tuple(spec for _, spec in outs),
            scratch_shapes=list(scratch),
        ),
        out_shape=tuple(shape for shape, _ in outs),
        compiler_params=pltpu.CompilerParams(
            vmem_limit_bytes=VMEM_LIMIT, dimension_semantics=("arbitrary",) * len(grid)
        ),
        cost_estimate=pl.CostEstimate(
            flops=micros * 300_000_000, bytes_accessed=micros * 300_000, transcendentals=0
        ),
    )(*operands)


def whole(shape):
    return pl.BlockSpec(shape, lambda i, *_: (0,) * len(shape))


def rows_of(count, width):
    return pl.BlockSpec((count, width), lambda i, *_: (i, 0))


def cols_of(height, count):
    return pl.BlockSpec((height, count), lambda i, *_: (0, i))


def struct(shape, dtype):
    return jax.ShapeDtypeStruct(shape, dtype)


def streamed(array):
    return pltpu.with_memory_space_constraint(array, pltpu.HBM)


def far(shape, dtype):
    return pltpu.HBM(shape, dtype)


def dot(left, right):
    return jnp.dot(left, right, preferred_element_type=F32)


def contract_rows(left, right):
    return lax.dot_general(left, right, (((0,), (0,)), ((), ())), preferred_element_type=F32)


def contract_cols(left, right):
    return lax.dot_general(left, right, (((1,), (1,)), ((), ())), preferred_element_type=F32)


def normalize(total):
    centered = total - jnp.mean(total, axis=-1, keepdims=True)
    variance = jnp.mean(centered * centered, axis=-1, keepdims=True)
    scale_inv = lax.rsqrt(variance + LN_EPS)
    return (centered * scale_inv, scale_inv)


def normalize_back(upstream, normed, scale_inv, gain):
    scaled = upstream * gain
    return scale_inv * (
        scaled
        - jnp.mean(scaled, axis=-1, keepdims=True)
        - normed * jnp.mean(scaled * normed, axis=-1, keepdims=True)
    )


def gelu_and_slope(pre):
    below = 0.5 + 0.5 * lax.erf(pre * 0.5**0.5)
    return pre * below, below + pre * jnp.exp(pre * pre * -0.5) * (2 * jnp.pi) ** -0.5


def two_heads(block, lane_low):
    zero = jnp.zeros_like(block)
    return jnp.concatenate([jnp.where(lane_low, block, zero), jnp.where(lane_low, zero, block)], 0)


def lane_is_low(rows):
    return lax.broadcasted_iota(jnp.int32, (rows, PAIR_LANES), 1) < HD


def column_sum(value):
    return jnp.sum(value, axis=0, keepdims=True)


def placed(refs, place):
    count = refs[0].shape[0]
    return refs[place // count].at[place % count]


def fetches(order_ref, own_refs, other_refs, target, sems, rows, width, start=0, lane=0):
    core = order_ref[4, 0]
    copies = []
    for place in range(sems.shape[0]):
        pair = []
        for side, refs in enumerate((own_refs, other_refs)):
            half = core if side == 0 else 1 - core
            row = pl.multiple_of(order_ref[side, place] * rows, rows)
            pair.append(
                pltpu.make_async_copy(
                    placed(refs, place).at[:, pl.ds(lane, width)],
                    target.at[pl.ds(row, rows), pl.ds(pl.multiple_of(start + half * width, LANES), width)],
                    sems.at[place, side],
                )
            )
        copies.append(pair)
    return copies


def begin(copies):
    for pair in copies:
        for copy in pair:
            copy.start()


def finish(copies):
    for pair in copies:
        for copy in pair:
            copy.wait()


def in_turn(count, *stages):
    held = stages[0](0)
    for n in range(count):
        value, held = held, stages[0](n + 1) if n + 1 < count else None
        for stage in stages[1:]:
            value = stage(n, value)


def projection_forward(order, tokens, own, other, affine_rows, after=()):
    rows, width = tokens.shape
    half = width // 2
    chips, block = 2 * own[0].shape[0], own[0].shape[1]

    def kernel(
        order_ref, tokens_ref, own_a, own_b, other_a, other_b,
        w_ref, proj_ref, affine_ref, out_ref, columns, sems, column_sems,
    ):
        own_refs, other_refs = (own_a, own_b), (other_a, other_b)
        step = pl.program_id(0)
        params = [
            pltpu.make_async_copy(
                placed(own_refs, p).at[:, pl.ds(4 * half, LANES)],
                columns.at[pl.ds(pl.multiple_of(order_ref[0, p] * block, block), block), :],
                column_sems.at[p],
            )
            for p in range(chips)
        ]
        parts = [
            fetches(order_ref, own_refs, other_refs, w_ref, sems.at[k], block, half, k * width, k * half)
            for k in range(3)
        ]
        parts.append(fetches(order_ref, own_refs, other_refs, proj_ref, sems.at[3], block, half, 0, 3 * half))

        @pl.when(step == 0)
        def _():
            for copy in params:
                copy.start()
            for copies in parts:
                begin(copies)
            for copy in params:
                copy.wait()
            affine_ref[...] = columns[...].astype(F32).T[:affine_rows]

        for k in range(3):

            @pl.when(step == k)
            def _():
                finish(parts[k])
                for n in range(width // TILE):
                    cols = slice(n * TILE, (n + 1) * TILE)
                    value = dot(tokens_ref[...], w_ref[:, k * width + n * TILE : k * width + (n + 1) * TILE])
                    if k != 1:
                        value += affine_ref[4 + k // 2 : 5 + k // 2, cols]
                    out_ref[:, cols] = value.astype(BF16)

        @pl.when(step == 2)
        def _():
            finish(parts[3])

    return call(
        kernel,
        (3,),
        [(tokens, whole(tokens.shape)), *((blocks, ANY) for blocks in (*own, *other))],
        [
            (far((width, 3 * width), BF16), whole((width, 3 * width))),
            (struct((width, width), BF16), whole((width, width))),
            (struct((affine_rows, width), F32), whole((affine_rows, width))),
            (struct((rows, 3 * width), BF16), cols_of(rows, width)),
        ],
        [
            pltpu.VMEM((width, LANES), BF16),
            pltpu.SemaphoreType.DMA((4, chips, 2)),
            pltpu.SemaphoreType.DMA((chips,)),
        ],
        8,
        after,
        order,
    )


def attention_forward(tokens, projected, proj_w, affine, after=()):
    rows, width = tokens.shape
    spans, pairs = rows // L, width // PAIR_LANES
    each = PART // L

    def kernel(
        tokens_ref, projected_ref, proj_ref, affine_ref,
        attention_ref, context_ref, normed_ref, inv_ref, skip_ref,
    ):
        lane_low = lane_is_low(L)

        def read(n, part):
            s, p = divmod(n, pairs)
            at = part * width + p * PAIR_LANES
            return projected_ref[s * L : (s + 1) * L, at : at + PAIR_LANES]

        def scored(n):
            return contract_cols(two_heads(read(n, 0) * jnp.asarray(HD**-0.5, BF16), lane_low), read(n, 1))

        def weighed(n, scores):
            s, p = divmod(n, pairs)
            exponent = jnp.exp(scores - jnp.max(scores, axis=-1, keepdims=True))
            low = (exponent * (1.0 / jnp.sum(exponent, axis=-1, keepdims=True))).astype(BF16)
            attention_ref[s, p] = low
            both = dot(low, read(n, 2))
            context_ref[s * L : (s + 1) * L, p * PAIR_LANES : (p + 1) * PAIR_LANES] = jnp.where(
                lane_low, both[:L], both[L:]
            ).astype(BF16)

        in_turn(each * pairs, scored, weighed)
        total = dot(context_ref[...], proj_ref[...]) + affine_ref[6:7, :]
        normed, inv = normalize(tokens_ref[...].astype(F32) + total)
        normed_ref[...] = normed.astype(BF16)
        inv_ref[...] = jnp.broadcast_to(inv, (PART, LANES))
        skip_ref[...] = (normed * affine_ref[0:1, :] + affine_ref[1:2, :]).astype(BF16)

    return call(
        kernel,
        (rows // PART,),
        [
            (tokens, rows_of(PART, width)),
            (projected, rows_of(PART, 3 * width)),
            (proj_w, whole(proj_w.shape)),
            (affine, whole(affine.shape)),
        ],
        [
            (
                far((spans, pairs, 2 * L, L), BF16),
                pl.BlockSpec((each, pairs, 2 * L, L), lambda i, *_: (i, 0, 0, 0)),
            ),
            (far((rows, width), BF16), rows_of(PART, width)),
            (far((rows, width), BF16), rows_of(PART, width)),
            (far((rows, LANES), F32), rows_of(PART, LANES)),
            (struct((rows, width), BF16), rows_of(PART, width)),
        ],
        (),
        12,
        after,
    )


def inner_forward(order, side, skip_low, blocks, affine, after=()):
    rows, width = skip_low.shape
    count, block, half = blocks[0].shape
    chips = 2 * count

    def kernel(order_ref, skip_ref, first_ref, second_ref, affine_ref, w_ref, act_ref, slope_ref, sems):
        step = pl.program_id(0)

        def copies(p):
            row = pl.multiple_of(order_ref[side, p] * block, block)
            return pltpu.make_async_copy(
                placed((first_ref, second_ref), p), w_ref.at[pl.ds(row, block), :], sems.at[p]
            )

        @pl.when(step == 0)
        def _():
            for b in range(chips):
                copies(b).start()
            for b in range(chips):
                copies(b).wait()

        first = order_ref[4, 0] if side == 0 else 1 - order_ref[4, 0]
        bias = affine_ref[pl.ds(8 + first * (half // width) + step, 1), :]
        parts = rows // PART

        def entered(n):
            k, r = divmod(n, parts)
            weight = w_ref[:, pl.ds(pl.multiple_of(step * width + k * TILE, LANES), TILE)]
            return dot(skip_ref[r * PART : (r + 1) * PART, :], weight)

        def activated(n, value):
            k, r = divmod(n, parts)
            at, cols = slice(r * PART, (r + 1) * PART), slice(k * TILE, (k + 1) * TILE)
            act, slope = gelu_and_slope(value + bias[:, cols])
            act_ref[at, cols] = act.astype(BF16)
            slope_ref[at, cols] = slope.astype(BF16)

        in_turn(width // TILE * parts, entered, activated)

    return call(
        kernel,
        (half // width,),
        [(skip_low, whole(skip_low.shape)), (blocks[0], ANY), (blocks[1], ANY), (affine, whole(affine.shape))],
        [
            (far((width, half), BF16), whole((width, half))),
            (struct((rows, half), BF16), cols_of(rows, width)),
            (far((rows, half), BF16), cols_of(rows, width)),
        ],
        [pltpu.SemaphoreType.DMA((chips,))],
        10,
        after,
        order,
    )


def outer_forward(order, act_own, act_other, own, other, skip_low, affine, mlm_grad, live_rows, after=()):
    rows, wide = act_own.shape
    hidden, width = 2 * wide, skip_low.shape[1]
    chips, block = 2 * own[0].shape[0], own[0].shape[1]
    spans = rows // L
    many = 2
    tile = many * PART

    def kernel(
        order_ref, act_own_ref, act_other_ref, own_a, own_b, other_a, other_b, skip_ref, affine_ref, mlm_ref, live_ref,
        w_ref, out_ref, low_ref, sums_ref, cls_ref, cls_normed_ref, cls_inv_ref, sems,
    ):
        step = pl.program_id(0)

        core = order_ref[4, 0]

        def entered(n):
            at = slice(n * PART, (n + 1) * PART)
            total = 0.0
            for k, ref in enumerate((act_own_ref, act_other_ref)):
                start = (core if k == 0 else 1 - core) * wide
                total = total + dot(ref[at, :], w_ref[pl.ds(pl.multiple_of(start, LANES), wide), :])
            return total

        def ended(n, total):
            at = slice(n * PART, (n + 1) * PART)
            normed, inv = normalize(skip_ref[at, :].astype(F32) + (total + affine_ref[7:8, :]))
            out = (normed * affine_ref[2:3, :] + affine_ref[3:4, :]).astype(BF16)
            out_ref[at, :] = out
            line = lax.broadcasted_iota(jnp.int32, (PART, 1), 0)
            live = line < live_ref[0] - (step * many + n) * PART
            upstream = jnp.where(live, mlm_ref[at, :].astype(F32), 0.0)
            grad = normalize_back(upstream, normed, inv, affine_ref[2:3, :])
            low_ref[at, :] = grad.astype(BF16)
            for k, value in enumerate((upstream * normed, upstream, grad)):
                sums_ref[k : k + 1, :] += column_sum(value)
            for s in range(PART // L):
                row, to = slice(s * L, s * L + 1), pl.ds((step * many + n) * (PART // L) + s, 1)
                cls_ref[to, :] = out[s * L : s * L + 16].astype(F32)[:1]
                cls_normed_ref[to, :] = normed[row]
                cls_inv_ref[to, :] = jnp.broadcast_to(inv[row], (1, LANES))

        copies = fetches(order_ref, (own_a, own_b), (other_a, other_b), w_ref, sems, block, width // 2)

        @pl.when(step == 0)
        def _():
            begin(copies)
            sums_ref[...] = jnp.zeros_like(sums_ref)
            finish(copies)

        in_turn(many, entered, ended)

    return call(
        kernel,
        (rows // tile,),
        [
            (act_own, rows_of(tile, wide)),
            (act_other, rows_of(tile, wide)),
            *((blocks, ANY) for blocks in (*own, *other)),
            (skip_low, rows_of(tile, width)),
            (affine, whole(affine.shape)),
            (streamed(mlm_grad), rows_of(tile, width)),
            (live_rows, SMEM),
        ],
        [
            (far((hidden, width), BF16), whole((hidden, width))),
            (far((rows, width), BF16), rows_of(tile, width)),
            (struct((rows, width), BF16), rows_of(tile, width)),
            (struct((8, width), F32), whole((8, width))),
            (struct((spans, width), F32), whole((spans, width))),
            (struct((spans, width), F32), whole((spans, width))),
            (struct((spans, LANES), F32), whole((spans, LANES))),
        ],
        [pltpu.SemaphoreType.DMA((chips, 2))],
        8,
        after,
        order,
    )


def loss_and_gradient(own, other, match, key_live, anchor_live):
    scale = own.shape[1] ** -0.5
    sims = contract_cols(own.astype(BF16), other.astype(BF16)) * scale
    step = jnp.zeros_like(sims)
    loss = None
    for axis, live in ((1, key_live), (0, anchor_live)):
        masked = jnp.where(live > 0, sims, -1000000000.0)
        peak = jnp.max(masked, axis=axis, keepdims=True)
        weights = jnp.where(live > 0, jnp.exp(masked - peak), 0.0)
        total = jnp.sum(weights, axis=axis, keepdims=True)
        active = jnp.max(match, axis=axis, keepdims=True)
        step += active * (weights / total - match)
        if loss is None:
            hit = jnp.sum(match * sims, axis=axis, keepdims=True)
            loss = jnp.sum(jnp.where(active > 0, peak + jnp.log(total) - hit, 0.0), axis=0, keepdims=True)
    step *= LOSS_WEIGHT * scale
    gradient = jnp.zeros_like(own)
    for k in range(other.shape[0]):
        gradient += step[:, k : k + 1] * other[k : k + 1, :]
    return loss, gradient


def outer_backward(order, grad_low, sums, cls, cls_other, masks, cls_normed, cls_inv, act_own, act_other, affine, after=()):
    rows, width = grad_low.shape
    hidden = 2 * act_own.shape[1]
    chips = order.shape[1]
    block, half = hidden // chips, width // 2
    tile = 4 * block
    turn = chips // 8
    spans = rows // L

    def kernel(
        order_ref, low_in_ref, sums_in_ref, cls_ref, cls_other_ref, masks_ref, normed_ref, inv_ref, act_own_ref, act_other_ref, affine_ref,
        low_ref, sums_ref, loss_ref, own_ref, other_ref, own_held, other_held, sems,
    ):
        step = pl.program_id(0)

        @pl.when(step == 0)
        def _():
            loss, up = loss_and_gradient(
                cls_ref[...], cls_other_ref[...], masks_ref[0], masks_ref[1], masks_ref[2]
            )
            normed = normed_ref[...]
            more = normalize_back(up, normed, inv_ref[:, :1], affine_ref[2:3, :])
            loss_ref[...] = jnp.broadcast_to(loss, loss_ref.shape)
            for k, value in enumerate((up * normed, up, more)):
                sums_ref[k : k + 1, :] = sums_in_ref[k : k + 1, :] + column_sum(value)
            low_ref[...] = low_in_ref[...]
            line = lax.broadcasted_iota(jnp.int32, (16, 1), 0)
            for s in range(spans):
                at = slice(s * L, s * L + 16)
                changed = low_in_ref[at, :].astype(F32) + jnp.where(line == 0, more[s : s + 1], 0.0)
                low_ref[at, :] = changed.astype(BF16)

        core = order_ref[4, 0]

        def gradient(act_ref, first):
            def entered(n):
                return contract_rows(act_ref[:, n * 2 * block : (n + 1) * 2 * block], low_ref[...])

            def ended(n, value):
                low, high = value[:, :half], value[:, half:]
                parts = (jnp.where(core == 0, low, high), jnp.where(core == 0, high, low))
                for side, (part, held, out) in enumerate(
                    zip(parts, (own_held, other_held), (own_ref, other_ref))
                ):
                    for k in range(2):
                        b = first + 2 * n + k
                        held[b] = part[k * block : (k + 1) * block].astype(BF16)
                        pltpu.make_async_copy(
                            held.at[b], out.at[order_ref[2 + side, b]], sems.at[side, b]
                        ).start()

            in_turn(2, entered, ended)

        @pl.when(step < turn)
        def _():
            gradient(act_own_ref, core * (chips // 2) + 4 * step)

        @pl.when(step >= turn)
        def _():
            gradient(act_other_ref, (1 - core) * (chips // 2) + 4 * (step - turn))

        @pl.when(step == 2 * turn - 1)
        def _():
            for side, (held, out) in enumerate(((own_held, own_ref), (other_held, other_ref))):
                for b in range(chips):
                    pltpu.make_async_copy(
                        held.at[b], out.at[order_ref[2 + side, b]], sems.at[side, b]
                    ).wait()

    shape = (chips, block, half)
    return call(
        kernel,
        (hidden // tile,),
        [
            (grad_low, whole(grad_low.shape)),
            (sums, whole(sums.shape)),
            (cls, whole(cls.shape)),
            (cls_other, whole(cls.shape)),
            (masks, whole(masks.shape)),
            (cls_normed, whole(cls.shape)),
            (cls_inv, whole(cls_inv.shape)),
            (act_own, pl.BlockSpec((rows, tile), lambda i, *_: (0, jnp.minimum(i, turn - 1)))),
            (act_other, pl.BlockSpec((rows, tile), lambda i, *_: (0, jnp.maximum(i - turn, 0)))),
            (affine, whole(affine.shape)),
        ],
        [
            (struct((rows, width), BF16), whole((rows, width))),
            (struct((8, width), F32), whole((8, width))),
            (struct((8, LANES), F32), whole((8, LANES))),
            (far(shape, BF16), ANY),
            (far(shape, BF16), ANY),
        ],
        [
            pltpu.VMEM(shape, BF16),
            pltpu.VMEM(shape, BF16),
            pltpu.SemaphoreType.DMA((2, chips)),
        ],
        8,
        after,
        order,
    )


def inner_backward(order, side, low, slope, outer_w, skip_low, after=()):
    rows, width = low.shape
    hidden = 2 * slope.shape[1]
    chips = order.shape[1]
    block = width // chips
    steps = hidden // 2 // width

    def kernel(order_ref, low_ref, slope_ref, outer_ref, skip_ref, inner_ref, bias_ref, out_ref):
        step = pl.program_id(0)

        def entered(n):
            return contract_cols(low_ref[...], outer_ref[n * TILE : (n + 1) * TILE, :])

        def sloped(n, value):
            cols = slice(n * TILE, (n + 1) * TILE)
            inner_grad = value * slope_ref[:, cols].astype(F32)
            bias_ref[pl.ds(step, 1), cols] = column_sum(inner_grad)
            inner_low = inner_grad.astype(BF16)
            inner_ref[:, cols] = inner_low
            return contract_rows(skip_ref[...], inner_low).astype(BF16)

        def stored(n, value):
            for b in range(chips):
                out_ref[order_ref[2 + side, b], :, n * TILE : (n + 1) * TILE] = value[b * block : (b + 1) * block]

        in_turn(width // TILE, entered, sloped, stored)

    def place(i, table):
        half = table[4, 0] if side == 0 else 1 - table[4, 0]
        return half * steps + i

    return call(
        kernel,
        (steps,),
        [
            (low, whole(low.shape)),
            (streamed(slope), cols_of(rows, width)),
            (streamed(outer_w), pl.BlockSpec((width, width), lambda i, table: (place(i, table), 0))),
            (skip_low, whole(skip_low.shape)),
        ],
        [
            (struct((rows, hidden // 2), BF16), cols_of(rows, width)),
            (struct((8, width), F32), whole((8, width))),
            (
                struct((chips, block, hidden // 2), BF16),
                pl.BlockSpec((chips, block, width), lambda i, *_: (0, 0, i)),
            ),
        ],
        (),
        8,
        after,
        order,
    )


def skip_backward(inner_own, inner_other, w_own, w_other, grad_two_low, normed_one, inv_one, affine, proj_w, after=()):
    rows, width = grad_two_low.shape
    half = w_own.shape[1]
    many = 2
    tile = many * PART

    def kernel(
        own_ref, other_ref, w_own_ref, w_other_ref, grad_two_ref, normed_ref, inv_ref, affine_ref, proj_ref,
        low_ref, sums_ref, context_ref,
    ):
        step = pl.program_id(0)

        @pl.when(step == 0)
        def _():
            sums_ref[...] = jnp.zeros_like(sums_ref)

        def entered(n):
            at = slice(n * PART, (n + 1) * PART)
            up = grad_two_ref[at, :].astype(F32)
            for ref, weight in ((own_ref, w_own_ref), (other_ref, w_other_ref)):
                up = up + contract_cols(ref[at, :], weight[...])
            return up

        def ended(n, up):
            at = slice(n * PART, (n + 1) * PART)
            normed = normed_ref[at, :].astype(F32)
            grad = normalize_back(up, normed, inv_ref[at, :1], affine_ref[0:1, :])
            low = grad.astype(BF16)
            low_ref[at, :] = low
            for k, value in enumerate((up * normed, up, grad)):
                sums_ref[k : k + 1, :] += column_sum(value)
            context_ref[at, :] = contract_cols(low, proj_ref[...]).astype(BF16)

        in_turn(many, entered, ended)

    return call(
        kernel,
        (rows // tile,),
        [
            (inner_own, rows_of(tile, half)),
            (inner_other, rows_of(tile, half)),
            (streamed(w_own), whole(w_own.shape)),
            (streamed(w_other), whole(w_other.shape)),
            (grad_two_low, rows_of(tile, width)),
            (streamed(normed_one), rows_of(tile, width)),
            (streamed(inv_one), rows_of(tile, LANES)),
            (affine, whole(affine.shape)),
            (proj_w, whole(proj_w.shape)),
        ],
        [
            (struct((rows, width), BF16), rows_of(tile, width)),
            (struct((8, width), F32), whole((8, width))),
            (struct((rows, width), BF16), rows_of(tile, width)),
        ],
        (),
        8,
        after,
    )


def attention_backward(pairs, context_grad, projected, attention, after=()):
    rows, width = context_grad.shape
    spans, count = rows // L, len(pairs)
    wide = 3 * count * PAIR_LANES
    each = 2

    def kernel(grad_ref, projected_ref, attention_ref, out_ref, sums_ref):
        @pl.when(pl.program_id(0) == 0)
        def _():
            sums_ref[...] = jnp.zeros_like(sums_ref)

        lane_low = lane_is_low(L)
        def entered(m):
            s, n = divmod(m, count)
            at, line = pairs[n] * PAIR_LANES, slice(s * L, (s + 1) * L)
            grads = two_heads(grad_ref[line, at : at + PAIR_LANES], lane_low)
            v = projected_ref[line, 2 * width + at : 2 * width + at + PAIR_LANES]
            return grads, contract_cols(grads, v)

        def ended(m, value):
            s, n = divmod(m, count)
            at, line = pairs[n] * PAIR_LANES, slice(s * L, (s + 1) * L)
            q, k = (
                projected_ref[line, part * width + at : part * width + at + PAIR_LANES] for part in range(2)
            )
            grads, back = value
            low = attention_ref[s, pairs[n]]
            weights = low.astype(F32)
            product = back * weights
            score = (product - weights * jnp.sum(product, axis=-1, keepdims=True)) * HD**-0.5
            score_low = score.astype(BF16)
            both = dot(score_low, k)
            parts = (
                jnp.where(lane_low, both[:L], both[L:]),
                contract_rows(score_low, two_heads(q, lane_low)),
                contract_rows(low, grads),
            )
            for part, value in enumerate(parts):
                to = slice((part * count + n) * PAIR_LANES, (part * count + n + 1) * PAIR_LANES)
                out_ref[line, to] = value.astype(BF16)
                sums_ref[:, to] += column_sum(value)

        in_turn(each * count, entered, ended)

    return call(
        kernel,
        (spans // each,),
        [
            (context_grad, rows_of(each * L, width)),
            (streamed(projected), rows_of(each * L, 3 * width)),
            (streamed(attention), pl.BlockSpec((each, width // PAIR_LANES, 2 * L, L), lambda i, *_: (i, 0, 0, 0))),
        ],
        [
            (struct((rows, wide), BF16), rows_of(each * L, wide)),
            (struct((1, wide), F32), whole((1, wide))),
        ],
        (),
        3 * count,
        after,
    )


def store_blocks(order_ref, low, high, rows, own_ref, other_ref, lane):
    core = order_ref[4, 0]
    own = jnp.where(core == 0, low, high).astype(BF16)
    other = jnp.where(core == 0, high, low).astype(BF16)
    width = low.shape[1]
    for b in range(low.shape[0] // rows):
        at = slice(b * rows, (b + 1) * rows)
        own_ref[order_ref[2, b], :, lane : lane + width] = own[at]
        other_ref[order_ref[3, b], :, lane : lane + width] = other[at]


def qkv_backward(order, tokens, qkv_low, proj=None, sums=None, after=()):
    rows, width = tokens.shape
    chips = order.shape[1]
    block, half = width // chips, width // 2
    each = qkv_low.shape[1] // 6
    extra = half if proj is not None else LANES

    def affine_rows(sums_one, sums_two, first, second, bias_own, bias_other, lines, core):
        lines[...] = jnp.zeros_like(lines)
        lines[0:2, :] = sums_one[0:2, :]
        lines[2:4, :] = sums_two[0:2, :]
        for row, part in ((4, 0), (5, 2)):
            for h in range(2):
                at = h * half
                for ref in (first, second):
                    wide = ref.shape[1] // 6
                    lines[row : row + 1, at : at + wide] = ref[:, (2 * part + h) * wide : (2 * part + h + 1) * wide]
                    at += wide
        lines[6:7, :] = sums_one[2:3, :]
        lines[7:8, :] = sums_two[2:3, :]
        lines[8:10, :] = jnp.where(core == 0, bias_own[0:2, :], bias_other[0:2, :])
        lines[10:12, :] = jnp.where(core == 0, bias_other[0:2, :], bias_own[0:2, :])
        return lines[...].T

    def kernel(order_ref, tokens_ref, qkv_ref, *rest):
        rest, (own_ref, other_ref, lines) = rest[:-3], rest[-3:]

        def entered(k):
            if k < 3:
                return contract_rows(tokens_ref[...], qkv_ref[:, 2 * k * each : 2 * (k + 1) * each])
            if proj is not None:
                return contract_rows(rest[0][...], rest[1][...])
            value = affine_rows(*rest, lines, order_ref[4, 0])
            return jnp.concatenate([value, value], axis=1)

        def ended(k, value):
            middle = value.shape[1] // 2
            store_blocks(order_ref, value[:, :middle], value[:, middle:], block, own_ref, other_ref, k * each)

        in_turn(4, entered, ended)

    shape = (chips, block, 3 * each + extra)
    more = list(proj if proj is not None else sums)
    return call(
        kernel,
        (1,),
        [(array, whole(array.shape)) for array in (tokens, qkv_low, *more)],
        [(struct(shape, BF16), whole(shape)), (struct(shape, BF16), whole(shape))],
        [pltpu.VMEM((LANES, width), F32)],
        5,
        after,
        order,
    )


def tokens_backward(groups, qkv_lows, qkv_w, grad_one, after=()):
    rows, width = grad_one.shape

    def kernel(*refs):
        lows, (w_ref, grad_ref, out_ref, held) = refs[: len(groups)], refs[len(groups) :]
        for pairs, ref in zip(groups, lows):
            for part in range(3):
                for n, p in enumerate(pairs):
                    held[:, part * width + p * PAIR_LANES : part * width + (p + 1) * PAIR_LANES] = ref[
                        :, (part * len(pairs) + n) * PAIR_LANES : (part * len(pairs) + n + 1) * PAIR_LANES
                    ]
        out_ref[...] = contract_cols(held[...], w_ref[...]) + grad_ref[...].astype(F32)

    return call(
        kernel,
        (rows // PART,),
        [(low, rows_of(PART, low.shape[1])) for low in qkv_lows]
        + [(streamed(qkv_w), whole(qkv_w.shape)), (grad_one, rows_of(PART, width))],
        [(struct((rows, width), F32), rows_of(PART, width))],
        [pltpu.VMEM((PART, 3 * width), BF16)],
        8,
        after,
    )[0]


def summed(order, chunks, doubled=(), loss=None, before=None):
    counts = [len(parts) for parts in chunks]
    shapes = [(parts[0].shape[1] // 2, parts[0].shape[2]) for parts in chunks]
    extras = [loss] if loss is not None else []
    extras += [before] if before is not None else []
    arrays = [p for parts in chunks for p in parts]

    def kernel(order_ref, *refs):
        core = order_ref[4, 0]
        squares = 0.0
        outs = refs[len(arrays) + len(extras) :]
        at = 0
        for n, count in enumerate(counts):
            rows, cols = shapes[n]
            total = sum(ref[0].astype(F32) for ref in refs[at : at + count])
            at += count
            first, second = total[:rows], total[rows:]
            mine, theirs = jnp.where(core == 0, first, second), jnp.where(core == 0, second, first)
            outs[2 * n][...] = mine
            outs[2 * n + 1][...] = theirs
            squares += jnp.sum(mine * mine)
            theirs = theirs[:, : cols - LANES] if n in doubled else theirs
            squares += jnp.sum(theirs * theirs)
        line = lax.broadcasted_iota(jnp.int32, (8, LANES), 0)
        result = jnp.where(line == 0, squares, 0.0)
        if loss is not None:
            result += jnp.where(line == 1, refs[len(arrays)][0:1, :], 0.0)
        if before is not None:
            result += refs[len(arrays) + len(extras) - 1][...]
        outs[-1][...] = result

    return call(
        kernel,
        (1,),
        [(p, pl.BlockSpec((1, *p.shape[1:]), lambda i, *_: (0, 0, 0))) for p in arrays]
        + [(x, whole(x.shape)) for x in extras],
        [(struct(s, F32), whole(s)) for s in shapes for _ in range(2)]
        + [(struct((8, LANES), F32), whole((8, LANES)))],
        (),
        2,
        (),
        order,
    )


def adamw(order, totals, grads, weights, moments, squares, slots):
    count = len(weights)
    shapes = [w.shape for w in weights]
    rates = (RATE_MATRIX,) * (count - 1) + (RATE_AFFINE,)
    decays = (DECAY_MATRIX,) * (count - 1) + (DECAY_AFFINE,)

    def kernel(order_ref, totals_ref, *refs):
        core = order_ref[4, 0]
        grad_refs, refs = refs[: len(grads)], refs[len(grads) :]
        olds, outs = refs[: 3 * count], refs[3 * count :]
        norm = jnp.sqrt(totals_ref[0:1, :])
        outs[-1][...] = jnp.concatenate([norm, totals_ref[1:2, :] / slots, jnp.zeros((6, LANES), F32)], 0)
        factor = jnp.minimum(1.0, CLIP_NORM / (norm[:, 0:1] + 1e-06))

        def update(n, at, gradient):
            master, moment, square = (olds[3 * n + k][at] for k in range(3))
            clipped = gradient * factor
            moment = BETA_ONE * moment + (1.0 - BETA_ONE) * clipped
            square = BETA_TWO * square + (1.0 - BETA_TWO) * clipped * clipped
            mean_hat = moment / (1.0 - BETA_ONE**STEP)
            square_hat = square / (1.0 - BETA_TWO**STEP)
            master = master - rates[n] * (mean_hat / (jnp.sqrt(square_hat) + ADAM_EPS) + decays[n] * master)
            for k, value in enumerate((master, moment, square)):
                outs[3 * n + k][at] = value

        def pieces(n, start, chunk, lane, width):
            mine, got = grad_refs[2 * chunk], grad_refs[2 * chunk + 1]
            for h in range(2):
                first, second = mine[:, lane : lane + width], got[:, lane : lane + width]
                value = jnp.where(core == h, first, second)
                update(n, (slice(None), slice(start[h], start[h] + width)), value)

        width = shapes[0][1] // 3
        half = width // 2
        each = half // 3
        for k in range(3):
            at = k * width
            pieces(0, (at, at + half), 3, k * each, each)
            pieces(0, (at + each, at + half + each), 2, 2 * k * each, 2 * each)
        pieces(1, (0, half), 2, 6 * each, half)
        pieces(2, (0, shapes[2][1] // 2), 1, 0, shapes[2][1] // 2)
        pieces(3, (0, half), 0, 0, half)
        update(4, (slice(None), slice(None)), grad_refs[-1][...])

    olds = [array for n in range(count) for array in (weights[n], moments[n], squares[n])]
    return call(
        kernel,
        (1,),
        [(a, whole(a.shape)) for a in (totals, *grads, *map(streamed, olds))],
        [(far(s, F32), whole(s)) for s in shapes for _ in range(3)]
        + [(struct((8, LANES), F32), whole((8, LANES)))],
        (),
        4,
        (),
        order,
    )


def body(
    tokens,
    mlm_grad,
    doc_ids,
    span_counts,
    qkv_weight,
    proj_weight,
    inner_weight,
    outer_weight,
    affine_params,
    qkv_moment,
    proj_moment,
    inner_moment,
    outer_moment,
    affine_moment,
    qkv_square,
    proj_square,
    inner_square,
    outer_square,
    affine_square,
):
    rows, width = tokens.shape
    spans = rows // L
    half = width // 2
    chips = lax.axis_size("dp")
    order = block_order(flip_steps(chips))
    order_outer = block_order(near_first(chips))
    hidden = inner_weight.shape[1]
    pairs = width // PAIR_LANES
    affine_rows = affine_params.shape[0]
    affine_cols = jnp.pad(affine_params.astype(BF16).T, ((0, 0), (0, LANES - affine_rows)))
    block_one = chip_rows(
        jnp.concatenate([qkv_weight.astype(BF16), proj_weight.astype(BF16)], 1), (half,) * 4, affine_cols
    )
    block_two = chip_rows(inner_weight.astype(BF16), (hidden // 2,))
    block_three = chip_rows(outer_weight.astype(BF16), (half,))
    rows_chip, rows_outer = block_one.shape[0], block_three.shape[0]
    table, table_outer = kernel_order(order, rows_chip), kernel_order(order_outer, rows_chip)

    side = lax.axis_index("pair")
    own_ids, other_ids = pick(side, doc_ids[0], doc_ids[1]), pick(side, doc_ids[1], doc_ids[0])
    own_count, other_count = (
        pick(side, span_counts[0], span_counts[1]),
        pick(side, span_counts[1], span_counts[0]),
    )
    slot = jnp.arange(spans)
    anchor_live = jnp.broadcast_to((slot < own_count)[:, None], (spans, spans))
    key_live = jnp.broadcast_to((slot < other_count)[None, :], (spans, spans))
    match = (own_ids[:, None] == other_ids[None, :]) & anchor_live & key_live
    masks = jnp.stack([match, key_live, anchor_live]).astype(F32)
    live_rows = (own_count * L)[None]

    steps, steps_outer = flip_steps(chips), near_first(chips)
    one, two, three = Gather(block_one, steps), Gather(block_two, steps), Gather(block_three, steps_outer)
    one.step()
    three.step()
    first = one.step()
    three.step(three.got)
    first = (first, three.got)
    one.step(*first)
    two.step(*first)
    second = (one.got, two.got)
    one.step(*second)
    two.step(*second)
    third = (one.got, two.got)
    three.step(*second)
    own, other = one.finish(order, rows_chip, *third)
    two.step(*third)
    qkv_w, proj_w, affine, projected = projection_forward(table, tokens, own, other, affine_rows)
    two.step(two.got, projected)
    three.step()
    attention, context, normed_one, inv_one, skip_low = attention_forward(tokens, projected, proj_w, affine)
    own, other = two.finish(order, rows_chip, skip_low)
    w_own, act_own, slope_own = inner_forward(table, 0, skip_low, own, affine)
    w_other, act_other, slope_other = inner_forward(table, 1, skip_low, other, affine)
    own, other = three.finish(order_outer, rows_outer, act_own)
    outer_w, layer_out, low, sums_two, cls, cls_normed, cls_inv = outer_forward(
        table_outer, act_own, act_other, own, other, skip_low, affine, mlm_grad, live_rows
    )
    low, sums_two, loss, own, other = outer_backward(
        table, low, sums_two, cls, core_swapped(cls), masks, cls_normed, cls_inv, act_own, act_other, affine
    )

    red_outer = Reduce(*in_order(order, own, other, rows_outer))
    inner_other, bias_other, blocks_other = inner_backward(table, 1, low, slope_other, outer_w, skip_low)
    core_done = red_outer.last()
    got = red_outer.step()
    inner_own, bias_own, blocks_own = inner_backward(table, 0, low, slope_own, outer_w, skip_low, (core_done,))
    red_inner = Reduce(*in_order(order, blocks_own, blocks_other, rows_chip))
    grad_one_low, sums_one, context_grad = skip_backward(
        inner_own, inner_other, w_own, w_other, low, normed_one, inv_one, affine, proj_w,
        (red_inner.last(), got),
    )
    groups = (
        tuple(p for p in range(pairs) if p % (pairs // 2)),
        tuple(p for p in range(pairs) if not p % (pairs // 2)),
    )
    qkv_low, qkv_sums = [None, None], [None, None]
    got_outer, got_inner = red_outer.step(), red_inner.step()
    qkv_low[0], qkv_sums[0] = attention_backward(groups[0], context_grad, projected, attention)
    own, other = qkv_backward(table, tokens, qkv_low[0], (context, grad_one_low), None, (got_outer,))
    red_first = Reduce(*in_order(order, own, other, rows_chip))
    core_done = red_first.last()
    qkv_low[1], qkv_sums[1] = attention_backward(groups[1], context_grad, projected, attention, (got_inner,))
    got_outer, got_inner = red_outer.step(), red_inner.step()
    own, other = qkv_backward(
        table, tokens, qkv_low[1], None, (sums_one, sums_two, qkv_sums[1], qkv_sums[0], bias_own, bias_other),
        (core_done,),
    )
    red_first.step()
    red_second = Reduce(*in_order(order, own, other, rows_chip))
    core_done = red_second.last()
    red_second.step()
    input_grad = tokens_backward(groups, qkv_low, qkv_w, grad_one_low, (core_done,))
    red_first.step(input_grad)
    red_second.step(input_grad)
    outer_mine, outer_theirs, inner_mine, inner_theirs, squares = summed(
        table, (red_outer.finish(), red_inner.finish())
    )
    first_mine, first_theirs, second_mine, second_theirs, squares = summed(
        table, (red_first.finish(), red_second.finish()), (1,), loss, squares
    )
    totals = total_over_devices(squares)
    grads = []
    for mine, theirs in (
        (outer_mine, outer_theirs),
        (inner_mine, inner_theirs),
        (first_mine, first_theirs),
        (second_mine, second_theirs),
    ):
        grads += [mine, core_swapped(theirs)]
    grads.append(second_mine[:, half : half + affine_rows].T)
    slots = spans * lax.axis_size("dp") * lax.axis_size("pair")
    updated = adamw(
        table,
        totals,
        grads,
        (qkv_weight, proj_weight, inner_weight, outer_weight, affine_params),
        (qkv_moment, proj_moment, inner_moment, outer_moment, affine_moment),
        (qkv_square, proj_square, inner_square, outer_square, affine_square),
        slots,
    )
    state = [updated[3 * n + k] for k in range(3) for n in range(5)]
    return (*state, layer_out, input_grad, updated[-1][0, 0], updated[-1][1, 0])


def solution(mesh):
    placed = (
        P(("dp", "pair"), None),
        P(("dp", "pair"), None),
        P("dp", None),
        P("dp"),
        P(("dp", "pair"), None),
        P(("dp", "pair"), None),
        P(("dp", "pair"), None),
        P(("dp", "pair"), None),
        P(None, ("dp", "pair")),
        P(("dp", "pair"), None),
        P(("dp", "pair"), None),
        P(("dp", "pair"), None),
        P(("dp", "pair"), None),
        P(None, ("dp", "pair")),
        P(("dp", "pair"), None),
        P(("dp", "pair"), None),
        P(("dp", "pair"), None),
        P(("dp", "pair"), None),
        P(None, ("dp", "pair")),
    )
    return jax.shard_map(
        body,
        mesh=mesh,
        in_specs=placed,
        out_specs=(
            P(("dp", "pair"), None),
            P(("dp", "pair"), None),
            P(("dp", "pair"), None),
            P(("dp", "pair"), None),
            P(None, ("dp", "pair")),
            P(("dp", "pair"), None),
            P(("dp", "pair"), None),
            P(("dp", "pair"), None),
            P(("dp", "pair"), None),
            P(None, ("dp", "pair")),
            P(("dp", "pair"), None),
            P(("dp", "pair"), None),
            P(("dp", "pair"), None),
            P(("dp", "pair"), None),
            P(None, ("dp", "pair")),
            P(("dp", "pair"), None),
            P(("dp", "pair"), None),
            P(),
            P(),
        ),
        check_vma=False,
    )
```
